32 devices in a mesh: grp: 2 (over x), sec: 16 (over z, y, core).
Axes of the slice: x: 2, y: 2, z: 4, core: 2. Of those that a mesh axis runs over, the one named last changes fastest.
Arguments:
- psi: bfloat16 [32, 1024, 512], P(('grp', 'sec')), parts along dimension 0, may hold values from -6 to 6
- left_env: bfloat16 [32, 4, 1024, 1024], P(('grp', 'sec')), parts along dimension 0, may hold values from -1 to 2, as said below
- right_env: bfloat16 [32, 4, 512, 512], P(('grp', 'sec')), parts along dimension 0, may hold values from -1 to 2, as said below
- row_sizes: int32 [32], P(('grp', 'sec')), parts along dimension 0, may hold values from 64 to 1024, as said below
- col_sizes: int32 [32], P(('grp', 'sec')), parts along dimension 0, may hold values from 64 to 512, as said below
Outputs:
- sigma: bfloat16 [32, 1024, 512], P(('grp', 'sec')), parts along dimension 0
- energy: float32 [2], P('grp'), parts along dimension 0
The draws below stay inside these ranges and needn't reach their ends.
There are 2 independent parts, one for each index of `grp`. The reference program is written for one: setup_inputs(seed, part) draws one part's arguments, and reference() takes and returns one part's arrays. A program takes and returns all parts, laid end to end along the dimension named above; each array names one. Nothing has to cross between parts.
Inputs may be any that keep to these rules, and one draw needn't show every extreme that they name: `row_sizes`: every sector's left width is at least 64, and some sector's is exactly 1024. `col_sizes`: every sector's right width is at least 64, and some sector's is exactly 512. `left_env`: the blocks of term group 0 have a positive diagonal. `right_env`: the blocks of term group 0 have a positive diagonal.
All inputs are finite; a program needn't handle non-finite values.
Results may differ from the reference program's by a relative error of at most 0.0049.
Values sent between devices are 32-bit elements; how exact they have to be, the bound alone decides.
No kernel may reach another device: no remote copies, remote signals or barrier semaphores. Data moves between devices by JAX's collectives and lax.ppermute only.
A program may use at most 64 MiB of HBM per device.

```python
import jax
import jax.numpy as jnp
from jax import lax

MB = 1024
MR = 512
TG = 4
SECTORS = 16


def shifted_blocks(key, width):
    noise = jax.random.truncated_normal(key, -4.0, 4.0, (SECTORS, TG, width, width), jnp.float32)
    noise = noise * width ** (-0.5)
    diagonal = jnp.eye(width, dtype=jnp.float32)[None, None, :, :]
    first_group = (jnp.arange(TG, dtype=jnp.int32) == 0).astype(jnp.float32)[None, :, None, None]
    return noise + diagonal * first_group


def draw_left_env(key, part):
    key = jax.random.fold_in(key, 31)
    return shifted_blocks(key, MB).astype(jnp.bfloat16)


def draw_right_env(key, part):
    key = jax.random.fold_in(key, 37)
    return shifted_blocks(key, MR).astype(jnp.bfloat16)


def draw_row_sizes(key, part):
    key = jax.random.fold_in(key, 11)
    first, second = jax.random.split(key)
    values = jax.random.randint(first, (SECTORS,), MB // 16, MB + 1)
    chosen = jax.random.randint(second, (), 0, SECTORS)
    return values.at[chosen].set(MB).astype(jnp.int32)


def draw_col_sizes(key, part):
    key = jax.random.fold_in(key, 23)
    first, second = jax.random.split(key)
    values = jax.random.randint(first, (SECTORS,), MR // 8, MR + 1)
    chosen = jax.random.randint(second, (), 0, SECTORS)
    return values.at[chosen].set(MR).astype(jnp.int32)


def block_levels(own_key, dims, pieces, low, high):
    loudness, own = 1.0, jax.random.fold_in(own_key, 6)
    for position, parts in pieces:
        heights = jnp.exp(jax.random.uniform(jax.random.fold_in(own, position), (parts,), jnp.float32, low / len(pieces), high / len(pieces)))
        loudness = loudness * jnp.repeat(heights, dims[position] // parts).reshape([-1 if axis == position else 1 for axis in range(len(dims))])
    return loudness


def normal_values(own_key, dims, deviation, limit, cuts=(), held_as=jnp.bfloat16):
    result = jax.random.normal(own_key, dims, jnp.float32) * deviation
    if len(cuts) > 0:
        result = block_levels(own_key, dims, cuts, -0.22, 0.18) * result
    return jnp.clip(result, min=-limit, max=limit).astype(held_as)


def setup_inputs(seed: int = 0, part: int = 0) -> dict:
    splits = jax.random.split(jax.random.key(seed), 6)
    part_splits = jax.random.split(jax.random.fold_in(splits[5], part), 6)
    psi = normal_values(part_splits[0], (SECTORS, MB, MR), 1.0, 6.0, ((0, 16),))
    left_env = draw_left_env(jax.random.fold_in(jax.random.fold_in(splits[5], part), 71), part)
    right_env = draw_right_env(jax.random.fold_in(jax.random.fold_in(splits[5], part), 71), part)
    row_sizes = draw_row_sizes(jax.random.fold_in(jax.random.fold_in(splits[5], part), 71), part)
    col_sizes = draw_col_sizes(jax.random.fold_in(jax.random.fold_in(splits[5], part), 71), part)
    return {"psi": psi, "left_env": left_env, "right_env": right_env, "row_sizes": row_sizes, "col_sizes": col_sizes}


term_shifts = (0, 1, 2, -1)


def one_sector(args):
    left_block, psi_block, right_block = args
    left = jnp.dot(left_block, psi_block, preferred_element_type=jnp.float32).astype(jnp.bfloat16)
    return jnp.dot(left, right_block, preferred_element_type=jnp.float32)


def reference(psi, left_env, right_env, row_sizes, col_sizes):
    rows = jnp.arange(MB, dtype=jnp.int32)[None, :, None] < row_sizes[:, None, None]
    cols = jnp.arange(MR, dtype=jnp.int32)[None, None, :] < col_sizes[:, None, None]
    live = jnp.logical_and(rows, cols)
    psi_live = jnp.where(live, psi, jnp.zeros_like(psi))
    total = jnp.zeros((SECTORS, MB, MR), jnp.float32)
    for term, delta in enumerate(term_shifts):
        block = lax.map(one_sector, (left_env[:, term], psi_live, right_env[:, term]))
        if delta > 0:
            block = jnp.concatenate([jnp.zeros((delta, MB, MR), jnp.float32), block[:-delta]], axis=0)
        elif delta < 0:
            block = jnp.concatenate([block[-delta:], jnp.zeros((-delta, MB, MR), jnp.float32)], axis=0)
        total = total + block
    total = jnp.where(live, total, jnp.zeros_like(total))
    sigma = total.astype(jnp.bfloat16)
    energy = jnp.sum(psi_live.astype(jnp.float32) * total).reshape((1,))
    return sigma, energy
```

```python
import functools

import jax
import jax.numpy as jnp
from jax import lax
from jax.experimental import pallas as pl
from jax.experimental.pallas import tpu as pltpu
from jax.sharding import PartitionSpec as P

PARTS = 2
VMEM = 48 * 1024 * 1024


def params():
    return pltpu.CompilerParams(vmem_limit_bytes=VMEM, dimension_semantics=("arbitrary",))


def mask_kernel(size_ref, psi_ref, out_ref):
    rows = lax.broadcasted_iota(jnp.int32, psi_ref.shape, 0) < size_ref[0]
    cols = lax.broadcasted_iota(jnp.int32, psi_ref.shape, 1) < size_ref[1]
    values = psi_ref[...].astype(jnp.float32)
    out_ref[...] = jnp.where(jnp.logical_and(rows, cols), values, 0.0).astype(out_ref.dtype)


def masked(psi, sizes):
    return pl.pallas_call(
        mask_kernel,
        out_shape=jax.ShapeDtypeStruct(psi.shape, psi.dtype),
        in_specs=[
            pl.BlockSpec(memory_space=pltpu.SMEM),
            pl.BlockSpec(memory_space=pltpu.VMEM),
        ],
        out_specs=pl.BlockSpec(memory_space=pltpu.VMEM),
        compiler_params=pltpu.CompilerParams(vmem_limit_bytes=VMEM),
        name="mask_psi",
    )(sizes, psi)


def term_kernel(added, term_ref, live_ref, left_ref, right_ref, *refs):
    out_ref = refs[-1]
    left = jnp.dot(left_ref[0, 0], live_ref[...], preferred_element_type=jnp.float32)
    value = jnp.dot(
        left.astype(jnp.bfloat16), right_ref[0, 0], preferred_element_type=jnp.float32
    )
    if added:
        value = value + refs[0][...]
    out_ref[...] = value


def term_rows(term, live, left_env, right_env, first, count, added=None):
    width, cols = live.shape
    block = min(256, count)
    in_specs = [
        pl.BlockSpec((width, cols), lambda i, t: (0, 0)),
        pl.BlockSpec((1, 1, block, width), lambda i, t: (0, t[0], first // block + i, 0)),
        pl.BlockSpec((1, 1, cols, cols), lambda i, t: (0, t[0], 0, 0)),
    ]
    operands = [live, left_env, right_env]
    if added is not None:
        in_specs.append(pl.BlockSpec((block, cols), lambda i, t: (i, 0)))
        operands.append(added)
    return pl.pallas_call(
        functools.partial(term_kernel, added is not None),
        out_shape=jax.ShapeDtypeStruct((count, cols), jnp.float32),
        grid_spec=pltpu.PrefetchScalarGridSpec(
            num_scalar_prefetch=1,
            grid=(count // block,),
            in_specs=in_specs,
            out_specs=pl.BlockSpec((block, cols), lambda i, t: (i, 0)),
        ),
        compiler_params=params(),
        cost_estimate=pl.CostEstimate(
            flops=2 * count * cols * (width + cols),
            bytes_accessed=2 * (width * cols + count * width + cols * cols) + 4 * count * cols,
            transcendentals=0,
        ),
        name="term_rows",
    )(jnp.reshape(term, (1,)), *operands)


def finish_kernel(first, steps, info_ref, *refs):
    live_ref, own_ref, a_ref, b_ref, c_ref, before_ref = refs[:6]
    sigma_ref, energy_ref, sum_ref = refs[-3:]
    step = pl.program_id(0)
    block, cols = own_ref.shape
    which = info_ref[2]
    arrived = jnp.where(
        which == 0, a_ref[...], jnp.where(which == 1, b_ref[...], c_ref[...])
    )
    total = own_ref[...] + arrived
    row = lax.broadcasted_iota(jnp.int32, (block, cols), 0) + (first + step * block)
    col = lax.broadcasted_iota(jnp.int32, (block, cols), 1)
    inside = jnp.logical_and(row < info_ref[0], col < info_ref[1])
    total = jnp.where(inside, total, 0.0)
    sigma_ref[0] = total.astype(sigma_ref.dtype)
    part = jnp.sum(
        jnp.reshape(live_ref[...].astype(jnp.float32) * total, (block // 8, 8, cols)), axis=0
    )

    @pl.when(step == 0)
    def _():
        sum_ref[...] = jnp.zeros_like(sum_ref)

    sum_ref[...] += part

    @pl.when(step == steps - 1)
    def _():
        energy_ref[0] = before_ref[0] + jnp.sum(sum_ref[...])


def finish(info, live, own, arrivals, before, sigma, first):
    count, cols = own.shape
    block = min(256, count)
    base = first // block

    def arrival(which):
        return pl.BlockSpec((block, cols), lambda i, n: (jnp.where(n[2] == which, i, 0), 0))

    in_specs = [
        pl.BlockSpec((block, cols), lambda i, n: (base + i, 0)),
        pl.BlockSpec((block, cols), lambda i, n: (i, 0)),
        arrival(0),
        arrival(1),
        arrival(2),
        pl.BlockSpec(memory_space=pltpu.SMEM),
    ]
    operands = [live, own, *arrivals, before]
    aliases = {}
    if sigma is not None:
        in_specs.append(pl.BlockSpec(memory_space=pl.ANY))
        operands.append(sigma)
        aliases = {len(operands): 0}
    steps = count // block
    return pl.pallas_call(
        functools.partial(finish_kernel, first, steps),
        out_shape=(
            jax.ShapeDtypeStruct((1, *live.shape), jnp.bfloat16),
            jax.ShapeDtypeStruct((1,), jnp.float32),
        ),
        grid_spec=pltpu.PrefetchScalarGridSpec(
            num_scalar_prefetch=1,
            grid=(steps,),
            in_specs=in_specs,
            out_specs=[
                pl.BlockSpec((1, block, cols), lambda i, n: (0, base + i, 0)),
                pl.BlockSpec(memory_space=pltpu.SMEM),
            ],
            scratch_shapes=[pltpu.VMEM((8, cols), jnp.float32)],
        ),
        input_output_aliases=aliases,
        compiler_params=params(),
        cost_estimate=pl.CostEstimate(
            flops=4 * count * cols, bytes_accessed=12 * count * cols, transcendentals=0
        ),
        name="finish_rows",
    )(info, *operands)


def on_device(psi, left_env, right_env, row_sizes, col_sizes):
    sectors = lax.axis_size("sec")
    sector = lax.axis_index("sec")
    even = sector % 2 == 0
    place = sector % 4

    def send(value, *hops):
        pairs = [
            (s, s + steps)
            for at, steps in hops
            for s in range(at, sectors, 4)
            if 0 <= s + steps < sectors
        ]
        return lax.ppermute(value, "sec", pairs)

    rows = psi.shape[1]
    part = rows // PARTS
    sizes = jnp.concatenate([row_sizes, col_sizes])
    live = masked(psi[0], sizes)
    one = jnp.where(even, 2, 1).astype(jnp.int32)
    two = jnp.where(even, 3, 2).astype(jnp.int32)
    three = jnp.where(even, 1, 3).astype(jnp.int32)

    first_blocks, second_blocks = [], []
    for p in range(PARTS):
        first_blocks.append(term_rows(one, live, left_env, right_env, p * part, part))
    for p in range(PARTS):
        second_blocks.append(term_rows(two, live, left_env, right_env, p * part, part))

    raised, relayed = [], []
    for p in range(PARTS):
        pair = send(first_blocks[p], (0, 1), (2, 1))
        both = first_blocks[p] + pair
        pairs_up = [(s, s + 1) for s in range(1, sectors, 4) if s + 1 < sectors]
        pairs_up += [(s, s - 3) for s in range(3, sectors, 4) if s + 1 < sectors]
        raised.append(lax.ppermute(both, "sec", pairs_up))
    crossed = []
    for p in range(PARTS):
        along = send(second_blocks[p], (3, 3), (0, -3))
        crossed.append(send(second_blocks[p] + along, (1, 2), (2, -1)))
    for p in range(PARTS):
        relayed.append(send(raised[p], (0, 4)))

    swapped, own = [], []
    for p in range(PARTS):
        third = term_rows(three, live, left_env, right_env, p * part, part)
        swapped.append(send(third, (0, 1), (1, -1), (2, 1), (3, -1)))
    for p in range(PARTS):
        own.append(
            term_rows(jnp.int32(0), live, left_env, right_env, p * part, part, swapped[p])
        )

    which = jnp.where(place == 0, 1, jnp.where(place == 2, 0, 2)).astype(jnp.int32)
    info = jnp.concatenate([sizes, jnp.reshape(which, (1,))])
    energy, sigma = jnp.zeros((1,), jnp.float32), None
    for p in range(PARTS):
        sigma, energy = finish(
            info, live, own[p], (raised[p], relayed[p], crossed[p]), energy, sigma, p * part
        )
    return sigma, lax.psum(energy, "sec")


def solution(mesh):
    return jax.shard_map(
        on_device,
        mesh=mesh,
        in_specs=(
            P(("grp", "sec"), None, None),
            P(("grp", "sec"), None, None, None),
            P(("grp", "sec"), None, None, None),
            P(("grp", "sec")),
            P(("grp", "sec")),
        ),
        out_specs=(P(("grp", "sec"), None, None), P("grp")),
        check_vma=False,
    )
```

```python
import functools

import jax
import jax.numpy as jnp
from jax import lax
from jax.experimental import pallas as pl
from jax.experimental.pallas import tpu as pltpu
from jax.sharding import PartitionSpec as P

PARTS = 2
MIB = 1024 * 1024

ANY = pl.BlockSpec(memory_space=pl.ANY)
HBM = pl.BlockSpec(memory_space=pltpu.HBM)
SMEM = pl.BlockSpec(memory_space=pltpu.SMEM)
WHOLE = pl.BlockSpec(memory_space=pltpu.VMEM)


def params(mib=8):
    return pltpu.CompilerParams(vmem_limit_bytes=mib * MIB)


def term_kernel(slot, first, blocks, masks, adds, tokens, *refs):
    refs = list(refs)
    info_ref, live_ref, left_hbm, right_hbm = refs[:4]
    refs = refs[4:]
    add_ref = refs.pop(0) if adds else None
    refs = refs[tokens:]
    out_ref = refs.pop(0)
    live_out = refs.pop(0) if masks else None
    left_buf, right_buf = refs[:2]
    sems = refs[-1]
    psi_buf = refs[2] if masks else None
    block = left_buf.shape[1]
    term = info_ref[slot]
    copies = []
    if masks:
        psi_copy = pltpu.make_async_copy(live_ref, psi_buf, sems.at[blocks + 1])
        psi_copy.start()
    for i in range(blocks):
        copy = pltpu.make_async_copy(
            left_hbm.at[0, term, pl.ds(first + i * block, block), :], left_buf.at[i], sems.at[i]
        )
        copy.start()
        copies.append(copy)
        if i == 0:
            right_copy = pltpu.make_async_copy(
                right_hbm.at[0, term], right_buf, sems.at[blocks]
            )
            right_copy.start()
    if masks:
        psi_copy.wait()
        rows, cols = psi_buf.shape
        step = 128
        col = lax.broadcasted_iota(jnp.int32, (step, cols), 1) < info_ref[5]
        row = lax.broadcasted_iota(jnp.int32, (step, cols), 0)
        for r in range(0, rows, step):
            inside = jnp.logical_and(row < info_ref[4] - r, col)
            values = psi_buf[r : r + step, :].astype(jnp.float32)
            live_out[r : r + step, :] = jnp.where(inside, values, 0.0).astype(jnp.bfloat16)
        live_ref = live_out
    for i in range(blocks):
        copies[i].wait()
        left = jnp.dot(left_buf[i], live_ref[...], preferred_element_type=jnp.float32)
        if i == 0:
            right_copy.wait()
        value = jnp.dot(
            left.astype(jnp.bfloat16), right_buf[...], preferred_element_type=jnp.float32
        )
        span = pl.ds(i * block, block)
        if adds:
            value = value + add_ref[span, :]
        out_ref[span, :] = value


def term_rows(
    info, slot, live, left_env, right_env, first, count, block, masks=False, added=None, tokens=()
):
    width, cols = live.shape[-2:]
    blocks = count // block
    in_specs = [SMEM, HBM if masks else WHOLE, HBM, HBM]
    operands = [info, live, left_env, right_env]
    if added is not None:
        in_specs.append(WHOLE)
        operands.append(added)
    in_specs += [ANY] * len(tokens)
    operands += tokens
    out_shape = [jax.ShapeDtypeStruct((count, cols), jnp.float32)]
    scratch = [
        pltpu.VMEM((blocks, block, width), jnp.bfloat16),
        pltpu.VMEM((cols, cols), jnp.bfloat16),
    ]
    if masks:
        out_shape.append(jax.ShapeDtypeStruct((width, cols), jnp.bfloat16))
        scratch.append(pltpu.VMEM((width, cols), jnp.bfloat16))
    scratch.append(pltpu.SemaphoreType.DMA((blocks + 2,)))
    out = pl.pallas_call(
        functools.partial(
            term_kernel, slot, first, blocks, masks, added is not None, len(tokens)
        ),
        out_shape=out_shape,
        in_specs=in_specs,
        out_specs=[WHOLE] * len(out_shape),
        scratch_shapes=scratch,
        compiler_params=params(50),
        cost_estimate=pl.CostEstimate(
            flops=2 * count * cols * (width + cols),
            bytes_accessed=2 * (count * width + cols * cols) + 4 * count * cols,
            transcendentals=0,
        ),
        name=f"term_slot{slot}",
    )(*operands)
    return out if masks else out[0]


def add_kernel(a_ref, b_ref, out_ref):
    rows = a_ref.shape[0]
    step = 64

    def body(i, _):
        span = pl.ds(pl.multiple_of(i * step, step), step)
        out_ref[span, :] = a_ref[span, :] + b_ref[span, :]
        return _

    lax.fori_loop(0, rows // step, body, 0)


def add(a, b):
    return pl.pallas_call(
        add_kernel,
        out_shape=jax.ShapeDtypeStruct(a.shape, a.dtype),
        in_specs=[WHOLE, WHOLE],
        out_specs=WHOLE,
        compiler_params=params(),
        cost_estimate=pl.CostEstimate(flops=a.size, bytes_accessed=12 * a.size, transcendentals=0),
        name="add_blocks",
    )(a, b)


def finish_kernel(first, steps, info_ref, live_ref, own_ref, a_ref, b_ref, c_ref, *refs):
    before_ref = refs[0]
    sigma_ref, energy_ref, sum_ref = refs[-3:]
    step = pl.program_id(0)
    block, cols = sigma_ref.shape[1:]
    span = pl.ds(pl.multiple_of(step * block, block), block)
    row = lax.broadcasted_iota(jnp.int32, (block, cols), 0) + (first + step * block)
    col = lax.broadcasted_iota(jnp.int32, (block, cols), 1)
    inside = jnp.logical_and(row < info_ref[4], col < info_ref[5])

    @pl.when(step == 0)
    def _():
        sum_ref[...] = jnp.zeros_like(sum_ref)

    def work(arrival):
        total = jnp.where(inside, own_ref[span, :] + arrival[span, :], 0.0)
        sigma_ref[0] = total.astype(sigma_ref.dtype)
        here = pl.ds(pl.multiple_of(first + step * block, block), block)
        product = live_ref[here, :].astype(jnp.float32) * total
        sum_ref[...] += jnp.sum(jnp.reshape(product, (block // 8, 8, cols)), axis=0)

    for n, arrival in enumerate((a_ref, b_ref, c_ref)):
        pl.when(info_ref[6] == n)(functools.partial(work, arrival))

    @pl.when(step == steps - 1)
    def _():
        energy_ref[0] = before_ref[0] + jnp.sum(sum_ref[...])


def finish(info, live, own, arrivals, before, sigma, first):
    count, cols = own.shape
    block = 128
    base = first // block
    steps = count // block
    in_specs = [SMEM] + [WHOLE] * 5 + [SMEM]
    operands = [info, live, own, *arrivals, before]
    aliases = {}
    if sigma is not None:
        in_specs.append(ANY)
        aliases = {len(operands): 0}
        operands.append(sigma)
    return pl.pallas_call(
        functools.partial(finish_kernel, first, steps),
        out_shape=(
            jax.ShapeDtypeStruct((1, *live.shape), jnp.bfloat16),
            jax.ShapeDtypeStruct((1,), jnp.float32),
        ),
        grid=(steps,),
        in_specs=in_specs,
        out_specs=[pl.BlockSpec((1, block, cols), lambda i: (0, base + i, 0)), SMEM],
        scratch_shapes=[pltpu.VMEM((8, cols), jnp.float32)],
        input_output_aliases=aliases,
        compiler_params=params(),
        cost_estimate=pl.CostEstimate(
            flops=4 * count * cols, bytes_accessed=12 * count * cols, transcendentals=0
        ),
        name="finish_rows",
    )(*operands)


def sum_over_sectors(value, sectors):
    if sectors & (sectors - 1):
        return lax.psum(value, "sec")
    stride = 1
    while stride < sectors:
        radix = min(4, sectors // stride)
        arrived = [
            lax.ppermute(value, "sec", [(s, s ^ (n * stride)) for s in range(sectors)])
            for n in range(1, radix)
        ]
        if radix == 4:
            value = (value + arrived[0]) + (arrived[1] + arrived[2])
        else:
            value = value + arrived[0]
        stride *= radix
    return value


def on_device(psi, left_env, right_env, row_sizes, col_sizes):
    sectors = lax.axis_size("sec")
    sector = lax.axis_index("sec")
    even = sector % 2 == 0
    place = sector % 4

    def send(value, *hops):
        pairs = [
            (s, s + steps)
            for at, steps in hops
            for s in range(at, sectors, 4)
            if 0 <= s + steps < sectors
        ]
        return lax.ppermute(value, "sec", pairs)

    rows = psi.shape[1]
    part = rows // PARTS
    which = jnp.where(place == 0, 1, jnp.where(place == 2, 0, 2))
    orders = [jnp.where(even, 2, 1), jnp.where(even, 3, 2), jnp.where(even, 1, 3), 0]
    info = jnp.stack([*orders, row_sizes[0], col_sizes[0], which]).astype(jnp.int32)

    first_blocks, raised, both = [], [], []
    block, live = term_rows(info, 0, psi[0], left_env, right_env, 0, part, part, masks=True)
    first_blocks.append(block)
    for p in range(1, PARTS):
        first_blocks.append(term_rows(info, 0, live, left_env, right_env, p * part, part, part))
    pairs_up = [(s, s + 1) for s in range(1, sectors, 4) if s + 1 < sectors]
    pairs_up += [(s, s - 3) for s in range(3, sectors, 4) if s + 1 < sectors]
    for p in range(PARTS):
        both.append(add(first_blocks[p], send(first_blocks[p], (0, 1), (2, 1))))
        raised.append(lax.ppermute(both[p], "sec", pairs_up))

    crossed = []
    for p in range(PARTS):
        block = term_rows(
            info, 1, live, left_env, right_env, p * part, part, 256, tokens=(both[p],)
        )
        along = send(block, (3, 3), (0, -3))
        crossed.append(send(add(block, along), (1, 2), (2, -1)))

    swapped, own, relayed = [], [], []
    for p in range(PARTS):
        third = term_rows(
            info, 2, live, left_env, right_env, p * part, part, 128, tokens=(both[-1],)
        )
        swapped.append(send(third, (0, 1), (1, -1), (2, 1), (3, -1)))
    for p in range(PARTS):
        own.append(
            term_rows(
                info, 3, live, left_env, right_env, p * part, part, 64, added=swapped[p]
            )
        )
    for p in range(PARTS):
        relayed.append(send(raised[p], (0, 4)))

    energy, sigma = jnp.zeros((1,), jnp.float32), None
    for p in range(PARTS):
        sigma, energy = finish(
            info, live, own[p], (raised[p], relayed[p], crossed[p]), energy, sigma, p * part
        )
    return sigma, sum_over_sectors(energy, sectors)


def solution(mesh):
    return jax.shard_map(
        on_device,
        mesh=mesh,
        in_specs=(
            P(("grp", "sec"), None, None),
            P(("grp", "sec"), None, None, None),
            P(("grp", "sec"), None, None, None),
            P(("grp", "sec")),
            P(("grp", "sec")),
        ),
        out_specs=(P(("grp", "sec"), None, None), P("grp")),
        check_vma=False,
    )
```

```python
import functools

import jax
import jax.numpy as jnp
from jax import lax
from jax.experimental import pallas as pl
from jax.experimental.pallas import tpu as pltpu
from jax.sharding import PartitionSpec as P

MIB = 1024 * 1024

ANY = pl.BlockSpec(memory_space=pl.ANY)
HBM = pl.BlockSpec(memory_space=pltpu.HBM)
SMEM = pl.BlockSpec(memory_space=pltpu.SMEM)
WHOLE = pl.BlockSpec(memory_space=pltpu.VMEM)
TOKEN = jax.ShapeDtypeStruct((8, 128), jnp.float32)
SMALL = pl.CostEstimate(flops=200000000, bytes_accessed=1000000, transcendentals=0)


def params(mib=8):
    return pltpu.CompilerParams(vmem_limit_bytes=mib * MIB)


def term_kernel(slot, first, blocks, masks, adds, tokens, *refs):
    refs = list(refs)
    info_ref, live_ref, left_hbm, right_hbm = refs[:4]
    refs = refs[4:]
    add_ref = refs.pop(0) if adds else None
    refs = refs[tokens:]
    out_ref, _ = refs[:2]
    refs = refs[2:]
    live_out = refs.pop(0) if masks else None
    left_buf, right_buf = refs[:2]
    sems = refs[-1]
    psi_buf = refs[2] if masks else None
    block = left_buf.shape[1]
    term = info_ref[slot]
    copies = []
    if masks:
        psi_copy = pltpu.make_async_copy(live_ref, psi_buf, sems.at[blocks + 1])
        psi_copy.start()
    for i in range(blocks):
        copy = pltpu.make_async_copy(
            left_hbm.at[0, term, pl.ds(first + i * block, block), :], left_buf.at[i], sems.at[i]
        )
        copy.start()
        copies.append(copy)
        if i == 0:
            right_copy = pltpu.make_async_copy(
                right_hbm.at[0, term], right_buf, sems.at[blocks]
            )
            right_copy.start()
    if masks:
        psi_copy.wait()
        rows, cols = psi_buf.shape
        step = 128
        col = lax.broadcasted_iota(jnp.int32, (step, cols), 1) < info_ref[5]
        row = lax.broadcasted_iota(jnp.int32, (step, cols), 0)
        for r in range(0, rows, step):
            inside = jnp.logical_and(row < info_ref[4] - r, col)
            values = psi_buf[r : r + step, :].astype(jnp.float32)
            live_out[r : r + step, :] = jnp.where(inside, values, 0.0).astype(jnp.bfloat16)
        live_ref = live_out
    for i in range(blocks):
        copies[i].wait()
        left = jnp.dot(left_buf[i], live_ref[...], preferred_element_type=jnp.float32)
        if i == 0:
            right_copy.wait()
        value = jnp.dot(
            left.astype(jnp.bfloat16), right_buf[...], preferred_element_type=jnp.float32
        )
        span = pl.ds(i * block, block)
        if adds:
            value = value + add_ref[span, :]
        out_ref[span, :] = value


def term_rows(
    info, slot, live, left_env, right_env, first, count, block, masks=False, added=None, tokens=()
):
    width, cols = live.shape[-2:]
    blocks = count // block
    in_specs = [SMEM, HBM if masks else WHOLE, HBM, HBM]
    operands = [info, live, left_env, right_env]
    if added is not None:
        in_specs.append(WHOLE)
        operands.append(added)
    in_specs += [ANY] * len(tokens)
    operands += tokens
    out_shape = [jax.ShapeDtypeStruct((count, cols), jnp.float32), TOKEN]
    scratch = [
        pltpu.VMEM((blocks, block, width), jnp.bfloat16),
        pltpu.VMEM((cols, cols), jnp.bfloat16),
    ]
    if masks:
        out_shape.append(jax.ShapeDtypeStruct((width, cols), jnp.bfloat16))
        scratch.append(pltpu.VMEM((width, cols), jnp.bfloat16))
    scratch.append(pltpu.SemaphoreType.DMA((blocks + 2,)))
    out = pl.pallas_call(
        functools.partial(
            term_kernel, slot, first, blocks, masks, added is not None, len(tokens)
        ),
        out_shape=out_shape,
        in_specs=in_specs,
        out_specs=[WHOLE, ANY] + [WHOLE] * (len(out_shape) - 2),
        scratch_shapes=scratch,
        compiler_params=params(50),
        cost_estimate=SMALL,
        name=f"term_slot{slot}",
    )(*operands)
    return out


def add_kernel(a_ref, b_ref, *refs):
    out_ref = refs[-2]
    rows = a_ref.shape[0]
    step = 64

    def body(i, _):
        span = pl.ds(pl.multiple_of(i * step, step), step)
        out_ref[span, :] = a_ref[span, :] + b_ref[span, :]
        return _

    lax.fori_loop(0, rows // step, body, 0)


def add(a, b, *tokens):
    return pl.pallas_call(
        add_kernel,
        out_shape=(jax.ShapeDtypeStruct(a.shape, a.dtype), TOKEN),
        in_specs=[WHOLE, WHOLE] + [ANY] * len(tokens),
        out_specs=(WHOLE, ANY),
        compiler_params=params(),
        cost_estimate=SMALL,
        name="add_blocks",
    )(a, b, *tokens)


def touch(*values):
    return pl.pallas_call(
        lambda *refs: None,
        out_shape=TOKEN,
        in_specs=[ANY] * len(values),
        out_specs=ANY,
        compiler_params=params(),
        cost_estimate=SMALL,
        name="touch",
    )(*values)


def finish_kernel(first, info_ref, live_ref, own_ref, a_ref, b_ref, c_ref, before_ref, *refs):
    sigma_hbm, energy_ref, sigma_buf, sems = refs[-4:]
    count, cols = own_ref.shape
    step = 64
    piece = count // sems.shape[0]
    col = lax.broadcasted_iota(jnp.int32, (step, cols), 1) < info_ref[5]
    row = lax.broadcasted_iota(jnp.int32, (step, cols), 0)

    def copy(i):
        span = pl.ds(i * piece, piece)
        return pltpu.make_async_copy(
            sigma_buf.at[span, :], sigma_hbm.at[0, pl.ds(first + i * piece, piece), :], sems.at[i]
        )

    def work(arrival):
        energy = jnp.zeros((8, cols), jnp.float32)
        for i in range(count // piece):

            def body(n, energy):
                start = pl.multiple_of(i * piece + n * step, step)
                span = pl.ds(start, step)
                inside = jnp.logical_and(row < info_ref[4] - first - start, col)
                total = jnp.where(inside, own_ref[span, :] + arrival[span, :], 0.0)
                sigma_buf[span, :] = total.astype(sigma_buf.dtype)
                here = pl.ds(pl.multiple_of(first + start, step), step)
                product = live_ref[here, :].astype(jnp.float32) * total
                return energy + jnp.sum(jnp.reshape(product, (step // 8, 8, cols)), axis=0)

            energy = lax.fori_loop(0, piece // step, body, energy)
            copy(i).start()
        energy_ref[...] = before_ref[...] + jnp.sum(energy)

    for n, arrival in enumerate((a_ref, b_ref, c_ref)):
        pl.when(info_ref[6] == n)(functools.partial(work, arrival))
    for i in range(count // piece):
        copy(i).wait()


def finish(info, live, own, arrivals, before, sigma, first):
    count, cols = own.shape
    in_specs = [SMEM] + [WHOLE] * 6
    operands = [info, live, own, *arrivals, before]
    aliases = {}
    if sigma is not None:
        in_specs.append(ANY)
        aliases = {len(operands): 0}
        operands.append(sigma)
    return pl.pallas_call(
        functools.partial(finish_kernel, first),
        out_shape=(
            jax.ShapeDtypeStruct((1, *live.shape), jnp.bfloat16),
            jax.ShapeDtypeStruct(before.shape, jnp.float32),
        ),
        in_specs=in_specs,
        out_specs=(ANY, WHOLE),
        scratch_shapes=[pltpu.VMEM((count, cols), jnp.bfloat16), pltpu.SemaphoreType.DMA((4,))],
        input_output_aliases=aliases,
        compiler_params=params(),
        cost_estimate=SMALL,
        name="finish_rows",
    )(*operands)


def sum_kernel(in_ref, out_ref):
    out_ref[0] = jnp.sum(in_ref[:, :1])


def sum_over_sectors(value):
    arrived = lax.all_to_all(value, "sec", 0, 0, tiled=True)
    return pl.pallas_call(
        sum_kernel,
        out_shape=jax.ShapeDtypeStruct((1,), jnp.float32),
        in_specs=[WHOLE],
        out_specs=SMEM,
        compiler_params=params(),
        cost_estimate=SMALL,
        name="sum_energy",
    )(arrived)


def on_device(psi, left_env, right_env, row_sizes, col_sizes):
    sectors = lax.axis_size("sec")
    sector = lax.axis_index("sec")
    even = sector % 2 == 0
    place = sector % 4

    def send(value, *hops):
        pairs = [
            (s, s + steps)
            for at, steps in hops
            for s in range(at, sectors, 4)
            if 0 <= s + steps < sectors
        ]
        return lax.ppermute(value, "sec", pairs)

    rows = psi.shape[1]
    part = rows // 2
    which = jnp.where(place == 0, 1, jnp.where(place == 2, 0, 2))
    orders = [jnp.where(even, 2, 1), jnp.where(even, 3, 2), jnp.where(even, 1, 3), 0]
    info = jnp.stack([*orders, row_sizes[0], col_sizes[0], which]).astype(jnp.int32)

    def rows_of(slot, p, *tokens, added=None):
        return term_rows(
            info, slot, live, left_env, right_env, p * part, part, 512, added=added, tokens=tokens
        )

    pairs_up = [(s, s + 1) for s in range(1, sectors, 4) if s + 1 < sectors]
    pairs_up += [(s, s - 3) for s in range(3, sectors, 4) if s + 1 < sectors]

    def raise_one(value):
        return lax.ppermute(value, "sec", pairs_up)

    def up_chip(value):
        return send(value, (0, 1), (2, 1))

    def along(value):
        return send(value, (3, 3), (0, -3))

    def across(value):
        return send(value, (1, 2), (2, -1))

    def swap(value):
        return send(value, (0, 1), (1, -1), (2, 1), (3, -1))

    def relay(value):
        return send(value, (0, 4))

    first0, token, live = term_rows(
        info, 0, psi[0], left_env, right_env, 0, part, 512, masks=True
    )
    paired0 = up_chip(first0)
    first1, token = rows_of(0, 1, token)
    paired1 = up_chip(first1)
    both0, token = add(first0, paired0, token)
    raised0 = raise_one(both0)
    second0, token = rows_of(1, 0, token)
    moved0 = along(second0)
    both1, token = add(first1, paired1, token)
    raised1 = raise_one(both1)
    second1, token = rows_of(1, 1, token)
    moved1 = along(second1)
    third0, token = rows_of(2, 0, token)
    swapped0 = swap(third0)
    token = touch(raised0, token)
    relayed0 = relay(raised0)
    third1, token = rows_of(2, 1, token)
    swapped1 = swap(third1)
    summed0, token = add(second0, moved0, token)
    crossed0 = across(summed0)
    own0, token = rows_of(3, 0, token, added=swapped0)
    token = touch(raised1, token)
    relayed1 = relay(raised1)
    summed1, token = add(second1, moved1, token)
    crossed1 = across(summed1)
    token = touch(relayed0, token)
    own1, token = rows_of(3, 1, token, added=swapped1)

    energy = jnp.zeros((sectors, 128), jnp.float32)
    sigma, energy = finish(info, live, own0, (raised0, relayed0, crossed0), energy, None, 0)
    sigma, energy = finish(info, live, own1, (raised1, relayed1, crossed1), energy, sigma, part)
    return sigma, sum_over_sectors(energy)


def solution(mesh):
    return jax.shard_map(
        on_device,
        mesh=mesh,
        in_specs=(
            P(("grp", "sec"), None, None),
            P(("grp", "sec"), None, None, None),
            P(("grp", "sec"), None, None, None),
            P(("grp", "sec")),
            P(("grp", "sec")),
        ),
        out_specs=(P(("grp", "sec"), None, None), P("grp")),
        check_vma=False,
    )
```

```python
import functools

import jax
import jax.numpy as jnp
from jax import lax
from jax.experimental import pallas as pl
from jax.experimental.pallas import tpu as pltpu
from jax.sharding import PartitionSpec as P

MIB = 1024 * 1024

ANY = pl.BlockSpec(memory_space=pl.ANY)
HBM = pl.BlockSpec(memory_space=pltpu.HBM)
SMEM = pl.BlockSpec(memory_space=pltpu.SMEM)
WHOLE = pl.BlockSpec(memory_space=pltpu.VMEM)
TOKEN = jax.ShapeDtypeStruct((8, 128), jnp.float32)
SMALL = pl.CostEstimate(flops=200000000, bytes_accessed=1000000, transcendentals=0)


def params(mib=8):
    return pltpu.CompilerParams(vmem_limit_bytes=mib * MIB)


def mask_kernel(first, info_ref, psi_hbm, live_ref, wide_ref, _, psi_buf, sems):
    pieces = sems.shape[0]
    rows, cols = psi_buf.shape
    step = rows // pieces

    def copy(i):
        span = pl.ds(i * step, step)
        return pltpu.make_async_copy(psi_hbm.at[span, :], psi_buf.at[span, :], sems.at[i])

    for i in range(pieces):
        copy(i).start()
    col = lax.broadcasted_iota(jnp.int32, (step, cols), 1) < info_ref[5]
    row = lax.broadcasted_iota(jnp.int32, (step, cols), 0)
    for i in range(pieces):
        copy(i).wait()
        start = i * step
        inside = jnp.logical_and(row < info_ref[4] - start, col)
        values = jnp.where(inside, psi_buf[start : start + step, :].astype(jnp.float32), 0.0)
        live_ref[start : start + step, :] = values.astype(live_ref.dtype)
        if start >= first:
            wide_ref[start - first : start - first + step, :] = values


def masked(info, psi, first):
    rows, cols = psi.shape
    return pl.pallas_call(
        functools.partial(mask_kernel, first),
        out_shape=(
            jax.ShapeDtypeStruct(psi.shape, psi.dtype),
            jax.ShapeDtypeStruct((rows - first, cols), jnp.float32),
            TOKEN,
        ),
        in_specs=[SMEM, HBM],
        out_specs=(WHOLE, WHOLE, ANY),
        scratch_shapes=[pltpu.VMEM(psi.shape, psi.dtype), pltpu.SemaphoreType.DMA((8,))],
        compiler_params=params(52),
        cost_estimate=SMALL,
        name="mask_psi",
    )(info, psi)


def term_kernel(slot, first, blocks, adds, tokens, *refs):
    refs = list(refs)
    info_ref, live_ref, left_hbm, right_hbm = refs[:4]
    refs = refs[4:]
    add_ref = refs.pop(0) if adds else None
    refs = refs[tokens:]
    out_ref, _, left_buf, right_buf, sems = refs
    block = left_buf.shape[1]
    term = info_ref[slot]
    copies = []
    for i in range(blocks):
        copy = pltpu.make_async_copy(
            left_hbm.at[0, term, pl.ds(first + i * block, block), :], left_buf.at[i], sems.at[i]
        )
        copy.start()
        copies.append(copy)
        if i == 0:
            right_copy = pltpu.make_async_copy(
                right_hbm.at[0, term], right_buf, sems.at[blocks]
            )
            right_copy.start()
    for i in range(blocks):
        copies[i].wait()
        left = jnp.dot(left_buf[i], live_ref[...], preferred_element_type=jnp.float32)
        if i == 0:
            right_copy.wait()
        value = jnp.dot(
            left.astype(jnp.bfloat16), right_buf[...], preferred_element_type=jnp.float32
        )
        span = pl.ds(i * block, block)
        if adds:
            value = value + add_ref[span, :]
        out_ref[span, :] = value


def term_rows(
    info, slot, live, left_env, right_env, first, count, added=None, tokens=()
):
    width, cols = live.shape[-2:]
    blocks, block = 1, count
    in_specs = [SMEM, WHOLE, HBM, HBM]
    operands = [info, live, left_env, right_env]
    if added is not None:
        in_specs.append(WHOLE)
        operands.append(added)
    in_specs += [ANY] * len(tokens)
    operands += tokens
    out_shape = [jax.ShapeDtypeStruct((count, cols), jnp.float32), TOKEN]
    scratch = [
        pltpu.VMEM((blocks, block, width), jnp.bfloat16),
        pltpu.VMEM((cols, cols), jnp.bfloat16),
    ]
    scratch.append(pltpu.SemaphoreType.DMA((blocks + 1,)))
    out = pl.pallas_call(
        functools.partial(
            term_kernel, slot, first, blocks, added is not None, len(tokens)
        ),
        out_shape=out_shape,
        in_specs=in_specs,
        out_specs=[WHOLE, ANY],
        scratch_shapes=scratch,
        compiler_params=params(50),
        cost_estimate=SMALL,
        name=f"term_slot{slot}",
    )(*operands)
    return out


def add_kernel(a_ref, b_ref, *refs):
    out_ref = refs[-2]
    step = 64

    def body(i, _):
        span = pl.ds(pl.multiple_of(i * step, step), step)
        out_ref[span, :] = a_ref[span, :] + b_ref[span, :]
        return _

    lax.fori_loop(0, a_ref.shape[0] // step, body, 0)


def add(a, b, *tokens):
    return pl.pallas_call(
        add_kernel,
        out_shape=(jax.ShapeDtypeStruct(a.shape, a.dtype), TOKEN),
        in_specs=[WHOLE, WHOLE] + [ANY] * len(tokens),
        out_specs=(WHOLE, ANY),
        compiler_params=params(),
        cost_estimate=SMALL,
        name="add_blocks",
    )(a, b, *tokens)


def folded(values):
    rows, cols = values.shape
    return jnp.sum(jnp.reshape(values, (rows // 8, 8, cols)), axis=0)


def add_energy_kernel(a_ref, b_ref, psi_ref, _, out_ref, energy_ref, token_ref):
    step = 64

    def body(i, energy):
        span = pl.ds(pl.multiple_of(i * step, step), step)
        value = a_ref[span, :] + b_ref[span, :]
        out_ref[span, :] = value
        return energy + folded(value * psi_ref[span, :])

    zero = jnp.zeros((8, a_ref.shape[1]), jnp.float32)
    energy_ref[...] = lax.fori_loop(0, a_ref.shape[0] // step, body, zero)


def add_energy(a, b, psi, token):
    return pl.pallas_call(
        add_energy_kernel,
        out_shape=(
            jax.ShapeDtypeStruct(a.shape, a.dtype),
            jax.ShapeDtypeStruct((8, a.shape[1]), jnp.float32),
            TOKEN,
        ),
        in_specs=[WHOLE, WHOLE, WHOLE, ANY],
        out_specs=(WHOLE, WHOLE, ANY),
        compiler_params=params(),
        cost_estimate=SMALL,
        name="add_blocks_energy",
    )(a, b, psi, token)


def rest_kernel(first, info_ref, live_ref, own_ref, a_ref, b_ref, before_ref, out_ref):
    count, cols = own_ref.shape
    step = 64

    def work(arrival):
        def body(i, energy):
            start = pl.multiple_of(i * step, step)
            span = pl.ds(start, step)
            value = own_ref[span, :]
            if arrival is not None:
                value = value + arrival[span, :]
            here = pl.ds(pl.multiple_of(first + start, step), step)
            return energy + folded(value * live_ref[here, :].astype(jnp.float32))

        energy = lax.fori_loop(0, count // step, body, before_ref[...])
        out_ref[...] = jnp.full(out_ref.shape, jnp.sum(energy), jnp.float32)

    for n, arrival in enumerate((a_ref, b_ref, None)):
        pl.when(info_ref[6] == n)(functools.partial(work, arrival))


def rest(info, live, own, arrivals, before, first, sectors):
    return pl.pallas_call(
        functools.partial(rest_kernel, first),
        out_shape=jax.ShapeDtypeStruct((sectors, 128), jnp.float32),
        in_specs=[SMEM] + [WHOLE] * 5,
        out_specs=WHOLE,
        compiler_params=params(),
        cost_estimate=SMALL,
        name="rest_of_energy",
    )(info, live, own, *arrivals, before)


def touch(*values):
    return pl.pallas_call(
        lambda *refs: None,
        out_shape=TOKEN,
        in_specs=[ANY] * len(values),
        out_specs=ANY,
        compiler_params=params(),
        cost_estimate=SMALL,
        name="touch",
    )(*values)


def finish_kernel(first, info_ref, live_ref, own_ref, a_ref, b_ref, c_ref, before_ref, *refs):
    sigma_hbm, energy_ref, sigma_buf, sems = refs[-4:]
    count, cols = own_ref.shape
    step = 32
    piece = count // sems.shape[0]
    col = lax.broadcasted_iota(jnp.int32, (step, cols), 1) < info_ref[5]
    row = lax.broadcasted_iota(jnp.int32, (step, cols), 0)

    def copy(i):
        span = pl.ds(i * piece, piece)
        return pltpu.make_async_copy(
            sigma_buf.at[span, :], sigma_hbm.at[0, pl.ds(first + i * piece, piece), :], sems.at[i]
        )

    def work(arrival):
        energy = before_ref[...]
        for i in range(count // piece):

            def body(n, energy):
                start = pl.multiple_of(i * piece + n * step, step)
                span = pl.ds(start, step)
                inside = jnp.logical_and(row < info_ref[4] - first - start, col)
                total = jnp.where(inside, own_ref[span, :] + arrival[span, :], 0.0)
                sigma_buf[span, :] = total.astype(sigma_buf.dtype)
                if first > 0:
                    return energy
                here = pl.ds(pl.multiple_of(first + start, step), step)
                return energy + folded(live_ref[here, :].astype(jnp.float32) * total)

            energy = lax.fori_loop(0, piece // step, body, energy)
            copy(i).start()
        energy_ref[...] = energy

    for n, arrival in enumerate((a_ref, b_ref, c_ref)):
        pl.when(info_ref[6] == n)(functools.partial(work, arrival))
    for i in range(count // piece):
        copy(i).wait()


def finish(info, live, own, arrivals, before, sigma, first, *tokens):
    count, cols = own.shape
    in_specs = [SMEM] + [WHOLE] * 6
    operands = [info, live, own, *arrivals, before]
    aliases = {}
    if sigma is not None:
        in_specs.append(ANY)
        aliases = {len(operands): 0}
        operands.append(sigma)
    in_specs += [ANY] * len(tokens)
    operands += tokens
    return pl.pallas_call(
        functools.partial(finish_kernel, first),
        out_shape=(
            jax.ShapeDtypeStruct((1, *live.shape), jnp.bfloat16),
            jax.ShapeDtypeStruct(before.shape, jnp.float32),
        ),
        in_specs=in_specs,
        out_specs=(ANY, WHOLE),
        scratch_shapes=[pltpu.VMEM((count, cols), jnp.bfloat16), pltpu.SemaphoreType.DMA((4,))],
        input_output_aliases=aliases,
        compiler_params=params(),
        cost_estimate=SMALL,
        name="finish_rows",
    )(*operands)


def sum_kernel(in_ref, out_ref):
    out_ref[0] = jnp.sum(in_ref[:, :1])


def sum_over_sectors(value):
    arrived = lax.all_to_all(value, "sec", 0, 0, tiled=True)
    return pl.pallas_call(
        sum_kernel,
        out_shape=jax.ShapeDtypeStruct((1,), jnp.float32),
        in_specs=[WHOLE],
        out_specs=SMEM,
        compiler_params=params(),
        cost_estimate=SMALL,
        name="sum_energy",
    )(arrived)


def on_device(psi, left_env, right_env, row_sizes, col_sizes):
    sectors = lax.axis_size("sec")
    sector = lax.axis_index("sec")
    even = sector % 2 == 0
    place = sector % 4

    def send(value, *hops):
        pairs = [
            (s, s + steps)
            for at, steps in hops
            for s in range(at, sectors, 4)
            if 0 <= s + steps < sectors
        ]
        return lax.ppermute(value, "sec", pairs)

    rows = psi.shape[1]
    part = rows * 5 // 8
    which = jnp.where(place == 0, 1, jnp.where(place == 2, 0, 2))
    orders = [jnp.where(even, 2, 1), jnp.where(even, 3, 2), jnp.where(even, 1, 3), 0]
    info = jnp.stack([*orders, row_sizes[0], col_sizes[0], which]).astype(jnp.int32)

    def rows_of(slot, p, *tokens, added=None):
        count = rows - part if p else part
        return term_rows(
            info, slot, live, left_env, right_env, p * part, count, added=added, tokens=tokens
        )

    pairs_up = [(s, s + 1) for s in range(1, sectors, 4) if s + 1 < sectors]
    pairs_up += [(s, s - 3) for s in range(3, sectors, 4) if s + 1 < sectors]

    def raise_one(value):
        return lax.ppermute(value, "sec", pairs_up)

    def up_chip(value):
        return send(value, (0, 1), (2, 1))

    def along(value):
        return send(value, (3, 3), (0, -3))

    def across(value):
        return send(value, (1, 2), (2, -1))

    def swap(value):
        return send(value, (0, 1), (1, -1), (2, 1), (3, -1))

    def relay(value):
        return send(value, (0, 4))

    live, wide, token = masked(info, psi[0], part)
    seen = send(wide, (3, -2), (1, 1))
    first0, token = rows_of(0, 0, token)
    paired0 = up_chip(first0)
    first1, token = rows_of(0, 1, token)
    paired1 = up_chip(first1)
    both0, token = add(first0, paired0, token)
    raised0 = raise_one(both0)
    second0, token = rows_of(1, 0, token, seen)
    moved0 = along(second0)
    both1, token = add(first1, paired1, token)
    raised1 = raise_one(both1)
    second1, token = rows_of(1, 1, token)
    moved1 = along(second1)
    third0, token = rows_of(2, 0, token)
    swapped0 = swap(third0)
    token = touch(raised0, token)
    relayed0 = relay(raised0)
    third1, token = rows_of(2, 1, token)
    swapped1 = swap(third1)
    summed0, token = add(second0, moved0, token)
    crossed0 = across(summed0)
    token = touch(raised1, token)
    relayed1 = relay(raised1)
    own0, token = rows_of(3, 0, token, added=swapped0)
    summed1, energy, token = add_energy(second1, moved1, seen, token)
    crossed1 = across(summed1)
    token = touch(relayed0, token)
    own1, token = rows_of(3, 1, token, added=swapped1)

    sigma, energy = finish(info, live, own0, (raised0, relayed0, crossed0), energy, None, 0)
    energy = rest(info, live, own1, (raised1, relayed1), energy, part, sectors)
    energy = sum_over_sectors(energy)
    none = jnp.zeros((8, 128), jnp.float32)
    sigma, _ = finish(
        info, live, own1, (raised1, relayed1, crossed1), none, sigma, part, energy
    )
    return sigma, energy


def solution(mesh):
    return jax.shard_map(
        on_device,
        mesh=mesh,
        in_specs=(
            P(("grp", "sec"), None, None),
            P(("grp", "sec"), None, None, None),
            P(("grp", "sec"), None, None, None),
            P(("grp", "sec")),
            P(("grp", "sec")),
        ),
        out_specs=(P(("grp", "sec"), None, None), P("grp")),
        check_vma=False,
    )
```

```python
import functools

import jax
import jax.numpy as jnp
from jax import lax
from jax.experimental import pallas as pl
from jax.experimental.pallas import tpu as pltpu
from jax.sharding import PartitionSpec as P

MIB = 1024 * 1024
FIRST_MIB = 44
BRING_MIB = 42

ANY = pl.BlockSpec(memory_space=pl.ANY)
HBM = pl.BlockSpec(memory_space=pltpu.HBM)
SMEM = pl.BlockSpec(memory_space=pltpu.SMEM)
WHOLE = pl.BlockSpec(memory_space=pltpu.VMEM)
TOKEN = jax.ShapeDtypeStruct((8, 128), jnp.float32)
SMALL = pl.CostEstimate(flops=200000000, bytes_accessed=1000000, transcendentals=0)


def params(mib=8):
    return pltpu.CompilerParams(vmem_limit_bytes=mib * MIB)


def fetch(info_ref, slot, left_hbm, right_hbm, left_ref, right_ref, sems):
    term = info_ref[slot]
    half = left_ref.shape[0] // 2
    copies = []
    for i in range(2):
        span = pl.ds(i * half, half)
        copies.append(
            pltpu.make_async_copy(left_hbm.at[0, term, span, :], left_ref.at[span, :], sems.at[i])
        )
    copies.insert(1, pltpu.make_async_copy(right_hbm.at[0, term], right_ref, sems.at[2]))
    return copies


def multiply(left, live, right):
    first = jnp.dot(left, live, preferred_element_type=jnp.float32).astype(jnp.bfloat16)
    return jnp.dot(first, right, preferred_element_type=jnp.float32)


def first_kernel(info_ref, psi_hbm, left_hbm, right_hbm, *refs):
    out_ref, _, live_ref, left0, right0, left1, right1, psi_buf, sems, psi_sems = refs
    pieces = psi_sems.shape[0]
    rows, cols = psi_buf.shape
    step = rows // pieces

    def copy(i):
        span = pl.ds(i * step, step)
        return pltpu.make_async_copy(psi_hbm.at[span, :], psi_buf.at[span, :], psi_sems.at[i])

    for i in range(pieces):
        copy(i).start()
    needed = fetch(info_ref, 0, left_hbm, right_hbm, left0, right0, sems.at[0])
    ahead = fetch(info_ref, 1, left_hbm, right_hbm, left1, right1, sems.at[1])
    needed[0].start()
    needed[1].start()
    col = lax.broadcasted_iota(jnp.int32, (step, cols), 1) < info_ref[5]
    row = lax.broadcasted_iota(jnp.int32, (step, cols), 0)
    for i in range(pieces):
        copy(i).wait()
        inside = jnp.logical_and(row < info_ref[4] - i * step, col)
        values = psi_buf[i * step : (i + 1) * step, :].astype(jnp.float32)
        live_ref[i * step : (i + 1) * step, :] = jnp.where(inside, values, 0.0).astype(
            live_ref.dtype
        )
    for later in (needed[2], *ahead):
        later.start()
    needed[0].wait()
    needed[1].wait()
    out_ref[...] = multiply(left0[: out_ref.shape[0], :], live_ref[...], right0[...])
    for later in (needed[2], *ahead):
        later.wait()


def operand_shapes(width, cols):
    return [
        jax.ShapeDtypeStruct((width, width), jnp.bfloat16),
        jax.ShapeDtypeStruct((cols, cols), jnp.bfloat16),
    ]


def first_rows(info, psi, left_env, right_env, count):
    width, cols = psi.shape
    out_shape = [jax.ShapeDtypeStruct((count, cols), jnp.float32), TOKEN]
    out_shape += [jax.ShapeDtypeStruct(psi.shape, psi.dtype), *operand_shapes(width, cols) * 2]
    return pl.pallas_call(
        first_kernel,
        out_shape=out_shape,
        in_specs=[SMEM, HBM, HBM, HBM],
        out_specs=[WHOLE, ANY] + [WHOLE] * 5,
        scratch_shapes=[
            pltpu.VMEM(psi.shape, psi.dtype),
            pltpu.SemaphoreType.DMA((2, 3)),
            pltpu.SemaphoreType.DMA((4,)),
        ],
        compiler_params=params(FIRST_MIB),
        cost_estimate=SMALL,
        name="first_rows",
    )(info, psi, left_env, right_env)


def term_kernel(first, adds, slot, tokens, info_ref, live_ref, left_ref, right_ref, *refs):
    refs = list(refs)
    add_ref = refs.pop(0) if adds else None
    copies = []
    if slot is not None:
        left_hbm, right_hbm = refs[:2]
        sems = refs[-1]
        out_ref, _, left_next, right_next = refs[2 + tokens : -1]
        copies = fetch(info_ref, slot, left_hbm, right_hbm, left_next, right_next, sems)
        for copy in copies:
            copy.start()
    else:
        out_ref, _ = refs[tokens:]
    count = out_ref.shape[0]
    block = min(count, 512)
    for i in range(count // block):
        span = pl.ds(i * block, block)
        value = multiply(left_ref[pl.ds(first + i * block, block), :], live_ref[...], right_ref[...])
        if adds:
            value = value + add_ref[span, :]
        out_ref[span, :] = value
    for copy in copies:
        copy.wait()


def term_rows(info, live, operands, first, count, *tokens, added=None, bring=None):
    width, cols = live.shape
    in_specs = [SMEM, WHOLE, WHOLE, WHOLE]
    args = [info, live, *operands]
    out_shape = [jax.ShapeDtypeStruct((count, cols), jnp.float32), TOKEN]
    out_specs = [WHOLE, ANY]
    scratch = []
    slot = None
    if added is not None:
        in_specs.append(WHOLE)
        args.append(added)
    if bring is not None:
        slot = bring[0]
        in_specs += [HBM, HBM]
        args += bring[1:]
        out_shape += operand_shapes(width, cols)
        out_specs += [WHOLE, WHOLE]
        scratch.append(pltpu.SemaphoreType.DMA((3,)))
    return pl.pallas_call(
        functools.partial(term_kernel, first, added is not None, slot, len(tokens)),
        out_shape=out_shape,
        in_specs=in_specs + [ANY] * len(tokens),
        out_specs=out_specs,
        scratch_shapes=scratch,
        compiler_params=params(12 if slot is None else BRING_MIB),
        cost_estimate=SMALL,
        name="term_rows",
    )(*args, *tokens)


def add_kernel(a_ref, b_ref, *refs):
    out_ref = refs[-2]
    rows = a_ref.shape[0]
    step = 64

    def body(i, _):
        span = pl.ds(pl.multiple_of(i * step, step), step)
        out_ref[span, :] = a_ref[span, :] + b_ref[span, :]
        return _

    lax.fori_loop(0, rows // step, body, 0)


def add(a, b, *tokens):
    return pl.pallas_call(
        add_kernel,
        out_shape=(jax.ShapeDtypeStruct(a.shape, a.dtype), TOKEN),
        in_specs=[WHOLE, WHOLE] + [ANY] * len(tokens),
        out_specs=(WHOLE, ANY),
        compiler_params=params(),
        cost_estimate=SMALL,
        name="add_blocks",
    )(a, b, *tokens)


def touch(*values):
    return pl.pallas_call(
        lambda *refs: None,
        out_shape=TOKEN,
        in_specs=[ANY] * len(values),
        out_specs=ANY,
        compiler_params=params(),
        cost_estimate=SMALL,
        name="touch",
    )(*values)


def finish_kernel(first, info_ref, live_ref, own_ref, a_ref, b_ref, c_ref, before_ref, *refs):
    sigma_hbm, energy_ref, sigma_buf, sems = refs[-4:]
    count, cols = own_ref.shape
    step = 64
    piece = count // sems.shape[0]
    col = lax.broadcasted_iota(jnp.int32, (step, cols), 1) < info_ref[5]
    row = lax.broadcasted_iota(jnp.int32, (step, cols), 0)

    def copy(i):
        span = pl.ds(i * piece, piece)
        return pltpu.make_async_copy(
            sigma_buf.at[span, :], sigma_hbm.at[0, pl.ds(first + i * piece, piece), :], sems.at[i]
        )

    def work(arrival):
        energy = jnp.zeros((8, cols), jnp.float32)
        for i in range(count // piece):

            def body(n, energy):
                start = pl.multiple_of(i * piece + n * step, step)
                span = pl.ds(start, step)
                inside = jnp.logical_and(row < info_ref[4] - first - start, col)
                total = jnp.where(inside, own_ref[span, :] + arrival[span, :], 0.0)
                sigma_buf[span, :] = total.astype(sigma_buf.dtype)
                here = pl.ds(pl.multiple_of(first + start, step), step)
                product = live_ref[here, :].astype(jnp.float32) * total
                return energy + jnp.sum(jnp.reshape(product, (step // 8, 8, cols)), axis=0)

            energy = lax.fori_loop(0, piece // step, body, energy)
            copy(i).start()
        energy_ref[...] = before_ref[...] + jnp.sum(energy)

    for n, arrival in enumerate((a_ref, b_ref, c_ref)):
        pl.when(info_ref[6] == n)(functools.partial(work, arrival))
    for i in range(count // piece):
        copy(i).wait()


def finish(info, live, own, arrivals, before, sigma, first):
    count, cols = own.shape
    in_specs = [SMEM] + [WHOLE] * 6
    operands = [info, live, own, *arrivals, before]
    aliases = {}
    if sigma is not None:
        in_specs.append(ANY)
        aliases = {len(operands): 0}
        operands.append(sigma)
    return pl.pallas_call(
        functools.partial(finish_kernel, first),
        out_shape=(
            jax.ShapeDtypeStruct((1, *live.shape), jnp.bfloat16),
            jax.ShapeDtypeStruct(before.shape, jnp.float32),
        ),
        in_specs=in_specs,
        out_specs=(ANY, WHOLE),
        scratch_shapes=[pltpu.VMEM((count, cols), jnp.bfloat16), pltpu.SemaphoreType.DMA((4,))],
        input_output_aliases=aliases,
        compiler_params=params(),
        cost_estimate=SMALL,
        name="finish_rows",
    )(*operands)


def sum_kernel(in_ref, out_ref):
    out_ref[0] = jnp.sum(in_ref[:, :1])


def sum_over_sectors(value):
    arrived = lax.all_to_all(value, "sec", 0, 0, tiled=True)
    return pl.pallas_call(
        sum_kernel,
        out_shape=jax.ShapeDtypeStruct((1,), jnp.float32),
        in_specs=[WHOLE],
        out_specs=SMEM,
        compiler_params=params(),
        cost_estimate=SMALL,
        name="sum_energy",
    )(arrived)


def on_device(psi, left_env, right_env, row_sizes, col_sizes):
    sectors = lax.axis_size("sec")
    sector = lax.axis_index("sec")
    even = sector % 2 == 0
    place = sector % 4

    def send(value, *hops):
        pairs = [
            (s, s + steps)
            for at, steps in hops
            for s in range(at, sectors, 4)
            if 0 <= s + steps < sectors
        ]
        return lax.ppermute(value, "sec", pairs)

    rows = psi.shape[1]
    part = rows // 2
    which = jnp.where(place == 0, 1, jnp.where(place == 2, 0, 2))
    orders = [jnp.where(even, 2, 1), jnp.where(even, 3, 2), jnp.where(even, 1, 3), 0]
    info = jnp.stack([*orders, row_sizes[0], col_sizes[0], which]).astype(jnp.int32)

    pairs_up = [(s, s + 1) for s in range(1, sectors, 4) if s + 1 < sectors]
    pairs_up += [(s, s - 3) for s in range(3, sectors, 4) if s + 1 < sectors]

    def raise_one(value):
        return lax.ppermute(value, "sec", pairs_up)

    def up_chip(value):
        return send(value, (0, 1), (2, 1))

    def along(value):
        return send(value, (3, 3), (0, -3))

    def across(value):
        return send(value, (1, 2), (2, -1))

    def swap(value):
        return send(value, (0, 1), (1, -1), (2, 1), (3, -1))

    def relay(value):
        return send(value, (0, 4))

    first0, token, live, *ops = first_rows(info, psi[0], left_env, right_env, part)
    ops0, ops1 = ops[:2], ops[2:]
    paired0 = up_chip(first0)
    first1, token, *ops2 = term_rows(
        info, live, ops0, part, part, token, bring=(2, left_env, right_env)
    )
    paired1 = up_chip(first1)
    both0, token = add(first0, paired0, token)
    raised0 = raise_one(both0)
    second0, token, *ops3 = term_rows(
        info, live, ops1, 0, part, token, bring=(3, left_env, right_env)
    )
    moved0 = along(second0)
    both1, token = add(first1, paired1, token)
    raised1 = raise_one(both1)
    second1, token = term_rows(info, live, ops1, part, part, token)
    moved1 = along(second1)
    third0, token = term_rows(info, live, ops2, 0, part, token)
    swapped0 = swap(third0)
    token = touch(raised0, token)
    relayed0 = relay(raised0)
    third1, token = term_rows(info, live, ops2, part, part, token)
    swapped1 = swap(third1)
    summed0, token = add(second0, moved0, token)
    crossed0 = across(summed0)
    own0, token = term_rows(info, live, ops3, 0, part, token, added=swapped0)
    token = touch(raised1, token)
    relayed1 = relay(raised1)
    summed1, token = add(second1, moved1, token)
    crossed1 = across(summed1)
    token = touch(relayed0, token)
    own1, token = term_rows(info, live, ops3, part, part, token, added=swapped1)

    energy = jnp.zeros((sectors, 128), jnp.float32)
    sigma, energy = finish(info, live, own0, (raised0, relayed0, crossed0), energy, None, 0)
    sigma, energy = finish(info, live, own1, (raised1, relayed1, crossed1), energy, sigma, part)
    return sigma, sum_over_sectors(energy)


def solution(mesh):
    return jax.shard_map(
        on_device,
        mesh=mesh,
        in_specs=(
            P(("grp", "sec"), None, None),
            P(("grp", "sec"), None, None, None),
            P(("grp", "sec"), None, None, None),
            P(("grp", "sec")),
            P(("grp", "sec")),
        ),
        out_specs=(P(("grp", "sec"), None, None), P("grp")),
        check_vma=False,
    )
```

```python
import functools

import jax
import jax.numpy as jnp
from jax import lax
from jax.experimental import pallas as pl
from jax.experimental.pallas import tpu as pltpu
from jax.sharding import PartitionSpec as P

MIB = 1024 * 1024
FIRST_MIB = 44
BRING_MIB = 42

ANY = pl.BlockSpec(memory_space=pl.ANY)
HBM = pl.BlockSpec(memory_space=pltpu.HBM)
SMEM = pl.BlockSpec(memory_space=pltpu.SMEM)
WHOLE = pl.BlockSpec(memory_space=pltpu.VMEM)
TOKEN = jax.ShapeDtypeStruct((8, 128), jnp.float32)
SMALL = pl.CostEstimate(flops=200000000, bytes_accessed=1000000, transcendentals=0)


def params(mib=8):
    return pltpu.CompilerParams(vmem_limit_bytes=mib * MIB)


def fetch(info_ref, slot, left_hbm, right_hbm, left_ref, right_ref, sems):
    term = info_ref[slot]
    half = left_ref.shape[0] // 2
    copies = []
    for i in range(2):
        span = pl.ds(i * half, half)
        copies.append(
            pltpu.make_async_copy(left_hbm.at[0, term, span, :], left_ref.at[span, :], sems.at[i])
        )
    copies.insert(1, pltpu.make_async_copy(right_hbm.at[0, term], right_ref, sems.at[2]))
    return copies


def multiply(left, live, right):
    first = jnp.dot(left, live, preferred_element_type=jnp.float32).astype(jnp.bfloat16)
    return jnp.dot(first, right, preferred_element_type=jnp.float32)


def first_kernel(info_ref, psi_hbm, left_hbm, right_hbm, *refs):
    out_ref, _, live_ref, left0, right0, left1, right1, psi_buf, sems, psi_sems = refs
    pieces = psi_sems.shape[0]
    rows, cols = psi_buf.shape
    step = rows // pieces

    def copy(i):
        span = pl.ds(i * step, step)
        return pltpu.make_async_copy(psi_hbm.at[span, :], psi_buf.at[span, :], psi_sems.at[i])

    for i in range(pieces):
        copy(i).start()
    needed = fetch(info_ref, 0, left_hbm, right_hbm, left0, right0, sems.at[0])
    ahead = fetch(info_ref, 1, left_hbm, right_hbm, left1, right1, sems.at[1])
    needed[0].start()
    needed[1].start()
    col = lax.broadcasted_iota(jnp.int32, (step, cols), 1) < info_ref[5]
    row = lax.broadcasted_iota(jnp.int32, (step, cols), 0)
    for i in range(pieces):
        copy(i).wait()
        inside = jnp.logical_and(row < info_ref[4] - i * step, col)
        values = psi_buf[i * step : (i + 1) * step, :].astype(jnp.float32)
        live_ref[i * step : (i + 1) * step, :] = jnp.where(inside, values, 0.0).astype(
            live_ref.dtype
        )
    for later in (needed[2], *ahead):
        later.start()
    needed[0].wait()
    needed[1].wait()
    out_ref[...] = multiply(left0[: out_ref.shape[0], :], live_ref[...], right0[...])
    for later in (needed[2], *ahead):
        later.wait()


def operand_shapes(width, cols):
    return [
        jax.ShapeDtypeStruct((width, width), jnp.bfloat16),
        jax.ShapeDtypeStruct((cols, cols), jnp.bfloat16),
    ]


def first_rows(info, psi, left_env, right_env, count):
    width, cols = psi.shape
    out_shape = [jax.ShapeDtypeStruct((count, cols), jnp.float32), TOKEN]
    out_shape += [jax.ShapeDtypeStruct(psi.shape, psi.dtype), *operand_shapes(width, cols) * 2]
    return pl.pallas_call(
        first_kernel,
        out_shape=out_shape,
        in_specs=[SMEM, HBM, HBM, HBM],
        out_specs=[WHOLE, ANY] + [WHOLE] * 5,
        scratch_shapes=[
            pltpu.VMEM(psi.shape, psi.dtype),
            pltpu.SemaphoreType.DMA((2, 3)),
            pltpu.SemaphoreType.DMA((4,)),
        ],
        compiler_params=params(FIRST_MIB),
        cost_estimate=SMALL,
        name="first_rows",
    )(info, psi, left_env, right_env)


def term_kernel(first, adds, slot, tokens, info_ref, live_ref, left_ref, right_ref, *refs):
    refs = list(refs)
    add_ref = refs.pop(0) if adds else None
    copies = []
    if slot is not None:
        left_hbm, right_hbm = refs[:2]
        sems = refs[-1]
        out_ref, _, left_next, right_next = refs[2 + tokens : -1]
        copies = fetch(info_ref, slot, left_hbm, right_hbm, left_next, right_next, sems)
        for copy in copies:
            copy.start()
    else:
        out_ref, _ = refs[tokens:]
    count = out_ref.shape[0]
    block = min(count, 512)
    for i in range(count // block):
        span = pl.ds(i * block, block)
        value = multiply(left_ref[pl.ds(first + i * block, block), :], live_ref[...], right_ref[...])
        if adds:
            value = value + add_ref[span, :]
        out_ref[span, :] = value
    for copy in copies:
        copy.wait()


def term_rows(info, live, operands, first, count, *tokens, added=None, bring=None):
    width, cols = live.shape
    in_specs = [SMEM, WHOLE, WHOLE, WHOLE]
    args = [info, live, *operands]
    out_shape = [jax.ShapeDtypeStruct((count, cols), jnp.float32), TOKEN]
    out_specs = [WHOLE, ANY]
    scratch = []
    slot = None
    if added is not None:
        in_specs.append(WHOLE)
        args.append(added)
    if bring is not None:
        slot = bring[0]
        in_specs += [HBM, HBM]
        args += bring[1:]
        out_shape += operand_shapes(width, cols)
        out_specs += [WHOLE, WHOLE]
        scratch.append(pltpu.SemaphoreType.DMA((3,)))
    return pl.pallas_call(
        functools.partial(term_kernel, first, added is not None, slot, len(tokens)),
        out_shape=out_shape,
        in_specs=in_specs + [ANY] * len(tokens),
        out_specs=out_specs,
        scratch_shapes=scratch,
        compiler_params=params(12 if slot is None else BRING_MIB),
        cost_estimate=SMALL,
        name="term_rows",
    )(*args, *tokens)


def add_kernel(a_ref, b_ref, *refs):
    out_ref = refs[-2]
    rows = a_ref.shape[0]
    step = 64

    def body(i, _):
        span = pl.ds(pl.multiple_of(i * step, step), step)
        out_ref[span, :] = a_ref[span, :] + b_ref[span, :]
        return _

    lax.fori_loop(0, rows // step, body, 0)


def add(a, b, *tokens):
    return pl.pallas_call(
        add_kernel,
        out_shape=(jax.ShapeDtypeStruct(a.shape, a.dtype), TOKEN),
        in_specs=[WHOLE, WHOLE] + [ANY] * len(tokens),
        out_specs=(WHOLE, ANY),
        compiler_params=params(),
        cost_estimate=SMALL,
        name="add_blocks",
    )(a, b, *tokens)


def touch(*values):
    return pl.pallas_call(
        lambda *refs: None,
        out_shape=TOKEN,
        in_specs=[ANY] * len(values),
        out_specs=ANY,
        compiler_params=params(),
        cost_estimate=SMALL,
        name="touch",
    )(*values)


def hold(value, token):
    return pl.pallas_call(
        lambda *refs: None,
        out_shape=(jax.ShapeDtypeStruct(value.shape, value.dtype), TOKEN),
        in_specs=[ANY, ANY],
        out_specs=(ANY, ANY),
        input_output_aliases={0: 0},
        compiler_params=params(),
        cost_estimate=SMALL,
        name="hold",
    )(value, token)


def finish_kernel(first, info_ref, live_ref, own_ref, a_ref, b_ref, c_ref, before_ref, *refs):
    sigma_hbm, energy_ref, sigma_buf, sems = refs[-4:]
    count, cols = own_ref.shape
    step = 64
    piece = count // sems.shape[0]
    col = lax.broadcasted_iota(jnp.int32, (step, cols), 1) < info_ref[5]
    row = lax.broadcasted_iota(jnp.int32, (step, cols), 0)

    def copy(i):
        span = pl.ds(i * piece, piece)
        return pltpu.make_async_copy(
            sigma_buf.at[span, :], sigma_hbm.at[0, pl.ds(first + i * piece, piece), :], sems.at[i]
        )

    def work(arrival):
        energy = jnp.zeros((8, cols), jnp.float32)
        for i in range(count // piece):

            def body(n, energy):
                start = pl.multiple_of(i * piece + n * step, step)
                span = pl.ds(start, step)
                inside = jnp.logical_and(row < info_ref[4] - first - start, col)
                total = jnp.where(inside, own_ref[span, :] + arrival[span, :], 0.0)
                sigma_buf[span, :] = total.astype(sigma_buf.dtype)
                here = pl.ds(pl.multiple_of(first + start, step), step)
                product = live_ref[here, :].astype(jnp.float32) * total
                return energy + jnp.sum(jnp.reshape(product, (step // 8, 8, cols)), axis=0)

            energy = lax.fori_loop(0, piece // step, body, energy)
            copy(i).start()
        energy_ref[...] = before_ref[...] + jnp.sum(energy)

    for n, arrival in enumerate((a_ref, b_ref, c_ref)):
        pl.when(info_ref[6] == n)(functools.partial(work, arrival))
    for i in range(count // piece):
        copy(i).wait()


def finish(info, live, own, arrivals, before, sigma, first):
    count, cols = own.shape
    in_specs = [SMEM] + [WHOLE] * 6
    operands = [info, live, own, *arrivals, before]
    aliases = {}
    if sigma is not None:
        in_specs.append(ANY)
        aliases = {len(operands): 0}
        operands.append(sigma)
    return pl.pallas_call(
        functools.partial(finish_kernel, first),
        out_shape=(
            jax.ShapeDtypeStruct((1, *live.shape), jnp.bfloat16),
            jax.ShapeDtypeStruct(before.shape, jnp.float32),
        ),
        in_specs=in_specs,
        out_specs=(ANY, WHOLE),
        scratch_shapes=[pltpu.VMEM((count, cols), jnp.bfloat16), pltpu.SemaphoreType.DMA((4,))],
        input_output_aliases=aliases,
        compiler_params=params(),
        cost_estimate=SMALL,
        name="finish_rows",
    )(*operands)


def sum_kernel(in_ref, out_ref):
    out_ref[0] = jnp.sum(in_ref[:, :1])


def sum_over_sectors(value):
    arrived = lax.all_to_all(value, "sec", 0, 0, tiled=True)
    return pl.pallas_call(
        sum_kernel,
        out_shape=jax.ShapeDtypeStruct((1,), jnp.float32),
        in_specs=[WHOLE],
        out_specs=SMEM,
        compiler_params=params(),
        cost_estimate=SMALL,
        name="sum_energy",
    )(arrived)


def on_device(psi, left_env, right_env, row_sizes, col_sizes):
    sectors = lax.axis_size("sec")
    sector = lax.axis_index("sec")
    even = sector % 2 == 0
    place = sector % 4

    def send(value, *hops):
        pairs = [
            (s, s + steps)
            for at, steps in hops
            for s in range(at, sectors, 4)
            if 0 <= s + steps < sectors
        ]
        return lax.ppermute(value, "sec", pairs)

    rows = psi.shape[1]
    part = rows // 2
    which = jnp.where(place == 0, 1, jnp.where(place == 2, 0, 2))
    orders = [jnp.where(even, 2, 1), jnp.where(even, 3, 2), jnp.where(even, 1, 3), 0]
    info = jnp.stack([*orders, row_sizes[0], col_sizes[0], which]).astype(jnp.int32)

    pairs_up = [(s, s + 1) for s in range(1, sectors, 4) if s + 1 < sectors]
    pairs_up += [(s, s - 3) for s in range(3, sectors, 4) if s + 1 < sectors]

    def raise_one(value):
        return lax.ppermute(value, "sec", pairs_up)

    def up_chip(value):
        return send(value, (0, 1), (2, 1))

    def along(value):
        return send(value, (3, 3), (0, -3))

    def across(value):
        return send(value, (1, 2), (2, -1))

    def swap(value):
        return send(value, (0, 1), (1, -1), (2, 1), (3, -1))

    def relay(value):
        return send(value, (0, 4))

    first0, token, live, *ops = first_rows(info, psi[0], left_env, right_env, part)
    ops0, ops1 = ops[:2], ops[2:]
    paired0 = up_chip(first0)
    first1, token, *ops2 = term_rows(
        info, live, ops0, part, part, token, bring=(2, left_env, right_env)
    )
    paired1 = up_chip(first1)
    both0, token = add(first0, paired0, token)
    raised0 = raise_one(both0)
    second0, token, *ops3 = term_rows(
        info, live, ops1, 0, part, token, bring=(3, left_env, right_env)
    )
    moved0 = along(second0)
    both1, token = add(first1, paired1, token)
    raised1 = raise_one(both1)
    second1, token = term_rows(info, live, ops1, part, part, token)
    moved1 = along(second1)
    third0, token = term_rows(info, live, ops2, 0, part, token)
    swapped0 = swap(third0)
    raised0, token = hold(raised0, token)
    relayed0 = relay(raised0)
    third1, token = term_rows(info, live, ops2, part, part, token)
    swapped1 = swap(third1)
    summed0, token = add(second0, moved0, token)
    crossed0 = across(summed0)
    own0, token = term_rows(info, live, ops3, 0, part, token, added=swapped0)
    raised1, token = hold(raised1, token)
    relayed1 = relay(raised1)
    token = touch(relayed0, token)
    summed1, token = add(second1, moved1, token)
    crossed1 = across(summed1)

    energy = jnp.zeros((sectors, 128), jnp.float32)
    sigma, energy = finish(info, live, own0, (raised0, relayed0, crossed0), energy, None, 0)
    own1, token = term_rows(info, live, ops3, part, part, token, energy, added=swapped1)
    sigma, energy = finish(info, live, own1, (raised1, relayed1, crossed1), energy, sigma, part)
    return sigma, sum_over_sectors(energy)


def solution(mesh):
    return jax.shard_map(
        on_device,
        mesh=mesh,
        in_specs=(
            P(("grp", "sec"), None, None),
            P(("grp", "sec"), None, None, None),
            P(("grp", "sec"), None, None, None),
            P(("grp", "sec")),
            P(("grp", "sec")),
        ),
        out_specs=(P(("grp", "sec"), None, None), P("grp")),
        check_vma=False,
    )
```

```python
import functools

import jax
import jax.numpy as jnp
from jax import lax
from jax.experimental import pallas as pl
from jax.experimental.pallas import tpu as pltpu
from jax.sharding import PartitionSpec as P

MIB = 1024 * 1024
FIRST_MIB = 44
BRING_MIB = 42

ANY = pl.BlockSpec(memory_space=pl.ANY)
HBM = pl.BlockSpec(memory_space=pltpu.HBM)
SMEM = pl.BlockSpec(memory_space=pltpu.SMEM)
WHOLE = pl.BlockSpec(memory_space=pltpu.VMEM)
TOKEN = jax.ShapeDtypeStruct((8, 128), jnp.float32)
SMALL = pl.CostEstimate(flops=200000000, bytes_accessed=1000000, transcendentals=0)


def params(mib=8):
    return pltpu.CompilerParams(vmem_limit_bytes=mib * MIB)


def fetch(info_ref, slot, left_hbm, right_hbm, left_ref, right_ref, sems):
    term = info_ref[slot]
    half = left_ref.shape[0] // 2
    copies = []
    for i in range(2):
        span = pl.ds(i * half, half)
        copies.append(
            pltpu.make_async_copy(left_hbm.at[0, term, span, :], left_ref.at[span, :], sems.at[i])
        )
    copies.insert(1, pltpu.make_async_copy(right_hbm.at[0, term], right_ref, sems.at[2]))
    return copies


def multiply(left, live, right):
    first = jnp.dot(left, live, preferred_element_type=jnp.float32).astype(jnp.bfloat16)
    return jnp.dot(first, right, preferred_element_type=jnp.float32)


def first_kernel(info_ref, psi_hbm, left_hbm, right_hbm, *refs):
    out_ref, _, live_ref, left0, right0, left1, right1, psi_buf, sems, psi_sems = refs
    pieces = psi_sems.shape[0]
    rows, cols = psi_buf.shape
    step = rows // pieces

    def copy(i):
        span = pl.ds(i * step, step)
        return pltpu.make_async_copy(psi_hbm.at[span, :], psi_buf.at[span, :], psi_sems.at[i])

    for i in range(pieces):
        copy(i).start()
    needed = fetch(info_ref, 0, left_hbm, right_hbm, left0, right0, sems.at[0])
    ahead = fetch(info_ref, 1, left_hbm, right_hbm, left1, right1, sems.at[1])
    needed[0].start()
    needed[1].start()
    col = lax.broadcasted_iota(jnp.int32, (step, cols), 1) < info_ref[5]
    row = lax.broadcasted_iota(jnp.int32, (step, cols), 0)
    for i in range(pieces):
        copy(i).wait()
        inside = jnp.logical_and(row < info_ref[4] - i * step, col)
        values = psi_buf[i * step : (i + 1) * step, :].astype(jnp.float32)
        live_ref[i * step : (i + 1) * step, :] = jnp.where(inside, values, 0.0).astype(
            live_ref.dtype
        )
    for later in (needed[2], *ahead):
        later.start()
    needed[0].wait()
    needed[1].wait()
    out_ref[...] = multiply(left0[: out_ref.shape[0], :], live_ref[...], right0[...])
    for later in (needed[2], *ahead):
        later.wait()


def operand_shapes(width, cols):
    return [
        jax.ShapeDtypeStruct((width, width), jnp.bfloat16),
        jax.ShapeDtypeStruct((cols, cols), jnp.bfloat16),
    ]


def first_rows(info, psi, left_env, right_env, count):
    width, cols = psi.shape
    out_shape = [jax.ShapeDtypeStruct((count, cols), jnp.float32), TOKEN]
    out_shape += [jax.ShapeDtypeStruct(psi.shape, psi.dtype), *operand_shapes(width, cols) * 2]
    return pl.pallas_call(
        first_kernel,
        out_shape=out_shape,
        in_specs=[SMEM, HBM, HBM, HBM],
        out_specs=[WHOLE, ANY] + [WHOLE] * 5,
        scratch_shapes=[
            pltpu.VMEM(psi.shape, psi.dtype),
            pltpu.SemaphoreType.DMA((2, 3)),
            pltpu.SemaphoreType.DMA((4,)),
        ],
        compiler_params=params(FIRST_MIB),
        cost_estimate=SMALL,
        name="first_rows",
    )(info, psi, left_env, right_env)


def term_kernel(first, adds, slot, tokens, info_ref, live_ref, left_ref, right_ref, *refs):
    refs = list(refs)
    add_ref = refs.pop(0) if adds else None
    copies = []
    if slot is not None:
        left_hbm, right_hbm = refs[:2]
        sems = refs[-1]
        out_ref, _, left_next, right_next = refs[2 + tokens : -1]
        copies = fetch(info_ref, slot, left_hbm, right_hbm, left_next, right_next, sems)
        for copy in copies:
            copy.start()
    else:
        out_ref, _ = refs[tokens:]
    count = out_ref.shape[0]
    block = min(count, 512)
    for i in range(count // block):
        span = pl.ds(i * block, block)
        value = multiply(left_ref[pl.ds(first + i * block, block), :], live_ref[...], right_ref[...])
        if adds:
            value = value + add_ref[span, :]
        out_ref[span, :] = value
    for copy in copies:
        copy.wait()


def term_rows(info, live, operands, first, count, *tokens, added=None, bring=None):
    width, cols = live.shape
    in_specs = [SMEM, WHOLE, WHOLE, WHOLE]
    args = [info, live, *operands]
    out_shape = [jax.ShapeDtypeStruct((count, cols), jnp.float32), TOKEN]
    out_specs = [WHOLE, ANY]
    scratch = []
    slot = None
    if added is not None:
        in_specs.append(WHOLE)
        args.append(added)
    if bring is not None:
        slot = bring[0]
        in_specs += [HBM, HBM]
        args += bring[1:]
        out_shape += operand_shapes(width, cols)
        out_specs += [WHOLE, WHOLE]
        scratch.append(pltpu.SemaphoreType.DMA((3,)))
    return pl.pallas_call(
        functools.partial(term_kernel, first, added is not None, slot, len(tokens)),
        out_shape=out_shape,
        in_specs=in_specs + [ANY] * len(tokens),
        out_specs=out_specs,
        scratch_shapes=scratch,
        compiler_params=params(12 if slot is None else BRING_MIB),
        cost_estimate=SMALL,
        name="term_rows",
    )(*args, *tokens)


def add_kernel(a_ref, b_ref, *refs):
    out_ref = refs[-2]
    rows = a_ref.shape[0]
    step = 64

    def body(i, _):
        span = pl.ds(pl.multiple_of(i * step, step), step)
        out_ref[span, :] = a_ref[span, :] + b_ref[span, :]
        return _

    lax.fori_loop(0, rows // step, body, 0)


def add(a, b, *tokens):
    return pl.pallas_call(
        add_kernel,
        out_shape=(jax.ShapeDtypeStruct(a.shape, a.dtype), TOKEN),
        in_specs=[WHOLE, WHOLE] + [ANY] * len(tokens),
        out_specs=(WHOLE, ANY),
        compiler_params=params(),
        cost_estimate=SMALL,
        name="add_blocks",
    )(a, b, *tokens)


def touch(*values):
    return pl.pallas_call(
        lambda *refs: None,
        out_shape=TOKEN,
        in_specs=[ANY] * len(values),
        out_specs=ANY,
        compiler_params=params(),
        cost_estimate=SMALL,
        name="touch",
    )(*values)


def hold(value, token):
    return pl.pallas_call(
        lambda *refs: None,
        out_shape=(jax.ShapeDtypeStruct(value.shape, value.dtype), TOKEN),
        in_specs=[ANY, ANY],
        out_specs=(ANY, ANY),
        input_output_aliases={0: 0},
        compiler_params=params(),
        cost_estimate=SMALL,
        name="hold",
    )(value, token)


def folded(values):
    rows, cols = values.shape
    return jnp.sum(jnp.reshape(values, (rows // 8, 8, cols)), axis=0)


def finish_kernel(first, info_ref, live_ref, own_ref, a_ref, b_ref, c_ref, *refs):
    refs = list(refs)
    sigma_buf, sems = refs[-2:]
    energy_ref = refs.pop(-3) if first == 0 else None
    sigma_hbm = refs[-3]
    count, cols = own_ref.shape
    step = 64
    piece = count // sems.shape[0]
    col = lax.broadcasted_iota(jnp.int32, (step, cols), 1) < info_ref[5]
    row = lax.broadcasted_iota(jnp.int32, (step, cols), 0)

    def copy(i):
        span = pl.ds(i * piece, piece)
        return pltpu.make_async_copy(
            sigma_buf.at[span, :], sigma_hbm.at[0, pl.ds(first + i * piece, piece), :], sems.at[i]
        )

    def work(arrival):
        energy = jnp.zeros((8, cols), jnp.float32)
        for i in range(count // piece):
            for start in range(i * piece, (i + 1) * piece, step):
                span = pl.ds(start, step)
                inside = jnp.logical_and(row < info_ref[4] - (first + start), col)
                total = jnp.where(inside, own_ref[span, :] + arrival[span, :], 0.0)
                sigma_buf[span, :] = total.astype(sigma_buf.dtype)
                if energy_ref is not None:
                    energy += folded(live_ref[span, :].astype(jnp.float32) * total)
            copy(i).start()
        if energy_ref is not None:
            energy_ref[...] = energy

    for n, arrival in enumerate((a_ref, b_ref, c_ref)):
        pl.when(info_ref[6] == n)(functools.partial(work, arrival))
    for i in range(count // piece):
        copy(i).wait()


def finish(info, live, own, arrivals, sigma, first):
    count, cols = own.shape
    in_specs = [SMEM] + [WHOLE] * 5
    operands = [info, live, own, *arrivals]
    out_shape = [jax.ShapeDtypeStruct((1, *live.shape), jnp.bfloat16)]
    out_specs = [ANY]
    aliases = {}
    if sigma is not None:
        in_specs.append(ANY)
        aliases = {len(operands): 0}
        operands.append(sigma)
    if first == 0:
        out_shape.append(jax.ShapeDtypeStruct((8, cols), jnp.float32))
        out_specs.append(WHOLE)
    return pl.pallas_call(
        functools.partial(finish_kernel, first),
        out_shape=out_shape,
        in_specs=in_specs,
        out_specs=out_specs,
        scratch_shapes=[pltpu.VMEM((count, cols), jnp.bfloat16), pltpu.SemaphoreType.DMA((4,))],
        input_output_aliases=aliases,
        compiler_params=params(),
        cost_estimate=SMALL,
        name="finish_rows",
    )(*operands)


def energy_kernel(first, info_ref, live_ref, own_ref, a_ref, b_ref, c_ref, before_ref, out_ref):
    count, cols = own_ref.shape
    step = 64

    def work(arrival):
        energy = before_ref[...]
        for start in range(0, count, step):
            span = pl.ds(start, step)
            total = own_ref[span, :] + arrival[span, :]
            live = live_ref[pl.ds(first + start, step), :].astype(jnp.float32)
            energy += folded(live * total)
        out_ref[...] = jnp.full(out_ref.shape, jnp.sum(energy), jnp.float32)

    for n, arrival in enumerate((a_ref, b_ref, c_ref)):
        pl.when(info_ref[6] == n)(functools.partial(work, arrival))


def energy_of(info, live, own, arrivals, before, first):
    return pl.pallas_call(
        functools.partial(energy_kernel, first),
        out_shape=jax.ShapeDtypeStruct((1, 128), jnp.float32),
        in_specs=[SMEM] + [WHOLE] * 6,
        out_specs=WHOLE,
        compiler_params=params(),
        cost_estimate=SMALL,
        name="energy_rows",
    )(info, live, own, *arrivals, before)


def sum_kernel(in_ref, out_ref):
    out_ref[0] = jnp.sum(in_ref[:, :1])


def sum_over_sectors(value):
    arrived = lax.all_gather(value, "sec", axis=0, tiled=True)
    return pl.pallas_call(
        sum_kernel,
        out_shape=jax.ShapeDtypeStruct((1,), jnp.float32),
        in_specs=[WHOLE],
        out_specs=SMEM,
        compiler_params=params(),
        cost_estimate=SMALL,
        name="sum_energy",
    )(arrived)


def on_device(psi, left_env, right_env, row_sizes, col_sizes):
    sectors = lax.axis_size("sec")
    sector = lax.axis_index("sec")
    even = sector % 2 == 0
    place = sector % 4

    def send(value, *hops):
        pairs = [
            (s, s + steps)
            for at, steps in hops
            for s in range(at, sectors, 4)
            if 0 <= s + steps < sectors
        ]
        return lax.ppermute(value, "sec", pairs)

    rows = psi.shape[1]
    part = rows // 2
    which = jnp.where(place == 0, 1, jnp.where(place == 2, 0, 2))
    orders = [jnp.where(even, 2, 1), jnp.where(even, 3, 2), jnp.where(even, 1, 3), 0]
    info = jnp.stack([*orders, row_sizes[0], col_sizes[0], which]).astype(jnp.int32)

    pairs_up = [(s, s + 1) for s in range(1, sectors, 4) if s + 1 < sectors]
    pairs_up += [(s, s - 3) for s in range(3, sectors, 4) if s + 1 < sectors]

    def raise_one(value):
        return lax.ppermute(value, "sec", pairs_up)

    def up_chip(value):
        return send(value, (0, 1), (2, 1))

    def along(value):
        return send(value, (3, 3), (0, -3))

    def across(value):
        return send(value, (1, 2), (2, -1))

    def swap(value):
        return send(value, (0, 1), (1, -1), (2, 1), (3, -1))

    def relay(value):
        return send(value, (0, 4))

    first0, token, live, *ops = first_rows(info, psi[0], left_env, right_env, part)
    ops0, ops1 = ops[:2], ops[2:]
    paired0 = up_chip(first0)
    first1, token, *ops2 = term_rows(
        info, live, ops0, part, part, token, bring=(2, left_env, right_env)
    )
    paired1 = up_chip(first1)
    both0, token = add(first0, paired0, token)
    raised0 = raise_one(both0)
    second0, token, *ops3 = term_rows(
        info, live, ops1, 0, part, token, bring=(3, left_env, right_env)
    )
    moved0 = along(second0)
    both1, token = add(first1, paired1, token)
    raised1 = raise_one(both1)
    second1, token = term_rows(info, live, ops1, part, part, token)
    moved1 = along(second1)
    third0, token = term_rows(info, live, ops2, 0, part, token)
    swapped0 = swap(third0)
    raised0, token = hold(raised0, token)
    relayed0 = relay(raised0)
    third1, token = term_rows(info, live, ops2, part, part, token)
    swapped1 = swap(third1)
    summed0, token = add(second0, moved0, token)
    crossed0 = across(summed0)
    own0, token = term_rows(info, live, ops3, 0, part, token, added=swapped0)
    raised1, token = hold(raised1, token)
    relayed1 = relay(raised1)
    token = touch(relayed0, token)
    summed1, token = add(second1, moved1, token)
    crossed1 = across(summed1)

    sigma, energy = finish(info, live, own0, (raised0, relayed0, crossed0), None, 0)
    own1, token = term_rows(info, live, ops3, part, part, token, energy, added=swapped1)
    arrivals = (raised1, relayed1, crossed1)
    energy = sum_over_sectors(energy_of(info, live, own1, arrivals, energy, part))
    (sigma,) = finish(info, live, own1, arrivals, sigma, part)
    return sigma, energy


def solution(mesh):
    return jax.shard_map(
        on_device,
        mesh=mesh,
        in_specs=(
            P(("grp", "sec"), None, None),
            P(("grp", "sec"), None, None, None),
            P(("grp", "sec"), None, None, None),
            P(("grp", "sec")),
            P(("grp", "sec")),
        ),
        out_specs=(P(("grp", "sec"), None, None), P("grp")),
        check_vma=False,
    )
```

```python
import functools

import jax
import jax.numpy as jnp
from jax import lax
from jax.experimental import pallas as pl
from jax.experimental.pallas import tpu as pltpu
from jax.sharding import PartitionSpec as P

MIB = 1024 * 1024
FIRST_MIB = 48
BRING_MIB = 42

ANY = pl.BlockSpec(memory_space=pl.ANY)
HBM = pl.BlockSpec(memory_space=pltpu.HBM)
SMEM = pl.BlockSpec(memory_space=pltpu.SMEM)
WHOLE = pl.BlockSpec(memory_space=pltpu.VMEM)
TOKEN = jax.ShapeDtypeStruct((8, 128), jnp.float32)
SMALL = pl.CostEstimate(flops=200000000, bytes_accessed=1000000, transcendentals=0)


def params(mib=8):
    return pltpu.CompilerParams(vmem_limit_bytes=mib * MIB)


def fetch(info_ref, slot, left_hbm, right_hbm, left_ref, right_ref, sems):
    term = info_ref[slot]
    half = left_ref.shape[0] // 2
    copies = []
    for i in range(2):
        span = pl.ds(i * half, half)
        copies.append(
            pltpu.make_async_copy(left_hbm.at[0, term, span, :], left_ref.at[span, :], sems.at[i])
        )
    copies.insert(1, pltpu.make_async_copy(right_hbm.at[0, term], right_ref, sems.at[2]))
    return copies


def multiply(left, live, right):
    first = jnp.dot(left, live, preferred_element_type=jnp.float32).astype(jnp.bfloat16)
    return jnp.dot(first, right, preferred_element_type=jnp.float32)


def opening_kernel(slot, following, masks, tokens, info_ref, live_ref, left_hbm, right_hbm, *refs):
    refs = list(refs[tokens:])
    out_ref, _ = refs[:2]
    sems = refs[-1]
    operands = refs[2:-1]
    psi_ref = live_ref
    if masks:
        live_ref = operands.pop(0)
    own = fetch(info_ref, slot, left_hbm, right_hbm, *operands[:2], sems.at[0])
    late = [own.pop()]
    if following is not None:
        late += fetch(info_ref, following, left_hbm, right_hbm, *operands[2:], sems.at[1])
    for copy in own:
        copy.start()
    if masks:
        rows, cols = psi_ref.shape
        step = 128
        col = lax.broadcasted_iota(jnp.int32, (step, cols), 1) < info_ref[5]
        row = lax.broadcasted_iota(jnp.int32, (step, cols), 0)
        for start in range(0, rows, step):
            span = pl.ds(start, step)
            inside = jnp.logical_and(row < info_ref[4] - start, col)
            values = jnp.where(inside, psi_ref[span, :].astype(jnp.float32), 0.0)
            live_ref[span, :] = values.astype(live_ref.dtype)
    for copy in own:
        copy.wait()
    for copy in late:
        copy.start()
    out_ref[...] = multiply(operands[0][: out_ref.shape[0], :], live_ref[...], operands[1][...])
    for copy in late:
        copy.wait()


def operand_shapes(width, cols):
    return [
        jax.ShapeDtypeStruct((width, width), jnp.bfloat16),
        jax.ShapeDtypeStruct((cols, cols), jnp.bfloat16),
    ]


def opening_rows(info, live, envs, slot, count, *tokens, following=None, masks=False):
    width, cols = live.shape
    out_shape = [jax.ShapeDtypeStruct((count, cols), jnp.float32), TOKEN]
    if masks:
        out_shape.append(jax.ShapeDtypeStruct(live.shape, live.dtype))
    out_shape += operand_shapes(width, cols) * (1 if following is None else 2)
    return pl.pallas_call(
        functools.partial(opening_kernel, slot, following, masks, len(tokens)),
        out_shape=out_shape,
        in_specs=[SMEM, WHOLE, HBM, HBM] + [ANY] * len(tokens),
        out_specs=[WHOLE, ANY] + [WHOLE] * (len(out_shape) - 2),
        scratch_shapes=[pltpu.SemaphoreType.DMA((2, 3))],
        compiler_params=params(FIRST_MIB if masks else BRING_MIB),
        cost_estimate=SMALL,
        name="opening_rows",
    )(info, live, *envs, *tokens)


def term_kernel(first, adds, slot, tokens, info_ref, live_ref, left_ref, right_ref, *refs):
    refs = list(refs)
    add_ref = refs.pop(0) if adds else None
    copies = []
    if slot is not None:
        left_hbm, right_hbm = refs[:2]
        sems = refs[-1]
        out_ref, _, left_next, right_next = refs[2 + tokens : -1]
        copies = fetch(info_ref, slot, left_hbm, right_hbm, left_next, right_next, sems)
        for copy in copies:
            copy.start()
    else:
        out_ref, _ = refs[tokens:]
    count = out_ref.shape[0]
    block = min(count, 512)
    for i in range(count // block):
        span = pl.ds(i * block, block)
        value = multiply(left_ref[pl.ds(first + i * block, block), :], live_ref[...], right_ref[...])
        if adds:
            value = value + add_ref[span, :]
        out_ref[span, :] = value
    for copy in copies:
        copy.wait()


def term_rows(info, live, operands, first, count, *tokens, added=None, bring=None):
    width, cols = live.shape
    in_specs = [SMEM, WHOLE, WHOLE, WHOLE]
    args = [info, live, *operands]
    out_shape = [jax.ShapeDtypeStruct((count, cols), jnp.float32), TOKEN]
    out_specs = [WHOLE, ANY]
    scratch = []
    slot = None
    if added is not None:
        in_specs.append(WHOLE)
        args.append(added)
    if bring is not None:
        slot = bring[0]
        in_specs += [HBM, HBM]
        args += bring[1:]
        out_shape += operand_shapes(width, cols)
        out_specs += [WHOLE, WHOLE]
        scratch.append(pltpu.SemaphoreType.DMA((3,)))
    return pl.pallas_call(
        functools.partial(term_kernel, first, added is not None, slot, len(tokens)),
        out_shape=out_shape,
        in_specs=in_specs + [ANY] * len(tokens),
        out_specs=out_specs,
        scratch_shapes=scratch,
        compiler_params=params(12 if slot is None else BRING_MIB),
        cost_estimate=SMALL,
        name="term_rows",
    )(*args, *tokens)


def add_kernel(a_ref, b_ref, *refs):
    out_ref = refs[-2]
    rows = a_ref.shape[0]
    step = 64

    def body(i, _):
        span = pl.ds(pl.multiple_of(i * step, step), step)
        out_ref[span, :] = a_ref[span, :] + b_ref[span, :]
        return _

    lax.fori_loop(0, rows // step, body, 0)


def add(a, b, *tokens):
    return pl.pallas_call(
        add_kernel,
        out_shape=(jax.ShapeDtypeStruct(a.shape, a.dtype), TOKEN),
        in_specs=[WHOLE, WHOLE] + [ANY] * len(tokens),
        out_specs=(WHOLE, ANY),
        compiler_params=params(),
        cost_estimate=SMALL,
        name="add_blocks",
    )(a, b, *tokens)


def touch(*values):
    return pl.pallas_call(
        lambda *refs: None,
        out_shape=TOKEN,
        in_specs=[ANY] * len(values),
        out_specs=ANY,
        compiler_params=params(),
        cost_estimate=SMALL,
        name="touch",
    )(*values)


def hold(value, token):
    return pl.pallas_call(
        lambda *refs: None,
        out_shape=(jax.ShapeDtypeStruct(value.shape, value.dtype), TOKEN),
        in_specs=[ANY, ANY],
        out_specs=(ANY, ANY),
        input_output_aliases={0: 0},
        compiler_params=params(),
        cost_estimate=SMALL,
        name="hold",
    )(value, token)


def finish_kernel(first, info_ref, live_ref, own_ref, a_ref, b_ref, c_ref, before_ref, *refs):
    sigma_hbm, energy_ref, sigma_buf, sems = refs[-4:]
    count, cols = own_ref.shape
    step = 64
    piece = count // sems.shape[0]
    col = lax.broadcasted_iota(jnp.int32, (step, cols), 1) < info_ref[5]
    row = lax.broadcasted_iota(jnp.int32, (step, cols), 0)

    def copy(i):
        span = pl.ds(i * piece, piece)
        return pltpu.make_async_copy(
            sigma_buf.at[span, :], sigma_hbm.at[0, pl.ds(first + i * piece, piece), :], sems.at[i]
        )

    def work(arrival):
        energy = jnp.zeros((8, cols), jnp.float32)
        for i in range(count // piece):

            def body(n, energy):
                start = pl.multiple_of(i * piece + n * step, step)
                span = pl.ds(start, step)
                inside = jnp.logical_and(row < info_ref[4] - first - start, col)
                total = jnp.where(inside, own_ref[span, :] + arrival[span, :], 0.0)
                sigma_buf[span, :] = total.astype(sigma_buf.dtype)
                here = pl.ds(pl.multiple_of(first + start, step), step)
                product = live_ref[here, :].astype(jnp.float32) * total
                return energy + jnp.sum(jnp.reshape(product, (step // 8, 8, cols)), axis=0)

            energy = lax.fori_loop(0, piece // step, body, energy)
            copy(i).start()
        energy_ref[...] = before_ref[...] + jnp.sum(energy)

    for n, arrival in enumerate((a_ref, b_ref, c_ref)):
        pl.when(info_ref[6] == n)(functools.partial(work, arrival))
    for i in range(count // piece):
        copy(i).wait()


def finish(info, live, own, arrivals, before, sigma, first):
    count, cols = own.shape
    in_specs = [SMEM] + [WHOLE] * 6
    operands = [info, live, own, *arrivals, before]
    aliases = {}
    if sigma is not None:
        in_specs.append(ANY)
        aliases = {len(operands): 0}
        operands.append(sigma)
    return pl.pallas_call(
        functools.partial(finish_kernel, first),
        out_shape=(
            jax.ShapeDtypeStruct((1, *live.shape), jnp.bfloat16),
            jax.ShapeDtypeStruct(before.shape, jnp.float32),
        ),
        in_specs=in_specs,
        out_specs=(ANY, WHOLE),
        scratch_shapes=[pltpu.VMEM((count, cols), jnp.bfloat16), pltpu.SemaphoreType.DMA((4,))],
        input_output_aliases=aliases,
        compiler_params=params(),
        cost_estimate=SMALL,
        name="finish_rows",
    )(*operands)


def sum_kernel(in_ref, out_ref):
    out_ref[0] = jnp.sum(in_ref[:, :1])


def sum_over_sectors(value):
    arrived = lax.all_to_all(value, "sec", 0, 0, tiled=True)
    return pl.pallas_call(
        sum_kernel,
        out_shape=jax.ShapeDtypeStruct((1,), jnp.float32),
        in_specs=[WHOLE],
        out_specs=SMEM,
        compiler_params=params(),
        cost_estimate=SMALL,
        name="sum_energy",
    )(arrived)


def on_device(psi, left_env, right_env, row_sizes, col_sizes):
    sectors = lax.axis_size("sec")
    sector = lax.axis_index("sec")
    even = sector % 2 == 0
    place = sector % 4

    def send(value, *hops):
        pairs = [
            (s, s + steps)
            for at, steps in hops
            for s in range(at, sectors, 4)
            if 0 <= s + steps < sectors
        ]
        return lax.ppermute(value, "sec", pairs)

    rows = psi.shape[1]
    part = rows // 2
    which = jnp.where(place == 0, 1, jnp.where(place == 2, 0, 2))
    orders = [jnp.where(even, 2, 1), jnp.where(even, 3, 2), jnp.where(even, 1, 3), 0]
    info = jnp.stack([*orders, row_sizes[0], col_sizes[0], which]).astype(jnp.int32)

    pairs_up = [(s, s + 1) for s in range(1, sectors, 4) if s + 1 < sectors]
    pairs_up += [(s, s - 3) for s in range(3, sectors, 4) if s + 1 < sectors]

    def raise_one(value):
        return lax.ppermute(value, "sec", pairs_up)

    def up_chip(value):
        return send(value, (0, 1), (2, 1))

    def along(value):
        return send(value, (3, 3), (0, -3))

    def across(value):
        return send(value, (1, 2), (2, -1))

    def swap(value):
        return send(value, (0, 1), (1, -1), (2, 1), (3, -1))

    def relay(value):
        return send(value, (0, 4))

    envs = (left_env, right_env)
    first0, token, live, *ops0 = opening_rows(info, psi[0], envs, 0, part, masks=True)
    paired0 = up_chip(first0)
    first1, token = term_rows(info, live, ops0, part, part, token)
    paired1 = up_chip(first1)
    both0, token = add(first0, paired0, token)
    raised0 = raise_one(both0)
    second0, token, *ops = opening_rows(info, live, envs, 1, part, token, following=2)
    ops1, ops2 = ops[:2], ops[2:]
    moved0 = along(second0)
    both1, token = add(first1, paired1, token)
    raised1 = raise_one(both1)
    second1, token, *ops3 = term_rows(info, live, ops1, part, part, token, bring=(3, *envs))
    moved1 = along(second1)
    third0, token = term_rows(info, live, ops2, 0, part, token)
    swapped0 = swap(third0)
    raised0, token = hold(raised0, token)
    relayed0 = relay(raised0)
    third1, token = term_rows(info, live, ops2, part, part, token)
    swapped1 = swap(third1)
    summed0, token = add(second0, moved0, token)
    crossed0 = across(summed0)
    own0, token = term_rows(info, live, ops3, 0, part, token, added=swapped0)
    raised1, token = hold(raised1, token)
    relayed1 = relay(raised1)
    token = touch(relayed0, token)
    summed1, token = add(second1, moved1, token)
    crossed1 = across(summed1)

    energy = jnp.zeros((sectors, 128), jnp.float32)
    sigma, energy = finish(info, live, own0, (raised0, relayed0, crossed0), energy, None, 0)
    own1, token = term_rows(info, live, ops3, part, part, token, energy, added=swapped1)
    sigma, energy = finish(info, live, own1, (raised1, relayed1, crossed1), energy, sigma, part)
    return sigma, sum_over_sectors(energy)


def solution(mesh):
    return jax.shard_map(
        on_device,
        mesh=mesh,
        in_specs=(
            P(("grp", "sec"), None, None),
            P(("grp", "sec"), None, None, None),
            P(("grp", "sec"), None, None, None),
            P(("grp", "sec")),
            P(("grp", "sec")),
        ),
        out_specs=(P(("grp", "sec"), None, None), P("grp")),
        check_vma=False,
    )
```

```python
import functools

import jax
import jax.numpy as jnp
from jax import lax
from jax.experimental import pallas as pl
from jax.experimental.pallas import tpu as pltpu
from jax.sharding import PartitionSpec as P

MIB = 1024 * 1024
LEFT_PIECES, RIGHT_PIECES = 8, 2
FIRST_MIB = 48
BRING_MIB = 42

ANY = pl.BlockSpec(memory_space=pl.ANY)
HBM = pl.BlockSpec(memory_space=pltpu.HBM)
SMEM = pl.BlockSpec(memory_space=pltpu.SMEM)
WHOLE = pl.BlockSpec(memory_space=pltpu.VMEM)
TOKEN = jax.ShapeDtypeStruct((8, 128), jnp.float32)
SMALL = pl.CostEstimate(flops=200000000, bytes_accessed=1000000, transcendentals=0)


def params(mib=8):
    return pltpu.CompilerParams(vmem_limit_bytes=mib * MIB)


def fetch(info_ref, slot, left_hbm, right_hbm, left_ref, right_ref, sems):
    term = info_ref[slot]
    rows, cols = left_ref.shape[0], right_ref.shape[0]
    step = rows // LEFT_PIECES
    left, right = [], []
    for i in range(LEFT_PIECES):
        span = pl.ds(i * step, step)
        left.append(
            pltpu.make_async_copy(left_hbm.at[0, term, span, :], left_ref.at[span, :], sems.at[i])
        )
    step = cols // RIGHT_PIECES
    for i in range(RIGHT_PIECES):
        span = pl.ds(i * step, step)
        right.append(
            pltpu.make_async_copy(
                right_hbm.at[0, term, span, :], right_ref.at[span, :], sems.at[LEFT_PIECES + i]
            )
        )
    half = LEFT_PIECES // 2
    return left[:half] + right, left[half:]


def multiply(left, live, right):
    first = jnp.dot(left, live, preferred_element_type=jnp.float32).astype(jnp.bfloat16)
    return jnp.dot(first, right, preferred_element_type=jnp.float32)


def opening_kernel(slot, masks, tokens, info_ref, live_ref, left_hbm, right_hbm, *refs):
    refs = list(refs[tokens:])
    out_ref, _ = refs[:2]
    sems = refs[-1]
    operands = refs[2:-1]
    psi_ref = live_ref
    if masks:
        live_ref = operands.pop(0)
    own, late = fetch(info_ref, slot, left_hbm, right_hbm, *operands, sems)
    for copy in own + late:
        copy.start()
    if masks:
        rows, cols = psi_ref.shape
        step = 128
        col = lax.broadcasted_iota(jnp.int32, (step, cols), 1) < info_ref[5]
        row = lax.broadcasted_iota(jnp.int32, (step, cols), 0)
        for start in range(0, rows, step):
            span = pl.ds(start, step)
            inside = jnp.logical_and(row < info_ref[4] - start, col)
            values = jnp.where(inside, psi_ref[span, :].astype(jnp.float32), 0.0)
            live_ref[span, :] = values.astype(live_ref.dtype)
    for copy in own:
        copy.wait()
    out_ref[...] = multiply(operands[0][: out_ref.shape[0], :], live_ref[...], operands[1][...])
    for copy in late:
        copy.wait()


def operand_shapes(width, cols):
    return [
        jax.ShapeDtypeStruct((width, width), jnp.bfloat16),
        jax.ShapeDtypeStruct((cols, cols), jnp.bfloat16),
    ]


def opening_rows(info, live, envs, slot, count, *tokens, masks=False):
    width, cols = live.shape
    out_shape = [jax.ShapeDtypeStruct((count, cols), jnp.float32), TOKEN]
    if masks:
        out_shape.append(jax.ShapeDtypeStruct(live.shape, live.dtype))
    out_shape += operand_shapes(width, cols)
    return pl.pallas_call(
        functools.partial(opening_kernel, slot, masks, len(tokens)),
        out_shape=out_shape,
        in_specs=[SMEM, WHOLE, HBM, HBM] + [ANY] * len(tokens),
        out_specs=[WHOLE, ANY] + [WHOLE] * (len(out_shape) - 2),
        scratch_shapes=[pltpu.SemaphoreType.DMA((LEFT_PIECES + RIGHT_PIECES,))],
        compiler_params=params(FIRST_MIB if masks else BRING_MIB),
        cost_estimate=SMALL,
        name="opening_rows",
    )(info, live, *envs, *tokens)


def term_kernel(first, adds, slot, tokens, info_ref, live_ref, left_ref, right_ref, *refs):
    refs = list(refs)
    add_ref = refs.pop(0) if adds else None
    copies = []
    if slot is not None:
        left_hbm, right_hbm = refs[:2]
        sems = refs[-1]
        out_ref, _, left_next, right_next = refs[2 + tokens : -1]
        copies = sum(fetch(info_ref, slot, left_hbm, right_hbm, left_next, right_next, sems), [])
        for copy in copies:
            copy.start()
    else:
        out_ref, _ = refs[tokens:]
    count = out_ref.shape[0]
    block = min(count, 512)
    for i in range(count // block):
        span = pl.ds(i * block, block)
        value = multiply(left_ref[pl.ds(first + i * block, block), :], live_ref[...], right_ref[...])
        if adds:
            value = value + add_ref[span, :]
        out_ref[span, :] = value
    for copy in copies:
        copy.wait()


def term_rows(info, live, operands, first, count, *tokens, added=None, bring=None):
    width, cols = live.shape
    in_specs = [SMEM, WHOLE, WHOLE, WHOLE]
    args = [info, live, *operands]
    out_shape = [jax.ShapeDtypeStruct((count, cols), jnp.float32), TOKEN]
    out_specs = [WHOLE, ANY]
    scratch = []
    slot = None
    if added is not None:
        in_specs.append(WHOLE)
        args.append(added)
    if bring is not None:
        slot = bring[0]
        in_specs += [HBM, HBM]
        args += bring[1:]
        out_shape += operand_shapes(width, cols)
        out_specs += [WHOLE, WHOLE]
        scratch.append(pltpu.SemaphoreType.DMA((LEFT_PIECES + RIGHT_PIECES,)))
    return pl.pallas_call(
        functools.partial(term_kernel, first, added is not None, slot, len(tokens)),
        out_shape=out_shape,
        in_specs=in_specs + [ANY] * len(tokens),
        out_specs=out_specs,
        scratch_shapes=scratch,
        compiler_params=params(12 if slot is None else BRING_MIB),
        cost_estimate=SMALL,
        name="term_rows",
    )(*args, *tokens)


def add_kernel(a_ref, b_ref, *refs):
    out_ref = refs[-2]
    rows = a_ref.shape[0]
    step = 64

    def body(i, _):
        span = pl.ds(pl.multiple_of(i * step, step), step)
        out_ref[span, :] = a_ref[span, :] + b_ref[span, :]
        return _

    lax.fori_loop(0, rows // step, body, 0)


def add(a, b, *tokens):
    return pl.pallas_call(
        add_kernel,
        out_shape=(jax.ShapeDtypeStruct(a.shape, a.dtype), TOKEN),
        in_specs=[WHOLE, WHOLE] + [ANY] * len(tokens),
        out_specs=(WHOLE, ANY),
        compiler_params=params(),
        cost_estimate=SMALL,
        name="add_blocks",
    )(a, b, *tokens)


def touch(*values):
    return pl.pallas_call(
        lambda *refs: None,
        out_shape=TOKEN,
        in_specs=[ANY] * len(values),
        out_specs=ANY,
        compiler_params=params(),
        cost_estimate=SMALL,
        name="touch",
    )(*values)


def hold(value, token):
    return pl.pallas_call(
        lambda *refs: None,
        out_shape=(jax.ShapeDtypeStruct(value.shape, value.dtype), TOKEN),
        in_specs=[ANY, ANY],
        out_specs=(ANY, ANY),
        input_output_aliases={0: 0},
        compiler_params=params(),
        cost_estimate=SMALL,
        name="hold",
    )(value, token)


def finish_kernel(first, info_ref, live_ref, own_ref, a_ref, b_ref, c_ref, before_ref, *refs):
    sigma_hbm, energy_ref, sigma_buf, sems = refs[-4:]
    count, cols = own_ref.shape
    step = 64
    piece = count // sems.shape[0]
    col = lax.broadcasted_iota(jnp.int32, (step, cols), 1) < info_ref[5]
    row = lax.broadcasted_iota(jnp.int32, (step, cols), 0)

    def copy(i):
        span = pl.ds(i * piece, piece)
        return pltpu.make_async_copy(
            sigma_buf.at[span, :], sigma_hbm.at[0, pl.ds(first + i * piece, piece), :], sems.at[i]
        )

    def work(arrival):
        energy = jnp.zeros((8, cols), jnp.float32)
        for i in range(count // piece):

            def body(n, energy):
                start = pl.multiple_of(i * piece + n * step, step)
                span = pl.ds(start, step)
                inside = jnp.logical_and(row < info_ref[4] - first - start, col)
                total = jnp.where(inside, own_ref[span, :] + arrival[span, :], 0.0)
                sigma_buf[span, :] = total.astype(sigma_buf.dtype)
                here = pl.ds(pl.multiple_of(first + start, step), step)
                product = live_ref[here, :].astype(jnp.float32) * total
                return energy + jnp.sum(jnp.reshape(product, (step // 8, 8, cols)), axis=0)

            energy = lax.fori_loop(0, piece // step, body, energy)
            copy(i).start()
        energy_ref[...] = before_ref[...] + jnp.sum(energy)

    for n, arrival in enumerate((a_ref, b_ref, c_ref)):
        pl.when(info_ref[6] == n)(functools.partial(work, arrival))
    for i in range(count // piece):
        copy(i).wait()


def finish(info, live, own, arrivals, before, sigma, first):
    count, cols = own.shape
    in_specs = [SMEM] + [WHOLE] * 6
    operands = [info, live, own, *arrivals, before]
    aliases = {}
    if sigma is not None:
        in_specs.append(ANY)
        aliases = {len(operands): 0}
        operands.append(sigma)
    return pl.pallas_call(
        functools.partial(finish_kernel, first),
        out_shape=(
            jax.ShapeDtypeStruct((1, *live.shape), jnp.bfloat16),
            jax.ShapeDtypeStruct(before.shape, jnp.float32),
        ),
        in_specs=in_specs,
        out_specs=(ANY, WHOLE),
        scratch_shapes=[pltpu.VMEM((count, cols), jnp.bfloat16), pltpu.SemaphoreType.DMA((4,))],
        input_output_aliases=aliases,
        compiler_params=params(),
        cost_estimate=SMALL,
        name="finish_rows",
    )(*operands)


def sum_kernel(in_ref, out_ref):
    out_ref[0] = jnp.sum(in_ref[:, :1])


def sum_over_sectors(value):
    arrived = lax.all_to_all(value, "sec", 0, 0, tiled=True)
    return pl.pallas_call(
        sum_kernel,
        out_shape=jax.ShapeDtypeStruct((1,), jnp.float32),
        in_specs=[WHOLE],
        out_specs=SMEM,
        compiler_params=params(),
        cost_estimate=SMALL,
        name="sum_energy",
    )(arrived)


def on_device(psi, left_env, right_env, row_sizes, col_sizes):
    sectors = lax.axis_size("sec")
    sector = lax.axis_index("sec")
    even = sector % 2 == 0
    place = sector % 4

    def send(value, *hops):
        pairs = [
            (s, s + steps)
            for at, steps in hops
            for s in range(at, sectors, 4)
            if 0 <= s + steps < sectors
        ]
        return lax.ppermute(value, "sec", pairs)

    rows = psi.shape[1]
    part = rows // 2
    which = jnp.where(place == 0, 1, jnp.where(place == 2, 0, 2))
    orders = [jnp.where(even, 2, 1), jnp.where(even, 3, 2), jnp.where(even, 1, 3), 0]
    info = jnp.stack([*orders, row_sizes[0], col_sizes[0], which]).astype(jnp.int32)

    pairs_up = [(s, s + 1) for s in range(1, sectors, 4) if s + 1 < sectors]
    pairs_up += [(s, s - 3) for s in range(3, sectors, 4) if s + 1 < sectors]

    def raise_one(value):
        return lax.ppermute(value, "sec", pairs_up)

    def up_chip(value):
        return send(value, (0, 1), (2, 1))

    def along(value):
        return send(value, (3, 3), (0, -3))

    def across(value):
        return send(value, (1, 2), (2, -1))

    def swap(value):
        return send(value, (0, 1), (1, -1), (2, 1), (3, -1))

    def relay(value):
        return send(value, (0, 4))

    envs = (left_env, right_env)
    first0, token, live, *ops0 = opening_rows(info, psi[0], envs, 0, part, masks=True)
    paired0 = up_chip(first0)
    first1, token = term_rows(info, live, ops0, part, part, token)
    paired1 = up_chip(first1)
    both0, token = add(first0, paired0, token)
    raised0 = raise_one(both0)
    second0, token, *ops1 = opening_rows(info, live, envs, 1, part, token)
    moved0 = along(second0)
    both1, token = add(first1, paired1, token)
    raised1 = raise_one(both1)
    second1, token, *ops2 = term_rows(info, live, ops1, part, part, token, bring=(2, *envs))
    moved1 = along(second1)
    third0, token, *ops3 = term_rows(info, live, ops2, 0, part, token, bring=(3, *envs))
    swapped0 = swap(third0)
    raised0, token = hold(raised0, token)
    relayed0 = relay(raised0)
    third1, token = term_rows(info, live, ops2, part, part, token)
    swapped1 = swap(third1)
    summed0, token = add(second0, moved0, token)
    crossed0 = across(summed0)
    raised1, token = hold(raised1, token)
    relayed1 = relay(raised1)
    own0, token = term_rows(info, live, ops3, 0, part, token, added=swapped0)
    token = touch(relayed0, token)
    summed1, token = add(second1, moved1, token)
    crossed1 = across(summed1)

    energy = jnp.zeros((sectors, 128), jnp.float32)
    sigma, energy = finish(info, live, own0, (raised0, relayed0, crossed0), energy, None, 0)
    own1, token = term_rows(info, live, ops3, part, part, token, energy, added=swapped1)
    sigma, energy = finish(info, live, own1, (raised1, relayed1, crossed1), energy, sigma, part)
    return sigma, sum_over_sectors(energy)


def solution(mesh):
    return jax.shard_map(
        on_device,
        mesh=mesh,
        in_specs=(
            P(("grp", "sec"), None, None),
            P(("grp", "sec"), None, None, None),
            P(("grp", "sec"), None, None, None),
            P(("grp", "sec")),
            P(("grp", "sec")),
        ),
        out_specs=(P(("grp", "sec"), None, None), P("grp")),
        check_vma=False,
    )
```

```python
import functools

import jax
import jax.numpy as jnp
from jax import lax
from jax.experimental import pallas as pl
from jax.experimental.pallas import tpu as pltpu
from jax.sharding import PartitionSpec as P

MIB = 1024 * 1024
LEFT_PIECES, RIGHT_PIECES = 4, 2
PRE_MIB = 48
FIRST_MIB = 48
BRING_MIB = 42

ANY = pl.BlockSpec(memory_space=pl.ANY)
HBM = pl.BlockSpec(memory_space=pltpu.HBM)
SMEM = pl.BlockSpec(memory_space=pltpu.SMEM)
WHOLE = pl.BlockSpec(memory_space=pltpu.VMEM)
TOKEN = jax.ShapeDtypeStruct((8, 128), jnp.float32)
SMALL = pl.CostEstimate(flops=200000000, bytes_accessed=1000000, transcendentals=0)


def params(mib=8):
    return pltpu.CompilerParams(vmem_limit_bytes=mib * MIB)


def fetch(info_ref, bring, left_hbm, right_hbm, left_ref, right_ref, sems):
    slot, half, _ = bring
    term = info_ref[slot]
    rows = left_ref.shape[0]
    step = rows // LEFT_PIECES
    copies = []
    for i in range(LEFT_PIECES):
        there = left_hbm.at[0, term, pl.ds(half * rows + i * step, step), :]
        here = left_ref.at[pl.ds(i * step, step), :]
        copies.append(pltpu.make_async_copy(there, here, sems.at[i]))
    if right_ref is not None:
        step = right_ref.shape[0] // RIGHT_PIECES
        for i in range(RIGHT_PIECES):
            span = pl.ds(i * step, step)
            there = right_hbm.at[0, term, span, :]
            copies.append(
                pltpu.make_async_copy(there, right_ref.at[span, :], sems.at[LEFT_PIECES + i])
            )
    return copies


def bring_kernel(bring, info_ref, left_hbm, left_ref, _, sems):
    copies = fetch(info_ref, bring, left_hbm, None, left_ref, None, sems)
    for copy in copies:
        copy.start()
    for copy in copies:
        copy.wait()


def operand_shapes(width, cols, bring):
    left = jax.ShapeDtypeStruct((width // 2, width), jnp.bfloat16)
    right = jax.ShapeDtypeStruct((cols, cols), jnp.bfloat16)
    return [left, right] if bring[2] else [left]


def bring_left(info, left_env, bring):
    return pl.pallas_call(
        functools.partial(bring_kernel, bring),
        out_shape=[*operand_shapes(left_env.shape[-1], 0, bring), TOKEN],
        in_specs=[SMEM, HBM],
        out_specs=[WHOLE, ANY],
        scratch_shapes=[pltpu.SemaphoreType.DMA((LEFT_PIECES,))],
        compiler_params=params(PRE_MIB),
        cost_estimate=SMALL,
        name="bring_left",
    )(info, left_env)


def term_kernel(masks, adds, bring, tokens, info_ref, live_ref, left_ref, *refs):
    refs = list(refs)
    right_ref = None if masks else refs.pop(0)
    add_ref = refs.pop(0) if adds else None
    copies, right_copies = [], []
    if bring is not None:
        left_hbm, right_hbm = refs[:2]
        refs = refs[2:]
        sems = refs.pop()
    refs = refs[tokens:]
    out_ref, _ = refs[:2]
    refs = refs[2:]
    psi_ref = live_ref
    if masks:
        live_ref = refs.pop(0)
    if bring is not None:
        right_next = refs[1] if bring[2] else None
        copies = fetch(info_ref, bring, left_hbm, right_hbm, refs[0], right_next, sems)
        if masks:
            right_ref = right_next
            copies, right_copies = copies[:LEFT_PIECES], copies[LEFT_PIECES:]
        for copy in right_copies + copies:
            copy.start()
    if masks:
        rows, cols = psi_ref.shape
        step = 128
        col = lax.broadcasted_iota(jnp.int32, (step, cols), 1) < info_ref[5]
        row = lax.broadcasted_iota(jnp.int32, (step, cols), 0)
        for start in range(0, rows, step):
            span = pl.ds(start, step)
            inside = jnp.logical_and(row < info_ref[4] - start, col)
            values = jnp.where(inside, psi_ref[span, :].astype(jnp.float32), 0.0)
            live_ref[span, :] = values.astype(live_ref.dtype)
    value = jnp.dot(left_ref[...], live_ref[...], preferred_element_type=jnp.float32)
    for copy in right_copies:
        copy.wait()
    value = jnp.dot(
        value.astype(jnp.bfloat16), right_ref[...], preferred_element_type=jnp.float32
    )
    out_ref[...] = value + add_ref[...] if adds else value
    for copy in copies:
        copy.wait()


def term_rows(info, live, envs, left, right, *tokens, added=None, bring=None, masks=False):
    width, cols = live.shape
    in_specs = [SMEM, WHOLE, WHOLE]
    args = [info, live, left]
    if not masks:
        in_specs.append(WHOLE)
        args.append(right)
    out_shape = [jax.ShapeDtypeStruct((left.shape[0], cols), jnp.float32), TOKEN]
    scratch = []
    if added is not None:
        in_specs.append(WHOLE)
        args.append(added)
    if masks:
        out_shape.append(jax.ShapeDtypeStruct(live.shape, live.dtype))
    if bring is not None:
        in_specs += [HBM, HBM]
        args += envs
        out_shape += operand_shapes(width, cols, bring)
        scratch.append(pltpu.SemaphoreType.DMA((LEFT_PIECES + RIGHT_PIECES,)))
    return pl.pallas_call(
        functools.partial(term_kernel, masks, added is not None, bring, len(tokens)),
        out_shape=out_shape,
        in_specs=in_specs + [ANY] * len(tokens),
        out_specs=[WHOLE, ANY] + [WHOLE] * (len(out_shape) - 2),
        scratch_shapes=scratch,
        compiler_params=params(12 if bring is None else FIRST_MIB if masks else BRING_MIB),
        cost_estimate=SMALL,
        name="term_rows",
    )(*args, *tokens)


def add_kernel(a_ref, b_ref, *refs):
    out_ref = refs[-2]
    rows = a_ref.shape[0]
    step = 64

    def body(i, _):
        span = pl.ds(pl.multiple_of(i * step, step), step)
        out_ref[span, :] = a_ref[span, :] + b_ref[span, :]
        return _

    lax.fori_loop(0, rows // step, body, 0)


def add(a, b, *tokens):
    return pl.pallas_call(
        add_kernel,
        out_shape=(jax.ShapeDtypeStruct(a.shape, a.dtype), TOKEN),
        in_specs=[WHOLE, WHOLE] + [ANY] * len(tokens),
        out_specs=(WHOLE, ANY),
        compiler_params=params(),
        cost_estimate=SMALL,
        name="add_blocks",
    )(a, b, *tokens)


def touch(*values):
    return pl.pallas_call(
        lambda *refs: None,
        out_shape=TOKEN,
        in_specs=[ANY] * len(values),
        out_specs=ANY,
        compiler_params=params(),
        cost_estimate=SMALL,
        name="touch",
    )(*values)


def hold(value, token):
    return pl.pallas_call(
        lambda *refs: None,
        out_shape=(jax.ShapeDtypeStruct(value.shape, value.dtype), TOKEN),
        in_specs=[ANY, ANY],
        out_specs=(ANY, ANY),
        input_output_aliases={0: 0},
        compiler_params=params(),
        cost_estimate=SMALL,
        name="hold",
    )(value, token)


def finish_kernel(first, info_ref, live_ref, own_ref, a_ref, b_ref, c_ref, before_ref, *refs):
    sigma_hbm, energy_ref, sigma_buf, sems = refs[-4:]
    count, cols = own_ref.shape
    step = 64
    piece = count // sems.shape[0]
    col = lax.broadcasted_iota(jnp.int32, (step, cols), 1) < info_ref[5]
    row = lax.broadcasted_iota(jnp.int32, (step, cols), 0)

    def copy(i):
        span = pl.ds(i * piece, piece)
        return pltpu.make_async_copy(
            sigma_buf.at[span, :], sigma_hbm.at[0, pl.ds(first + i * piece, piece), :], sems.at[i]
        )

    def work(arrival):
        energy = jnp.zeros((8, cols), jnp.float32)
        for i in range(count // piece):

            def body(n, energy):
                start = pl.multiple_of(i * piece + n * step, step)
                span = pl.ds(start, step)
                inside = jnp.logical_and(row < info_ref[4] - first - start, col)
                total = jnp.where(inside, own_ref[span, :] + arrival[span, :], 0.0)
                sigma_buf[span, :] = total.astype(sigma_buf.dtype)
                here = pl.ds(pl.multiple_of(first + start, step), step)
                product = live_ref[here, :].astype(jnp.float32) * total
                return energy + jnp.sum(jnp.reshape(product, (step // 8, 8, cols)), axis=0)

            energy = lax.fori_loop(0, piece // step, body, energy)
            copy(i).start()
        energy_ref[...] = before_ref[...] + jnp.sum(energy)

    for n, arrival in enumerate((a_ref, b_ref, c_ref)):
        pl.when(info_ref[6] == n)(functools.partial(work, arrival))
    for i in range(count // piece):
        copy(i).wait()


def finish(info, live, own, arrivals, before, sigma, first):
    count, cols = own.shape
    in_specs = [SMEM] + [WHOLE] * 6
    operands = [info, live, own, *arrivals, before]
    aliases = {}
    if sigma is not None:
        in_specs.append(ANY)
        aliases = {len(operands): 0}
        operands.append(sigma)
    return pl.pallas_call(
        functools.partial(finish_kernel, first),
        out_shape=(
            jax.ShapeDtypeStruct((1, *live.shape), jnp.bfloat16),
            jax.ShapeDtypeStruct(before.shape, jnp.float32),
        ),
        in_specs=in_specs,
        out_specs=(ANY, WHOLE),
        scratch_shapes=[pltpu.VMEM((count, cols), jnp.bfloat16), pltpu.SemaphoreType.DMA((4,))],
        input_output_aliases=aliases,
        compiler_params=params(),
        cost_estimate=SMALL,
        name="finish_rows",
    )(*operands)


def sum_kernel(in_ref, out_ref):
    out_ref[0] = jnp.sum(in_ref[:, :1])


def sum_over_sectors(value):
    arrived = lax.all_to_all(value, "sec", 0, 0, tiled=True)
    return pl.pallas_call(
        sum_kernel,
        out_shape=jax.ShapeDtypeStruct((1,), jnp.float32),
        in_specs=[WHOLE],
        out_specs=SMEM,
        compiler_params=params(),
        cost_estimate=SMALL,
        name="sum_energy",
    )(arrived)


def on_device(psi, left_env, right_env, row_sizes, col_sizes):
    sectors = lax.axis_size("sec")
    sector = lax.axis_index("sec")
    even = sector % 2 == 0
    place = sector % 4

    def send(value, *hops):
        pairs = [
            (s, s + steps)
            for at, steps in hops
            for s in range(at, sectors, 4)
            if 0 <= s + steps < sectors
        ]
        return lax.ppermute(value, "sec", pairs)

    rows = psi.shape[1]
    part = rows // 2
    which = jnp.where(place == 0, 1, jnp.where(place == 2, 0, 2))
    orders = [jnp.where(even, 2, 1), jnp.where(even, 3, 2), jnp.where(even, 1, 3), 0]
    info = jnp.stack([*orders, row_sizes[0], col_sizes[0], which]).astype(jnp.int32)

    pairs_up = [(s, s + 1) for s in range(1, sectors, 4) if s + 1 < sectors]
    pairs_up += [(s, s - 3) for s in range(3, sectors, 4) if s + 1 < sectors]

    def raise_one(value):
        return lax.ppermute(value, "sec", pairs_up)

    def up_chip(value):
        return send(value, (0, 1), (2, 1))

    def along(value):
        return send(value, (3, 3), (0, -3))

    def across(value):
        return send(value, (1, 2), (2, -1))

    def swap(value):
        return send(value, (0, 1), (1, -1), (2, 1), (3, -1))

    def relay(value):
        return send(value, (0, 4))

    envs = (left_env, right_env)

    def term(left, right, *tokens, **more):
        return term_rows(info, live, envs, left, right, *tokens, **more)

    left, token = bring_left(info, left_env, (0, 0, False))
    first0, token, live, left, right = term_rows(
        info, psi[0], envs, left, None, token, bring=(0, 1, True), masks=True
    )
    paired0 = up_chip(first0)
    first1, token, left, right = term(left, right, token, bring=(1, 0, True))
    paired1 = up_chip(first1)
    both0, token = add(first0, paired0, token)
    raised0 = raise_one(both0)
    second0, token, left = term(left, right, token, bring=(1, 1, False))
    moved0 = along(second0)
    both1, token = add(first1, paired1, token)
    raised1 = raise_one(both1)
    second1, token, left, right = term(left, right, token, bring=(2, 0, True))
    moved1 = along(second1)
    third0, token, left = term(left, right, token, bring=(2, 1, False))
    swapped0 = swap(third0)
    raised0, token = hold(raised0, token)
    relayed0 = relay(raised0)
    third1, token, left, right = term(left, right, token, bring=(3, 0, True))
    swapped1 = swap(third1)
    summed0, token = add(second0, moved0, token)
    crossed0 = across(summed0)
    raised1, token = hold(raised1, token)
    relayed1 = relay(raised1)
    own0, token, left = term(left, right, token, added=swapped0, bring=(3, 1, False))
    token = touch(relayed0, token)
    summed1, token = add(second1, moved1, token)
    crossed1 = across(summed1)

    energy = jnp.zeros((sectors, 128), jnp.float32)
    sigma, energy = finish(info, live, own0, (raised0, relayed0, crossed0), energy, None, 0)
    own1, token = term(left, right, token, energy, added=swapped1)
    sigma, energy = finish(info, live, own1, (raised1, relayed1, crossed1), energy, sigma, part)
    return sigma, sum_over_sectors(energy)


def solution(mesh):
    return jax.shard_map(
        on_device,
        mesh=mesh,
        in_specs=(
            P(("grp", "sec"), None, None),
            P(("grp", "sec"), None, None, None),
            P(("grp", "sec"), None, None, None),
            P(("grp", "sec")),
            P(("grp", "sec")),
        ),
        out_specs=(P(("grp", "sec"), None, None), P("grp")),
        check_vma=False,
    )
```

```python
import functools

import jax
import jax.numpy as jnp
from jax import lax
from jax.experimental import pallas as pl
from jax.experimental.pallas import tpu as pltpu
from jax.sharding import PartitionSpec as P

MIB = 1024 * 1024
PIECE = 128
LEFT_PIECES, RIGHT_PIECES = 8, 2
FIRST_MIB = 46
BRING_MIB = 42

ANY = pl.BlockSpec(memory_space=pl.ANY)
HBM = pl.BlockSpec(memory_space=pltpu.HBM)
SMEM = pl.BlockSpec(memory_space=pltpu.SMEM)
WHOLE = pl.BlockSpec(memory_space=pltpu.VMEM)
TOKEN = jax.ShapeDtypeStruct((8, 128), jnp.float32)
SMALL = pl.CostEstimate(flops=200000000, bytes_accessed=1000000, transcendentals=0)


def params(mib=8):
    return pltpu.CompilerParams(vmem_limit_bytes=mib * MIB)


def fetch(info_ref, slot, left_hbm, right_hbm, left_ref, right_ref, sems):
    term = info_ref[slot]
    rows, cols = left_ref.shape[0], right_ref.shape[0]
    step = rows // LEFT_PIECES
    left, right = [], []
    for i in range(LEFT_PIECES):
        span = pl.ds(i * step, step)
        left.append(
            pltpu.make_async_copy(left_hbm.at[0, term, span, :], left_ref.at[span, :], sems.at[i])
        )
    step = cols // RIGHT_PIECES
    for i in range(RIGHT_PIECES):
        span = pl.ds(i * step, step)
        right.append(
            pltpu.make_async_copy(
                right_hbm.at[0, term, span, :], right_ref.at[span, :], sems.at[LEFT_PIECES + i]
            )
        )
    half = LEFT_PIECES // 2
    return left[:half] + right, left[half:]


def multiply(left, live, right):
    first = jnp.dot(left, live, preferred_element_type=jnp.float32).astype(jnp.bfloat16)
    return jnp.dot(first, right, preferred_element_type=jnp.float32)


def opening_kernel(slot, cut, tokens, info_ref, live_ref, left_hbm, right_hbm, *refs):
    masks = cut is not None
    refs = list(refs[tokens:])
    out_ref, _ = refs[:2]
    sems = refs[-1]
    operands = refs[2:-1]
    psi_ref = live_ref
    if masks:
        live_ref, wide_ref = operands[:2]
        operands = operands[2:]
    own, late = fetch(info_ref, slot, left_hbm, right_hbm, *operands, sems)
    for copy in own + late:
        copy.start()
    if masks:
        rows, cols = psi_ref.shape
        step = 128
        col = lax.broadcasted_iota(jnp.int32, (step, cols), 1) < info_ref[5]
        row = lax.broadcasted_iota(jnp.int32, (step, cols), 0)
        for start in range(0, rows, step):
            span = pl.ds(start, step)
            inside = jnp.logical_and(row < info_ref[4] - start, col)
            values = jnp.where(inside, psi_ref[span, :].astype(jnp.float32), 0.0)
            live_ref[span, :] = values.astype(live_ref.dtype)
            if start >= cut:
                wide_ref[pl.ds(start - cut, step), :] = values
    for copy in own:
        copy.wait()
    out_ref[...] = multiply(operands[0][: out_ref.shape[0], :], live_ref[...], operands[1][...])
    for copy in late:
        copy.wait()


def operand_shapes(width, cols):
    return [
        jax.ShapeDtypeStruct((width, width), jnp.bfloat16),
        jax.ShapeDtypeStruct((cols, cols), jnp.bfloat16),
    ]


def opening_rows(info, live, envs, slot, count, *tokens, cut=None):
    width, cols = live.shape
    out_shape = [jax.ShapeDtypeStruct((count, cols), jnp.float32), TOKEN]
    if cut is not None:
        out_shape.append(jax.ShapeDtypeStruct(live.shape, live.dtype))
        out_shape.append(jax.ShapeDtypeStruct((width - cut, cols), jnp.float32))
    out_shape += operand_shapes(width, cols)
    return pl.pallas_call(
        functools.partial(opening_kernel, slot, cut, len(tokens)),
        out_shape=out_shape,
        in_specs=[SMEM, WHOLE, HBM, HBM] + [ANY] * len(tokens),
        out_specs=[WHOLE, ANY] + [WHOLE] * (len(out_shape) - 2),
        scratch_shapes=[pltpu.SemaphoreType.DMA((LEFT_PIECES + RIGHT_PIECES,))],
        compiler_params=params(BRING_MIB if cut is None else FIRST_MIB),
        cost_estimate=SMALL,
        name="opening_rows",
    )(info, live, *envs, *tokens)


def term_kernel(first, parts, slot, tokens, info_ref, live_ref, left_ref, right_ref, *refs):
    refs = list(refs)
    add_refs = [refs.pop(0) for _ in range(parts)]
    copies = []
    if slot is not None:
        left_hbm, right_hbm = refs[:2]
        sems = refs[-1]
        out_ref, _, left_next, right_next = refs[2 + tokens : -1]
        copies = sum(fetch(info_ref, slot, left_hbm, right_hbm, left_next, right_next, sems), [])
        for copy in copies:
            copy.start()
    else:
        out_ref, _ = refs[tokens:]
    count = out_ref.shape[0]
    block = count // max(parts, 1)
    for i in range(count // block):
        span = pl.ds(i * block, block)
        value = multiply(left_ref[pl.ds(first + i * block, block), :], live_ref[...], right_ref[...])
        if parts:
            value = value + add_refs[i][...]
        out_ref[span, :] = value
    for copy in copies:
        copy.wait()


def term_rows(info, live, operands, first, count, *tokens, added=None, bring=None):
    width, cols = live.shape
    in_specs = [SMEM, WHOLE, WHOLE, WHOLE]
    args = [info, live, *operands]
    out_shape = [jax.ShapeDtypeStruct((count, cols), jnp.float32), TOKEN]
    out_specs = [WHOLE, ANY]
    scratch = []
    slot = None
    if added is not None:
        in_specs += [WHOLE] * len(added)
        args += added
    if bring is not None:
        slot = bring[0]
        in_specs += [HBM, HBM]
        args += bring[1:]
        out_shape += operand_shapes(width, cols)
        out_specs += [WHOLE, WHOLE]
        scratch.append(pltpu.SemaphoreType.DMA((LEFT_PIECES + RIGHT_PIECES,)))
    return pl.pallas_call(
        functools.partial(term_kernel, first, len(added or ()), slot, len(tokens)),
        out_shape=out_shape,
        in_specs=in_specs + [ANY] * len(tokens),
        out_specs=out_specs,
        scratch_shapes=scratch,
        compiler_params=params(12 if slot is None else BRING_MIB),
        cost_estimate=SMALL,
        name="term_rows",
    )(*args, *tokens)


def add_kernel(a_ref, b_ref, *refs):
    out_ref = refs[-2]
    rows = a_ref.shape[0]
    step = 64

    def body(i, _):
        span = pl.ds(pl.multiple_of(i * step, step), step)
        out_ref[span, :] = a_ref[span, :] + b_ref[span, :]
        return _

    lax.fori_loop(0, rows // step, body, 0)


def add(a, b, *tokens):
    return pl.pallas_call(
        add_kernel,
        out_shape=(jax.ShapeDtypeStruct(a.shape, a.dtype), TOKEN),
        in_specs=[WHOLE, WHOLE] + [ANY] * len(tokens),
        out_specs=(WHOLE, ANY),
        compiler_params=params(),
        cost_estimate=SMALL,
        name="add_blocks",
    )(a, b, *tokens)


def folded(values):
    rows, cols = values.shape
    return jnp.sum(jnp.reshape(values, (rows // 8, 8, cols)), axis=0)


def add_energy_kernel(a_ref, b_ref, psi_ref, _, out_ref, energy_ref, token_ref):
    step = 64

    def body(i, energy):
        span = pl.ds(pl.multiple_of(i * step, step), step)
        value = a_ref[span, :] + b_ref[span, :]
        out_ref[span, :] = value
        return energy + folded(value * psi_ref[span, :])

    zero = jnp.zeros((8, a_ref.shape[1]), jnp.float32)
    energy_ref[...] = lax.fori_loop(0, a_ref.shape[0] // step, body, zero)


def add_energy(a, b, psi, token):
    return pl.pallas_call(
        add_energy_kernel,
        out_shape=(
            jax.ShapeDtypeStruct(a.shape, a.dtype),
            jax.ShapeDtypeStruct((8, a.shape[1]), jnp.float32),
            TOKEN,
        ),
        in_specs=[WHOLE, WHOLE, WHOLE, ANY],
        out_specs=(WHOLE, WHOLE, ANY),
        compiler_params=params(),
        cost_estimate=SMALL,
        name="add_blocks_energy",
    )(a, b, psi, token)


def touch(*values):
    return pl.pallas_call(
        lambda *refs: None,
        out_shape=TOKEN,
        in_specs=[ANY] * len(values),
        out_specs=ANY,
        compiler_params=params(),
        cost_estimate=SMALL,
        name="touch",
    )(*values)


def hold(value, token):
    return pl.pallas_call(
        lambda *refs: None,
        out_shape=(jax.ShapeDtypeStruct(value.shape, value.dtype), TOKEN),
        in_specs=[ANY, ANY],
        out_specs=(ANY, ANY),
        input_output_aliases={0: 0},
        compiler_params=params(),
        cost_estimate=SMALL,
        name="hold",
    )(value, token)


def own_rows(owns, start):
    half = owns[0].shape[0]
    return owns[start // half][pl.ds(start % half, 64), :]


def finish_rows(first, info_ref, owns, arrival, sigma_hbm, buf, sems, live_ref=None):
    count, cols = arrival.shape
    step = 64
    col = lax.broadcasted_iota(jnp.int32, (step, cols), 1) < info_ref[5]
    row = lax.broadcasted_iota(jnp.int32, (step, cols), 0)
    energy = jnp.zeros((8, cols), jnp.float32)
    copies = finish_copies(first, count, sigma_hbm, buf, sems)
    for start in range(0, count, step):
        span, here = pl.ds(start, step), pl.ds(first + start, step)
        inside = jnp.logical_and(row < info_ref[4] - (first + start), col)
        total = jnp.where(inside, own_rows(owns, first + start) + arrival[span, :], 0.0)
        buf[span, :] = total.astype(buf.dtype)
        if live_ref is not None:
            energy += folded(live_ref[here, :].astype(jnp.float32) * total)
        if (start + step) % PIECE == 0:
            copies[start // PIECE].start()
    return energy


def finish_copies(first, count, sigma_hbm, buf, sems):
    copies = []
    for i in range(count // PIECE):
        here = buf.at[pl.ds(i * PIECE, PIECE), :]
        there = sigma_hbm.at[0, pl.ds(first + i * PIECE, PIECE), :]
        copies.append(pltpu.make_async_copy(here, there, sems.at[i]))
    return copies


def middle_kernel(cut, info_ref, own0_ref, own1_ref, live_ref, *refs):
    owns, raised, relayed, crossed = (own0_ref, own1_ref), refs[:2], refs[2:4], refs[4]
    sent_ref, sigma_hbm, energy_ref, buf, sems = refs[5:]
    rows = live_ref.shape[0]

    def put(energy):
        energy = jnp.sum(energy + sent_ref[...])
        energy_ref[...] = jnp.full(energy_ref.shape, energy, jnp.float32)

    for n, halves in enumerate((raised, relayed)):

        @pl.when(info_ref[6] == n)
        def _(halves=halves):
            half = rows // 2
            energy = jnp.zeros(sent_ref.shape, jnp.float32)
            for i, arrival in enumerate(halves):
                here = buf.at[pl.ds(i * half, half), :]
                energy += finish_rows(
                    i * half, info_ref, owns, arrival, sigma_hbm, here, sems.at[i], live_ref
                )
            put(energy)
            for i in range(2):
                here = buf.at[pl.ds(i * half, half), :]
                for copy in finish_copies(i * half, half, sigma_hbm, here, sems.at[i]):
                    copy.wait()

    @pl.when(info_ref[6] == 2)
    def _():
        energy = finish_rows(
            0, info_ref, owns, crossed, sigma_hbm, buf, sems.at[0], live_ref
        )
        for start in range(cut, rows, 64):
            span = pl.ds(start, 64)
            energy += folded(live_ref[span, :].astype(jnp.float32) * own_rows(owns, start))
        put(energy)
        for copy in finish_copies(0, cut, sigma_hbm, buf, sems.at[0]):
            copy.wait()


def last_kernel(cut, info_ref, own0_ref, own1_ref, c_ref, energies_ref, _, sigma_hbm, energy_ref, buf, sems):
    odd = info_ref[6] == 2

    @pl.when(odd)
    def _():
        finish_rows(cut, info_ref, (own0_ref, own1_ref), c_ref, sigma_hbm, buf, sems.at[0])

    energy_ref[0] = jnp.sum(energies_ref[:, :1])

    @pl.when(odd)
    def _():
        for copy in finish_copies(cut, c_ref.shape[0], sigma_hbm, buf, sems.at[0]):
            copy.wait()


def finish(kernel, name, args, sigma, energy, count):
    rows, cols = 2 * args[2].shape[0], args[2].shape[1]
    in_specs = [SMEM] + [WHOLE] * (len(args) - 1)
    aliases = {}
    if sigma is not None:
        in_specs.append(ANY)
        aliases = {len(args): 0}
        args = [*args, sigma]
    return pl.pallas_call(
        kernel,
        out_shape=(jax.ShapeDtypeStruct((1, rows, cols), jnp.bfloat16), energy),
        in_specs=in_specs,
        out_specs=(ANY, SMEM if energy.shape == (1,) else WHOLE),
        scratch_shapes=[
            pltpu.VMEM((count, cols), jnp.bfloat16),
            pltpu.SemaphoreType.DMA((2, rows // PIECE)),
        ],
        input_output_aliases=aliases,
        compiler_params=params(),
        cost_estimate=SMALL,
        name=name,
    )(*args)


def on_device(psi, left_env, right_env, row_sizes, col_sizes):
    sectors = lax.axis_size("sec")
    sector = lax.axis_index("sec")
    even = sector % 2 == 0
    place = sector % 4

    def send(value, *hops):
        pairs = [
            (s, s + steps)
            for at, steps in hops
            for s in range(at, sectors, 4)
            if 0 <= s + steps < sectors
        ]
        return lax.ppermute(value, "sec", pairs)

    rows = psi.shape[1]
    part = rows // 2
    cut = rows * 5 // 8
    which = jnp.where(place == 0, 1, jnp.where(place == 2, 0, 2))
    orders = [jnp.where(even, 2, 1), jnp.where(even, 3, 2), jnp.where(even, 1, 3), 0]
    info = jnp.stack([*orders, row_sizes[0], col_sizes[0], which]).astype(jnp.int32)

    pairs_up = [(s, s + 1) for s in range(1, sectors, 4) if s + 1 < sectors]
    pairs_up += [(s, s - 3) for s in range(3, sectors, 4) if s + 1 < sectors]

    def raise_one(value):
        return lax.ppermute(value, "sec", pairs_up)

    def up_chip(value):
        return send(value, (0, 1), (2, 1))

    def along(value):
        return send(value, (3, 3), (0, -3))

    def across(value):
        return send(value, (1, 2), (2, -1))

    def swap(value):
        return send(value, (0, 1), (1, -1), (2, 1), (3, -1))

    def relay(value):
        return send(value, (0, 4))

    envs = (left_env, right_env)
    first0, token, live, wide, *ops0 = opening_rows(info, psi[0], envs, 0, part, cut=cut)
    paired0 = up_chip(first0)
    seen = send(wide, (3, -2), (1, 1))
    first1, token = term_rows(info, live, ops0, part, part, token)
    paired1 = up_chip(first1)
    both0, token = add(first0, paired0, token)
    raised0 = raise_one(both0)
    second0, token, *ops1 = opening_rows(info, live, envs, 1, cut, token, seen)
    moved0 = along(second0)
    both1, token = add(first1, paired1, token)
    raised1 = raise_one(both1)
    second1, token, *ops2 = term_rows(
        info, live, ops1, cut, rows - cut, token, bring=(2, *envs)
    )
    moved1 = along(second1)
    third0, token, *ops3 = term_rows(info, live, ops2, 0, part, token, bring=(3, *envs))
    swapped0 = swap(third0)
    raised0, token = hold(raised0, token)
    relayed0 = relay(raised0)
    third1, token = term_rows(info, live, ops2, part, part, token)
    swapped1 = swap(third1)
    summed0, token = add(second0, moved0, token)
    crossed0 = across(summed0)
    raised1, token = hold(raised1, token)
    relayed1 = relay(raised1)
    own0, token = term_rows(info, live, ops3, 0, part, token, added=(swapped0,))
    token = touch(relayed0, token)
    summed1, sent, token = add_energy(second1, moved1, seen, token)
    crossed1 = across(summed1)
    own1, token = term_rows(info, live, ops3, part, part, token, added=(swapped1,))

    whole = jax.ShapeDtypeStruct((sectors, 128), jnp.float32)
    single = jax.ShapeDtypeStruct((1,), jnp.float32)
    sigma, energy = finish(
        functools.partial(middle_kernel, cut),
        "finish_middle",
        [info, own0, own1, live, raised0, raised1, relayed0, relayed1, crossed0, sent],
        None,
        whole,
        rows,
    )
    energies = lax.all_to_all(energy, "sec", 0, 0, tiled=True)
    return finish(
        functools.partial(last_kernel, cut),
        "finish_last",
        [info, own0, own1, crossed1, energies],
        sigma,
        single,
        rows - cut,
    )


def solution(mesh):
    return jax.shard_map(
        on_device,
        mesh=mesh,
        in_specs=(
            P(("grp", "sec"), None, None),
            P(("grp", "sec"), None, None, None),
            P(("grp", "sec"), None, None, None),
            P(("grp", "sec")),
            P(("grp", "sec")),
        ),
        out_specs=(P(("grp", "sec"), None, None), P("grp")),
        check_vma=False,
    )
```

```python
import functools

import jax
import jax.numpy as jnp
from jax import lax
from jax.experimental import pallas as pl
from jax.experimental.pallas import tpu as pltpu
from jax.sharding import PartitionSpec as P

MIB = 1024 * 1024
LEFT_PIECES, RIGHT_PIECES = 8, 2
FIRST_MIB = 44
BRING_MIB = 42

ANY = pl.BlockSpec(memory_space=pl.ANY)
HBM = pl.BlockSpec(memory_space=pltpu.HBM)
SMEM = pl.BlockSpec(memory_space=pltpu.SMEM)
WHOLE = pl.BlockSpec(memory_space=pltpu.VMEM)
TOKEN = jax.ShapeDtypeStruct((8, 128), jnp.float32)
SMALL = pl.CostEstimate(flops=200000000, bytes_accessed=1000000, transcendentals=0)


def params(mib=8):
    return pltpu.CompilerParams(vmem_limit_bytes=mib * MIB)


def fetch(info_ref, slot, count, left_hbm, right_hbm, left_ref, right_ref, sems):
    term = info_ref[slot]
    rows, cols = left_ref.shape[0], right_ref.shape[0]
    step = rows // LEFT_PIECES
    left, right = [], []
    for i in range(LEFT_PIECES):
        span = pl.ds(i * step, step)
        left.append(
            pltpu.make_async_copy(left_hbm.at[0, term, span, :], left_ref.at[span, :], sems.at[i])
        )
    step = cols // RIGHT_PIECES
    for i in range(RIGHT_PIECES):
        span = pl.ds(i * step, step)
        right.append(
            pltpu.make_async_copy(
                right_hbm.at[0, term, span, :], right_ref.at[span, :], sems.at[LEFT_PIECES + i]
            )
        )
    first = -(-count * LEFT_PIECES // rows)
    return left[:first] + right, left[first:]


def multiply(left, live, right):
    first = jnp.dot(left, live, preferred_element_type=jnp.float32).astype(jnp.bfloat16)
    return jnp.dot(first, right, preferred_element_type=jnp.float32)


def opening_kernel(slot, masks, tokens, info_ref, live_ref, left_hbm, right_hbm, *refs):
    refs = list(refs[tokens:])
    out_ref, _ = refs[:2]
    sems = refs[-1]
    operands = refs[2:-1]
    psi_ref = live_ref
    if masks:
        live_ref = operands.pop(0)
    own, late = fetch(info_ref, slot, out_ref.shape[0], left_hbm, right_hbm, *operands[:2], sems.at[0])
    for copy in own:
        copy.start()
    if len(operands) > 2:
        later = fetch(info_ref, slot + 1, 0, left_hbm, right_hbm, *operands[2:], sems.at[1])
        late = late + later[0] + later[1]
    if masks:
        rows, cols = psi_ref.shape
        step = 128
        col = lax.broadcasted_iota(jnp.int32, (step, cols), 1) < info_ref[5]
        row = lax.broadcasted_iota(jnp.int32, (step, cols), 0)
        for start in range(0, rows, step):
            span = pl.ds(start, step)
            inside = jnp.logical_and(row < info_ref[4] - start, col)
            values = jnp.where(inside, psi_ref[span, :].astype(jnp.float32), 0.0)
            live_ref[span, :] = values.astype(live_ref.dtype)
    for copy in own:
        copy.wait()
    for copy in late:
        copy.start()
    out_ref[...] = multiply(operands[0][: out_ref.shape[0], :], live_ref[...], operands[1][...])
    for copy in late:
        copy.wait()


def operand_shapes(width, cols):
    return [
        jax.ShapeDtypeStruct((width, width), jnp.bfloat16),
        jax.ShapeDtypeStruct((cols, cols), jnp.bfloat16),
    ]


def opening_rows(info, live, envs, slot, count, *tokens, masks=False):
    width, cols = live.shape
    out_shape = [jax.ShapeDtypeStruct((count, cols), jnp.float32), TOKEN]
    if masks:
        out_shape.append(jax.ShapeDtypeStruct(live.shape, live.dtype))
    out_shape += operand_shapes(width, cols) * 2
    return pl.pallas_call(
        functools.partial(opening_kernel, slot, masks, len(tokens)),
        out_shape=out_shape,
        in_specs=[SMEM, WHOLE, HBM, HBM] + [ANY] * len(tokens),
        out_specs=[WHOLE, ANY] + [WHOLE] * (len(out_shape) - 2),
        scratch_shapes=[pltpu.SemaphoreType.DMA((2, LEFT_PIECES + RIGHT_PIECES))],
        compiler_params=params(FIRST_MIB if masks else BRING_MIB),
        cost_estimate=SMALL,
        name="opening_rows",
    )(info, live, *envs, *tokens)


def term_kernel(first, adds, slot, tokens, info_ref, live_ref, left_ref, right_ref, *refs):
    refs = list(refs)
    add_refs = [refs.pop(0), refs.pop(0)] if adds else None
    copies = []
    if slot is not None:
        left_hbm, right_hbm = refs[:2]
        sems = refs[-1]
        out_ref, _, left_next, right_next = refs[2 + tokens : -1]
        copies = sum(fetch(info_ref, slot, 0, left_hbm, right_hbm, left_next, right_next, sems), [])
        for copy in copies:
            copy.start()
    else:
        out_ref, _ = refs[tokens:]
    count = out_ref.shape[0]
    block = count
    for i in range(count // block):
        span = pl.ds(i * block, block)
        value = multiply(left_ref[pl.ds(first + i * block, block), :], live_ref[...], right_ref[...])
        if adds:
            odd = info_ref[7] == 1
            value = value + jnp.where(odd, add_refs[1][span, :], add_refs[0][span, :])
        out_ref[span, :] = value
    for copy in copies:
        copy.wait()


def term_rows(info, live, operands, first, count, *tokens, added=None, bring=None):
    width, cols = live.shape
    in_specs = [SMEM, WHOLE, WHOLE, WHOLE]
    args = [info, live, *operands]
    out_shape = [jax.ShapeDtypeStruct((count, cols), jnp.float32), TOKEN]
    out_specs = [WHOLE, ANY]
    scratch = []
    slot = None
    if added is not None:
        in_specs += [WHOLE, WHOLE]
        args += added
    if bring is not None:
        slot = bring[0]
        in_specs += [HBM, HBM]
        args += bring[1:]
        out_shape += operand_shapes(width, cols)
        out_specs += [WHOLE, WHOLE]
        scratch.append(pltpu.SemaphoreType.DMA((LEFT_PIECES + RIGHT_PIECES,)))
    return pl.pallas_call(
        functools.partial(term_kernel, first, added is not None, slot, len(tokens)),
        out_shape=out_shape,
        in_specs=in_specs + [ANY] * len(tokens),
        out_specs=out_specs,
        scratch_shapes=scratch,
        compiler_params=params(12 if slot is None else BRING_MIB),
        cost_estimate=SMALL,
        name="term_rows",
    )(*args, *tokens)


def add_kernel(odd_only, info_ref, a_ref, b_ref, *refs):
    out_ref = refs[-2]
    step = 64

    def sums(i, _):
        span = pl.ds(pl.multiple_of(i * step, step), step)
        out_ref[span, :] = a_ref[span, :] + b_ref[span, :]
        return _

    def copies(i, _):
        span = pl.ds(pl.multiple_of(i * step, step), step)
        out_ref[span, :] = a_ref[span, :]
        return _

    count = a_ref.shape[0] // step
    if odd_only:
        odd = info_ref[7] == 1
        pl.when(odd)(lambda: lax.fori_loop(0, count, sums, None))
        pl.when(jnp.logical_not(odd))(lambda: lax.fori_loop(0, count, copies, None))
    else:
        lax.fori_loop(0, count, sums, None)


def add(info, a, b, token, odd_only=False):
    return pl.pallas_call(
        functools.partial(add_kernel, odd_only),
        out_shape=(jax.ShapeDtypeStruct(a.shape, a.dtype), TOKEN),
        in_specs=[SMEM, WHOLE, WHOLE, ANY],
        out_specs=(WHOLE, ANY),
        compiler_params=params(),
        cost_estimate=SMALL,
        name="add_blocks",
    )(info, a, b, token)


def touch(*values):
    return pl.pallas_call(
        lambda *refs: None,
        out_shape=TOKEN,
        in_specs=[ANY] * len(values),
        out_specs=ANY,
        compiler_params=params(),
        cost_estimate=SMALL,
        name="touch",
    )(*values)


def hold(value, token):
    return pl.pallas_call(
        lambda *refs: None,
        out_shape=(jax.ShapeDtypeStruct(value.shape, value.dtype), TOKEN),
        in_specs=[ANY, ANY],
        out_specs=(ANY, ANY),
        input_output_aliases={0: 0},
        compiler_params=params(),
        cost_estimate=SMALL,
        name="hold",
    )(value, token)


def finish_kernel(first, info_ref, live_ref, own_ref, a_ref, b_ref, c_ref, before_ref, *refs):
    sigma_hbm, energy_ref, sigma_buf, sems = refs[-4:]
    count, cols = own_ref.shape
    step = 64
    piece = 64
    col = lax.broadcasted_iota(jnp.int32, (step, cols), 1) < info_ref[5]
    row = lax.broadcasted_iota(jnp.int32, (step, cols), 0)

    def copy(i):
        span = pl.ds(i * piece, piece)
        return pltpu.make_async_copy(
            sigma_buf.at[span, :], sigma_hbm.at[0, pl.ds(first + i * piece, piece), :], sems.at[i]
        )

    def work(arrival):
        energy = jnp.zeros((8, cols), jnp.float32)
        for i in range(count // piece):

            def body(n, energy):
                start = pl.multiple_of(i * piece + n * step, step)
                span = pl.ds(start, step)
                inside = jnp.logical_and(row < info_ref[4] - first - start, col)
                total = jnp.where(inside, own_ref[span, :] + arrival[span, :], 0.0)
                sigma_buf[span, :] = total.astype(sigma_buf.dtype)
                here = pl.ds(pl.multiple_of(first + start, step), step)
                product = live_ref[here, :].astype(jnp.float32) * total
                return energy + jnp.sum(jnp.reshape(product, (step // 8, 8, cols)), axis=0)

            energy = lax.fori_loop(0, piece // step, body, energy)
            copy(i).start()
        energy_ref[...] = before_ref[...] + jnp.sum(energy)

    for n, arrival in enumerate((a_ref, b_ref, c_ref)):
        pl.when(info_ref[6] == n)(functools.partial(work, arrival))
    for i in range(count // piece):
        copy(i).wait()


def finish(info, live, own, arrivals, before, sigma, first):
    count, cols = own.shape
    in_specs = [SMEM] + [WHOLE] * 6
    operands = [info, live, own, *arrivals, before]
    aliases = {}
    if sigma is not None:
        in_specs.append(ANY)
        aliases = {len(operands): 0}
        operands.append(sigma)
    return pl.pallas_call(
        functools.partial(finish_kernel, first),
        out_shape=(
            jax.ShapeDtypeStruct((1, *live.shape), jnp.bfloat16),
            jax.ShapeDtypeStruct(before.shape, jnp.float32),
        ),
        in_specs=in_specs,
        out_specs=(ANY, WHOLE),
        scratch_shapes=[pltpu.VMEM((count, cols), jnp.bfloat16), pltpu.SemaphoreType.DMA((count // 64,))],
        input_output_aliases=aliases,
        compiler_params=params(),
        cost_estimate=SMALL,
        name="finish_rows",
    )(*operands)


def sum_kernel(in_ref, out_ref):
    out_ref[0] = jnp.sum(in_ref[:, :1])


def sum_over_sectors(value):
    arrived = lax.all_to_all(value, "sec", 0, 0, tiled=True)
    return pl.pallas_call(
        sum_kernel,
        out_shape=jax.ShapeDtypeStruct((1,), jnp.float32),
        in_specs=[WHOLE],
        out_specs=SMEM,
        compiler_params=params(),
        cost_estimate=SMALL,
        name="sum_energy",
    )(arrived)


def on_device(psi, left_env, right_env, row_sizes, col_sizes):
    sectors = lax.axis_size("sec")
    sector = lax.axis_index("sec")
    even = sector % 2 == 0
    place = sector % 4

    def send(value, *hops):
        pairs = [
            (s, s + steps)
            for at, steps in hops
            for s in range(at, sectors, 4)
            if 0 <= s + steps < sectors
        ]
        return lax.ppermute(value, "sec", pairs)

    rows = psi.shape[1]
    part = rows * 5 // 8
    rest = rows - part
    which = jnp.where(place == 0, 1, jnp.where(place == 2, 0, 2))
    slots = [jnp.where(even, 2, 3), 1, jnp.where(even, 3, 2), 0]
    info = jnp.stack([*slots, row_sizes[0], col_sizes[0], which, sector % 2]).astype(jnp.int32)
    up = [(s, s + 1) for s in range(1, sectors, 4) if s + 1 < sectors]
    up += [(s, s - 3) for s in range(3, sectors, 4) if s + 1 < sectors]
    up += [(s, s + 1) for s in range(0, sectors, 2)]

    def swap(value):
        return send(value, (0, 1), (1, -1), (2, 1), (3, -1))

    def raise_one(value):
        return lax.ppermute(value, "sec", up)

    def along(value):
        return send(value, (3, 3), (0, -3))

    def across(value):
        return send(value, (1, 2), (2, -1))

    def relay(value):
        return send(value, (0, 4))

    envs = (left_env, right_env)
    first0, token, live, *ops = opening_rows(info, psi[0], envs, 0, part, masks=True)
    ops0, ops1 = ops[:2], ops[2:]
    swapped0 = swap(first0)
    second0, token, *ops2 = term_rows(info, live, ops1, 0, part, token, bring=(2, *envs))
    both0, token = add(info, second0, swapped0, token, odd_only=True)
    raised0 = raise_one(both0)
    third0, token, *ops3 = term_rows(info, live, ops2, 0, part, token, bring=(3, *envs))
    moved0 = along(third0)
    third1, token = term_rows(info, live, ops2, part, rest, token)
    moved1 = along(third1)
    first1, token = term_rows(info, live, ops0, part, rest, token)
    swapped1 = swap(first1)
    second1, token = term_rows(info, live, ops1, part, rest, token)
    both1, token = add(info, second1, swapped1, token, odd_only=True)
    raised1 = raise_one(both1)
    raised0, token = hold(raised0, token)
    relayed0 = relay(raised0)
    summed0, token = add(info, third0, moved0, token)
    crossed0 = across(summed0)
    raised1, token = hold(raised1, token)
    relayed1 = relay(raised1)
    summed1, token = add(info, third1, moved1, token)
    crossed1 = across(summed1)
    own0, token = term_rows(info, live, ops3, 0, part, token, added=(swapped0, raised0))
    energy = jnp.zeros((sectors, 128), jnp.float32)
    sigma, energy = finish(info, live, own0, (raised0, relayed0, crossed0), energy, None, 0)
    token = energy
    own1, token = term_rows(info, live, ops3, part, rest, token, added=(swapped1, raised1))
    sigma, energy = finish(info, live, own1, (raised1, relayed1, crossed1), energy, sigma, part)
    return sigma, sum_over_sectors(energy)


def solution(mesh):
    return jax.shard_map(
        on_device,
        mesh=mesh,
        in_specs=(
            P(("grp", "sec"), None, None),
            P(("grp", "sec"), None, None, None),
            P(("grp", "sec"), None, None, None),
            P(("grp", "sec")),
            P(("grp", "sec")),
        ),
        out_specs=(P(("grp", "sec"), None, None), P("grp")),
        check_vma=False,
    )
```

```python
import functools

import jax
import jax.numpy as jnp
from jax import lax
from jax.experimental import pallas as pl
from jax.experimental.pallas import tpu as pltpu
from jax.sharding import PartitionSpec as P

MIB = 1024 * 1024
PIECE = 128
FIRST_MIB = 48
BRING_MIB = 44

ANY = pl.BlockSpec(memory_space=pl.ANY)
HBM = pl.BlockSpec(memory_space=pltpu.HBM)
SMEM = pl.BlockSpec(memory_space=pltpu.SMEM)
WHOLE = pl.BlockSpec(memory_space=pltpu.VMEM)
TOKEN = jax.ShapeDtypeStruct((8, 128), jnp.float32)
SMALL = pl.CostEstimate(flops=200000000, bytes_accessed=1000000, transcendentals=0)


def params(mib=8):
    return pltpu.CompilerParams(vmem_limit_bytes=mib * MIB)


def fetch(info_ref, bring, left_hbm, right_hbm, left_ref, right_ref, sems):
    slot, first, count, _ = bring
    term = info_ref[slot]
    copies = []
    for i in range(count // PIECE):
        there = left_hbm.at[0, term, pl.ds(first + i * PIECE, PIECE), :]
        here = left_ref.at[pl.ds(i * PIECE, PIECE), :]
        copies.append(pltpu.make_async_copy(there, here, sems.at[len(copies)]))
    if right_ref is not None:
        for i in range(right_ref.shape[0] // (2 * PIECE)):
            span = pl.ds(i * 2 * PIECE, 2 * PIECE)
            there = right_hbm.at[0, term, span, :]
            copies.append(
                pltpu.make_async_copy(there, right_ref.at[span, :], sems.at[len(copies)])
            )
    return copies


def operand_shapes(width, cols, brings):
    shapes = []
    for _, _, count, with_right in brings:
        shapes.append(jax.ShapeDtypeStruct((count, width), jnp.bfloat16))
        if with_right:
            shapes.append(jax.ShapeDtypeStruct((cols, cols), jnp.bfloat16))
    return shapes


def fetch_all(info_ref, brings, left_hbm, right_hbm, refs, sems):
    copies = []
    for i, bring in enumerate(brings):
        left_ref = refs.pop(0)
        right_ref = refs.pop(0) if bring[3] else None
        copies += fetch(info_ref, bring, left_hbm, right_hbm, left_ref, right_ref, sems.at[i])
    return copies


def first_kernel(count, brings, info_ref, psi_ref, left_hbm, right_hbm, *refs):
    out_ref, _, live_ref, right_ref = refs[:4]
    left_ref, sems, own_sems = refs[-3:]
    own = fetch(info_ref, (0, 0, count, True), left_hbm, right_hbm, left_ref, right_ref, own_sems)
    copies = fetch_all(info_ref, brings, left_hbm, right_hbm, list(refs[4:-3]), sems)
    for copy in own:
        copy.start()
    rows, cols = psi_ref.shape
    step = 128
    col = lax.broadcasted_iota(jnp.int32, (step, cols), 1) < info_ref[5]
    row = lax.broadcasted_iota(jnp.int32, (step, cols), 0)
    for start in range(0, rows, step):
        span = pl.ds(start, step)
        inside = jnp.logical_and(row < info_ref[4] - start, col)
        values = jnp.where(inside, psi_ref[span, :].astype(jnp.float32), 0.0)
        live_ref[span, :] = values.astype(live_ref.dtype)
    for copy in own:
        copy.wait()
    for copy in copies:
        copy.start()
    out_ref[...] = multiply(left_ref[...], live_ref[...], right_ref[...])
    for copy in copies:
        copy.wait()


def first_rows(info, psi, envs, count, brings):
    rows, cols = psi.shape
    out_shape = [jax.ShapeDtypeStruct((count, cols), jnp.float32), TOKEN]
    out_shape.append(jax.ShapeDtypeStruct(psi.shape, psi.dtype))
    out_shape.append(jax.ShapeDtypeStruct((cols, cols), jnp.bfloat16))
    out_shape += operand_shapes(rows, cols, brings)
    return pl.pallas_call(
        functools.partial(first_kernel, count, brings),
        out_shape=out_shape,
        in_specs=[SMEM, WHOLE, HBM, HBM],
        out_specs=[WHOLE, ANY] + [WHOLE] * (len(out_shape) - 2),
        scratch_shapes=[
            pltpu.VMEM((count, rows), jnp.bfloat16),
            pltpu.SemaphoreType.DMA((len(brings), 16)),
            pltpu.SemaphoreType.DMA((16,)),
        ],
        compiler_params=params(FIRST_MIB),
        cost_estimate=SMALL,
        name="first_rows",
    )(info, psi, *envs)


def multiply(left, live, right):
    first = jnp.dot(left, live, preferred_element_type=jnp.float32).astype(jnp.bfloat16)
    return jnp.dot(first, right, preferred_element_type=jnp.float32)


def term_kernel(adds, brings, tokens, info_ref, live_ref, left_ref, right_ref, *refs):
    refs = list(refs)
    add_refs = [refs.pop(0), refs.pop(0)] if adds else None
    copies = []
    if brings:
        left_hbm, right_hbm = refs[:2]
        refs = refs[2:]
        sems = refs.pop()
    out_ref = refs[tokens]
    if brings:
        copies = fetch_all(info_ref, brings, left_hbm, right_hbm, refs[tokens + 2 :], sems)
        for copy in copies:
            copy.start()
    value = multiply(left_ref[...], live_ref[...], right_ref[...])
    if adds:
        odd = info_ref[7] == 1
        value = value + jnp.where(odd, add_refs[1][...], add_refs[0][...])
    out_ref[...] = value
    for copy in copies:
        copy.wait()


def term_rows(info, live, envs, left, right, *tokens, added=None, brings=()):
    width, cols = live.shape
    in_specs = [SMEM, WHOLE, WHOLE, WHOLE]
    args = [info, live, left, right]
    out_shape = [jax.ShapeDtypeStruct((left.shape[0], cols), jnp.float32), TOKEN]
    scratch = []
    if added is not None:
        in_specs += [WHOLE, WHOLE]
        args += added
    if brings:
        in_specs += [HBM, HBM]
        args += envs
        out_shape += operand_shapes(width, cols, brings)
        scratch.append(pltpu.SemaphoreType.DMA((len(brings), 16)))
    return pl.pallas_call(
        functools.partial(term_kernel, added is not None, brings, len(tokens)),
        out_shape=out_shape,
        in_specs=in_specs + [ANY] * len(tokens),
        out_specs=[WHOLE, ANY] + [WHOLE] * (len(out_shape) - 2),
        scratch_shapes=scratch,
        compiler_params=params(BRING_MIB if brings else 12),
        cost_estimate=SMALL,
        name="term_rows",
    )(*args, *tokens)


def add_kernel(odd_only, info_ref, a_ref, b_ref, *refs):
    out_ref = refs[-2]
    step = 64

    def sums(i, _):
        span = pl.ds(pl.multiple_of(i * step, step), step)
        out_ref[span, :] = a_ref[span, :] + b_ref[span, :]
        return _

    def copies(i, _):
        span = pl.ds(pl.multiple_of(i * step, step), step)
        out_ref[span, :] = a_ref[span, :]
        return _

    count = a_ref.shape[0] // step
    if odd_only:
        odd = info_ref[7] == 1
        pl.when(odd)(lambda: lax.fori_loop(0, count, sums, None))
        pl.when(jnp.logical_not(odd))(lambda: lax.fori_loop(0, count, copies, None))
    else:
        lax.fori_loop(0, count, sums, None)


def add(info, a, b, token, odd_only=False):
    return pl.pallas_call(
        functools.partial(add_kernel, odd_only),
        out_shape=(jax.ShapeDtypeStruct(a.shape, a.dtype), TOKEN),
        in_specs=[SMEM, WHOLE, WHOLE, ANY],
        out_specs=(WHOLE, ANY),
        compiler_params=params(),
        cost_estimate=SMALL,
        name="add_blocks",
    )(info, a, b, token)


def touch(*values):
    return pl.pallas_call(
        lambda *refs: None,
        out_shape=TOKEN,
        in_specs=[ANY] * len(values),
        out_specs=ANY,
        compiler_params=params(),
        cost_estimate=SMALL,
        name="touch",
    )(*values)


def hold(value, token):
    return pl.pallas_call(
        lambda *refs: None,
        out_shape=(jax.ShapeDtypeStruct(value.shape, value.dtype), TOKEN),
        in_specs=[ANY, ANY],
        out_specs=(ANY, ANY),
        input_output_aliases={0: 0},
        compiler_params=params(),
        cost_estimate=SMALL,
        name="hold",
    )(value, token)


def finish_kernel(first, info_ref, live_ref, own_ref, a_ref, b_ref, c_ref, before_ref, *refs):
    sigma_hbm, energy_ref, sigma_buf, sems = refs[-4:]
    count, cols = own_ref.shape
    step = 64
    piece = PIECE
    col = lax.broadcasted_iota(jnp.int32, (step, cols), 1) < info_ref[5]
    row = lax.broadcasted_iota(jnp.int32, (step, cols), 0)

    def copy(i):
        span = pl.ds(i * piece, piece)
        return pltpu.make_async_copy(
            sigma_buf.at[span, :], sigma_hbm.at[0, pl.ds(first + i * piece, piece), :], sems.at[i]
        )

    def work(arrival):
        energy = jnp.zeros((8, cols), jnp.float32)
        for i in range(count // piece):

            def body(n, energy):
                start = pl.multiple_of(i * piece + n * step, step)
                span = pl.ds(start, step)
                inside = jnp.logical_and(row < info_ref[4] - first - start, col)
                total = jnp.where(inside, own_ref[span, :] + arrival[span, :], 0.0)
                sigma_buf[span, :] = total.astype(sigma_buf.dtype)
                here = pl.ds(pl.multiple_of(first + start, step), step)
                product = live_ref[here, :].astype(jnp.float32) * total
                return energy + jnp.sum(jnp.reshape(product, (step // 8, 8, cols)), axis=0)

            energy = lax.fori_loop(0, piece // step, body, energy)
            copy(i).start()
        energy_ref[...] = before_ref[...] + jnp.sum(energy)

    for n, arrival in enumerate((a_ref, b_ref, c_ref)):
        pl.when(info_ref[6] == n)(functools.partial(work, arrival))
    for i in range(count // piece):
        copy(i).wait()


def finish(info, live, own, arrivals, before, sigma, first):
    count, cols = own.shape
    in_specs = [SMEM] + [WHOLE] * 6
    operands = [info, live, own, *arrivals, before]
    aliases = {}
    if sigma is not None:
        in_specs.append(ANY)
        aliases = {len(operands): 0}
        operands.append(sigma)
    return pl.pallas_call(
        functools.partial(finish_kernel, first),
        out_shape=(
            jax.ShapeDtypeStruct((1, *live.shape), jnp.bfloat16),
            jax.ShapeDtypeStruct(before.shape, jnp.float32),
        ),
        in_specs=in_specs,
        out_specs=(ANY, WHOLE),
        scratch_shapes=[pltpu.VMEM((count, cols), jnp.bfloat16), pltpu.SemaphoreType.DMA((count // PIECE,))],
        input_output_aliases=aliases,
        compiler_params=params(),
        cost_estimate=SMALL,
        name="finish_rows",
    )(*operands)


def sum_kernel(in_ref, out_ref):
    out_ref[0] = jnp.sum(in_ref[:, :1])


def sum_over_sectors(value):
    arrived = lax.all_to_all(value, "sec", 0, 0, tiled=True)
    return pl.pallas_call(
        sum_kernel,
        out_shape=jax.ShapeDtypeStruct((1,), jnp.float32),
        in_specs=[WHOLE],
        out_specs=SMEM,
        compiler_params=params(),
        cost_estimate=SMALL,
        name="sum_energy",
    )(arrived)


def on_device(psi, left_env, right_env, row_sizes, col_sizes):
    sectors = lax.axis_size("sec")
    sector = lax.axis_index("sec")
    even = sector % 2 == 0
    place = sector % 4

    def send(value, *hops):
        pairs = [
            (s, s + steps)
            for at, steps in hops
            for s in range(at, sectors, 4)
            if 0 <= s + steps < sectors
        ]
        return lax.ppermute(value, "sec", pairs)

    rows = psi.shape[1]
    part = rows * 5 // 8
    rest = rows - part
    which = jnp.where(place == 0, 1, jnp.where(place == 2, 0, 2))
    slots = [jnp.where(even, 2, 3), 1, jnp.where(even, 3, 2), 0]
    info = jnp.stack([*slots, row_sizes[0], col_sizes[0], which, sector % 2]).astype(jnp.int32)
    up = [(s, s + 1) for s in range(1, sectors, 4) if s + 1 < sectors]
    up += [(s, s - 3) for s in range(3, sectors, 4) if s + 1 < sectors]
    up += [(s, s + 1) for s in range(0, sectors, 2)]

    def swap(value):
        return send(value, (0, 1), (1, -1), (2, 1), (3, -1))

    def raise_one(value):
        return lax.ppermute(value, "sec", up)

    def along(value):
        return send(value, (3, 3), (0, -3))

    def across(value):
        return send(value, (1, 2), (2, -1))

    def relay(value):
        return send(value, (0, 4))

    envs = (left_env, right_env)

    def term(left, right, *tokens, **more):
        return term_rows(info, live, envs, left, right, *tokens, **more)

    first0, token, live, right0, left, right1 = first_rows(
        info, psi[0], envs, part, ((1, 0, part, True),)
    )
    swapped0 = swap(first0)
    second0, token, left, right2 = term(left, right1, token, brings=((2, 0, part, True),))
    both0, token = add(info, second0, swapped0, token, odd_only=True)
    raised0 = raise_one(both0)
    third0, token, left, left1 = term(
        left, right2, token, brings=((2, part, rest, False), (1, part, rest, False))
    )
    moved0 = along(third0)
    third1, token, left = term(left, right2, token, brings=((0, part, rest, False),))
    moved1 = along(third1)
    first1, token, left3, right3 = term(left, right0, token, brings=((3, 0, part, True),))
    swapped1 = swap(first1)
    second1, token, left = term(left1, right1, token, brings=((3, part, rest, False),))
    both1, token = add(info, second1, swapped1, token, odd_only=True)
    raised1 = raise_one(both1)
    raised0, token = hold(raised0, token)
    relayed0 = relay(raised0)
    summed0, token = add(info, third0, moved0, token)
    crossed0 = across(summed0)
    raised1, token = hold(raised1, token)
    relayed1 = relay(raised1)
    summed1, token = add(info, third1, moved1, token)
    crossed1 = across(summed1)
    token = touch(relayed0, token)
    own0, token = term(left3, right3, token, added=(swapped0, raised0))

    energy = jnp.zeros((sectors, 128), jnp.float32)
    sigma, energy = finish(info, live, own0, (raised0, relayed0, crossed0), energy, None, 0)
    own1, token = term(left, right3, token, energy, added=(swapped1, raised1))
    sigma, energy = finish(info, live, own1, (raised1, relayed1, crossed1), energy, sigma, part)
    return sigma, sum_over_sectors(energy)


def solution(mesh):
    return jax.shard_map(
        on_device,
        mesh=mesh,
        in_specs=(
            P(("grp", "sec"), None, None),
            P(("grp", "sec"), None, None, None),
            P(("grp", "sec"), None, None, None),
            P(("grp", "sec")),
            P(("grp", "sec")),
        ),
        out_specs=(P(("grp", "sec"), None, None), P("grp")),
        check_vma=False,
    )
```

```python
import functools

import jax
import jax.numpy as jnp
from jax import lax
from jax.experimental import pallas as pl
from jax.experimental.pallas import tpu as pltpu
from jax.sharding import PartitionSpec as P

MIB = 1024 * 1024
LEFT_PIECES, RIGHT_PIECES = 8, 2
FIRST_MIB = 48
BRING_MIB = 42

ANY = pl.BlockSpec(memory_space=pl.ANY)
HBM = pl.BlockSpec(memory_space=pltpu.HBM)
SMEM = pl.BlockSpec(memory_space=pltpu.SMEM)
WHOLE = pl.BlockSpec(memory_space=pltpu.VMEM)
TOKEN = jax.ShapeDtypeStruct((8, 128), jnp.float32)
SMALL = pl.CostEstimate(flops=200000000, bytes_accessed=1000000, transcendentals=0)


def params(mib=8):
    return pltpu.CompilerParams(vmem_limit_bytes=mib * MIB)


def fetch(info_ref, slot, left_hbm, right_hbm, left_ref, right_ref, sems):
    term = info_ref[slot]
    rows, cols = left_ref.shape[0], right_ref.shape[0]
    step = rows // LEFT_PIECES
    left, right = [], []
    for i in range(LEFT_PIECES):
        span = pl.ds(i * step, step)
        left.append(
            pltpu.make_async_copy(left_hbm.at[0, term, span, :], left_ref.at[span, :], sems.at[i])
        )
    step = cols // RIGHT_PIECES
    for i in range(RIGHT_PIECES):
        span = pl.ds(i * step, step)
        right.append(
            pltpu.make_async_copy(
                right_hbm.at[0, term, span, :], right_ref.at[span, :], sems.at[LEFT_PIECES + i]
            )
        )
    half = LEFT_PIECES // 2
    return left[:half] + right, left[half:]


def multiply(left, live, right):
    first = jnp.dot(left, live, preferred_element_type=jnp.float32).astype(jnp.bfloat16)
    return jnp.dot(first, right, preferred_element_type=jnp.float32)


def opening_kernel(slot, masks, tokens, info_ref, live_ref, left_hbm, right_hbm, *refs):
    refs = list(refs[tokens:])
    out_ref, _ = refs[:2]
    sems = refs[-1]
    operands = refs[2:-1]
    psi_ref = live_ref
    if masks:
        live_ref = operands.pop(0)
    own, late = fetch(info_ref, slot, left_hbm, right_hbm, *operands, sems)
    for copy in own:
        copy.start()
    if masks:
        rows, cols = psi_ref.shape
        step = 128
        col = lax.broadcasted_iota(jnp.int32, (step, cols), 1) < info_ref[5]
        row = lax.broadcasted_iota(jnp.int32, (step, cols), 0)
        for start in range(0, rows, step):
            span = pl.ds(start, step)
            inside = jnp.logical_and(row < info_ref[4] - start, col)
            values = jnp.where(inside, psi_ref[span, :].astype(jnp.float32), 0.0)
            live_ref[span, :] = values.astype(live_ref.dtype)
    for copy in own:
        copy.wait()
    for copy in late:
        copy.start()
    out_ref[...] = multiply(operands[0][: out_ref.shape[0], :], live_ref[...], operands[1][...])
    for copy in late:
        copy.wait()


def operand_shapes(width, cols):
    return [
        jax.ShapeDtypeStruct((width, width), jnp.bfloat16),
        jax.ShapeDtypeStruct((cols, cols), jnp.bfloat16),
    ]


def opening_rows(info, live, envs, slot, count, *tokens, masks=False):
    width, cols = live.shape
    out_shape = [jax.ShapeDtypeStruct((count, cols), jnp.float32), TOKEN]
    if masks:
        out_shape.append(jax.ShapeDtypeStruct(live.shape, live.dtype))
    out_shape += operand_shapes(width, cols)
    return pl.pallas_call(
        functools.partial(opening_kernel, slot, masks, len(tokens)),
        out_shape=out_shape,
        in_specs=[SMEM, WHOLE, HBM, HBM] + [ANY] * len(tokens),
        out_specs=[WHOLE, ANY] + [WHOLE] * (len(out_shape) - 2),
        scratch_shapes=[pltpu.SemaphoreType.DMA((LEFT_PIECES + RIGHT_PIECES,))],
        compiler_params=params(FIRST_MIB if masks else BRING_MIB),
        cost_estimate=SMALL,
        name="opening_rows",
    )(info, live, *envs, *tokens)


def term_kernel(first, adds, slot, tokens, info_ref, live_ref, left_ref, right_ref, *refs):
    refs = list(refs)
    add_ref = refs.pop(0) if adds else None
    copies = []
    if slot is not None:
        left_hbm, right_hbm = refs[:2]
        sems = refs[-1]
        out_ref, _, left_next, right_next = refs[2 + tokens : -1]
        copies = sum(fetch(info_ref, slot, left_hbm, right_hbm, left_next, right_next, sems), [])
        for copy in copies:
            copy.start()
    else:
        out_ref, _ = refs[tokens:]
    count = out_ref.shape[0]
    block = min(count, 512)
    for i in range(count // block):
        span = pl.ds(i * block, block)
        value = multiply(left_ref[pl.ds(first + i * block, block), :], live_ref[...], right_ref[...])
        if adds:
            value = value + add_ref[span, :]
        out_ref[span, :] = value
    for copy in copies:
        copy.wait()


def term_rows(info, live, operands, first, count, *tokens, added=None, bring=None):
    width, cols = live.shape
    in_specs = [SMEM, WHOLE, WHOLE, WHOLE]
    args = [info, live, *operands]
    out_shape = [jax.ShapeDtypeStruct((count, cols), jnp.float32), TOKEN]
    out_specs = [WHOLE, ANY]
    scratch = []
    slot = None
    if added is not None:
        in_specs.append(WHOLE)
        args.append(added)
    if bring is not None:
        slot = bring[0]
        in_specs += [HBM, HBM]
        args += bring[1:]
        out_shape += operand_shapes(width, cols)
        out_specs += [WHOLE, WHOLE]
        scratch.append(pltpu.SemaphoreType.DMA((LEFT_PIECES + RIGHT_PIECES,)))
    return pl.pallas_call(
        functools.partial(term_kernel, first, added is not None, slot, len(tokens)),
        out_shape=out_shape,
        in_specs=in_specs + [ANY] * len(tokens),
        out_specs=out_specs,
        scratch_shapes=scratch,
        compiler_params=params(12 if slot is None else BRING_MIB),
        cost_estimate=SMALL,
        name="term_rows",
    )(*args, *tokens)


def add_kernel(a_ref, b_ref, *refs):
    out_ref = refs[-2]
    rows = a_ref.shape[0]
    step = 64

    def body(i, _):
        span = pl.ds(pl.multiple_of(i * step, step), step)
        out_ref[span, :] = a_ref[span, :] + b_ref[span, :]
        return _

    lax.fori_loop(0, rows // step, body, 0)


def add(a, b, *tokens):
    return pl.pallas_call(
        add_kernel,
        out_shape=(jax.ShapeDtypeStruct(a.shape, a.dtype), TOKEN),
        in_specs=[WHOLE, WHOLE] + [ANY] * len(tokens),
        out_specs=(WHOLE, ANY),
        compiler_params=params(),
        cost_estimate=SMALL,
        name="add_blocks",
    )(a, b, *tokens)


def touch(*values):
    return pl.pallas_call(
        lambda *refs: None,
        out_shape=TOKEN,
        in_specs=[ANY] * len(values),
        out_specs=ANY,
        compiler_params=params(),
        cost_estimate=SMALL,
        name="touch",
    )(*values)


def hold(value, token):
    return pl.pallas_call(
        lambda *refs: None,
        out_shape=(jax.ShapeDtypeStruct(value.shape, value.dtype), TOKEN),
        in_specs=[ANY, ANY],
        out_specs=(ANY, ANY),
        input_output_aliases={0: 0},
        compiler_params=params(),
        cost_estimate=SMALL,
        name="hold",
    )(value, token)


def finish_kernel(first, info_ref, live_ref, own_ref, a_ref, b_ref, c_ref, before_ref, *refs):
    sigma_hbm, energy_ref, sigma_buf, sems = refs[-4:]
    count, cols = own_ref.shape
    step = 64
    piece = count // sems.shape[0]
    col = lax.broadcasted_iota(jnp.int32, (step, cols), 1) < info_ref[5]
    row = lax.broadcasted_iota(jnp.int32, (step, cols), 0)

    def copy(i):
        span = pl.ds(i * piece, piece)
        return pltpu.make_async_copy(
            sigma_buf.at[span, :], sigma_hbm.at[0, pl.ds(first + i * piece, piece), :], sems.at[i]
        )

    def work(arrival):
        energy = jnp.zeros((8, cols), jnp.float32)
        for i in range(count // piece):

            def body(n, energy):
                start = pl.multiple_of(i * piece + n * step, step)
                span = pl.ds(start, step)
                inside = jnp.logical_and(row < info_ref[4] - first - start, col)
                total = jnp.where(inside, own_ref[span, :] + arrival[span, :], 0.0)
                sigma_buf[span, :] = total.astype(sigma_buf.dtype)
                here = pl.ds(pl.multiple_of(first + start, step), step)
                product = live_ref[here, :].astype(jnp.float32) * total
                return energy + jnp.sum(jnp.reshape(product, (step // 8, 8, cols)), axis=0)

            energy = lax.fori_loop(0, piece // step, body, energy)
            copy(i).start()
        energy_ref[...] = before_ref[...] + jnp.sum(energy)

    for n, arrival in enumerate((a_ref, b_ref, c_ref)):
        pl.when(info_ref[6] == n)(functools.partial(work, arrival))
    for i in range(count // piece):
        copy(i).wait()


def finish(info, live, own, arrivals, before, sigma, first):
    count, cols = own.shape
    in_specs = [SMEM] + [WHOLE] * 6
    operands = [info, live, own, *arrivals, before]
    aliases = {}
    if sigma is not None:
        in_specs.append(ANY)
        aliases = {len(operands): 0}
        operands.append(sigma)
    return pl.pallas_call(
        functools.partial(finish_kernel, first),
        out_shape=(
            jax.ShapeDtypeStruct((1, *live.shape), jnp.bfloat16),
            jax.ShapeDtypeStruct(before.shape, jnp.float32),
        ),
        in_specs=in_specs,
        out_specs=(ANY, WHOLE),
        scratch_shapes=[pltpu.VMEM((count, cols), jnp.bfloat16), pltpu.SemaphoreType.DMA((4,))],
        input_output_aliases=aliases,
        compiler_params=params(),
        cost_estimate=SMALL,
        name="finish_rows",
    )(*operands)


def sum_kernel(in_ref, out_ref):
    out_ref[0] = jnp.sum(in_ref[:, :1])


def sum_over_sectors(value):
    arrived = lax.all_to_all(value, "sec", 0, 0, tiled=True)
    return pl.pallas_call(
        sum_kernel,
        out_shape=jax.ShapeDtypeStruct((1,), jnp.float32),
        in_specs=[WHOLE],
        out_specs=SMEM,
        compiler_params=params(),
        cost_estimate=SMALL,
        name="sum_energy",
    )(arrived)


def on_device(psi, left_env, right_env, row_sizes, col_sizes):
    sectors = lax.axis_size("sec")
    sector = lax.axis_index("sec")
    even = sector % 2 == 0
    place = sector % 4

    def send(value, *hops):
        pairs = [
            (s, s + steps)
            for at, steps in hops
            for s in range(at, sectors, 4)
            if 0 <= s + steps < sectors
        ]
        return lax.ppermute(value, "sec", pairs)

    rows = psi.shape[1]
    part = rows // 2
    which = jnp.where(place == 0, 1, jnp.where(place == 2, 0, 2))
    orders = [jnp.where(even, 2, 1), jnp.where(even, 3, 2), jnp.where(even, 1, 3), 0]
    info = jnp.stack([*orders, row_sizes[0], col_sizes[0], which]).astype(jnp.int32)

    pairs_up = [(s, s + 1) for s in range(1, sectors, 4) if s + 1 < sectors]
    pairs_up += [(s, s - 3) for s in range(3, sectors, 4) if s + 1 < sectors]

    def raise_one(value):
        return lax.ppermute(value, "sec", pairs_up)

    def along(value):
        return send(value, (3, 3), (0, -3))

    def across(value):
        return send(value, (1, 2), (2, -1))

    def swap(value):
        return send(value, (0, 1), (1, -1), (2, 1), (3, -1))

    def relay(value):
        return send(value, (0, 4))

    envs = (left_env, right_env)
    first0, token, live, *ops0 = opening_rows(info, psi[0], envs, 0, part, masks=True)
    paired0 = swap(first0)
    first1, token = term_rows(info, live, ops0, part, part, token)
    paired1 = swap(first1)
    both0, token = add(first0, paired0, token)
    raised0 = raise_one(both0)
    second0, token, *ops1 = opening_rows(info, live, envs, 1, part, token)
    moved0 = along(second0)
    both1, token = add(first1, paired1, token)
    raised1 = raise_one(both1)
    second1, token, *ops2 = term_rows(info, live, ops1, part, part, token, bring=(2, *envs))
    moved1 = along(second1)
    third0, token, *ops3 = term_rows(info, live, ops2, 0, part, token, bring=(3, *envs))
    swapped0 = swap(third0)
    raised0, token = hold(raised0, token)
    relayed0 = relay(raised0)
    third1, token = term_rows(info, live, ops2, part, part, token)
    swapped1 = swap(third1)
    summed0, token = add(second0, moved0, token)
    crossed0 = across(summed0)
    raised1, token = hold(raised1, token)
    relayed1 = relay(raised1)
    own0, token = term_rows(info, live, ops3, 0, part, token, added=swapped0)
    token = touch(relayed0, token)
    summed1, token = add(second1, moved1, token)
    crossed1 = across(summed1)

    energy = jnp.zeros((sectors, 128), jnp.float32)
    sigma, energy = finish(info, live, own0, (raised0, relayed0, crossed0), energy, None, 0)
    own1, token = term_rows(info, live, ops3, part, part, token, energy, added=swapped1)
    sigma, energy = finish(info, live, own1, (raised1, relayed1, crossed1), energy, sigma, part)
    return sigma, sum_over_sectors(energy)


def solution(mesh):
    return jax.shard_map(
        on_device,
        mesh=mesh,
        in_specs=(
            P(("grp", "sec"), None, None),
            P(("grp", "sec"), None, None, None),
            P(("grp", "sec"), None, None, None),
            P(("grp", "sec")),
            P(("grp", "sec")),
        ),
        out_specs=(P(("grp", "sec"), None, None), P("grp")),
        check_vma=False,
    )
```

```python
import functools

import jax
import jax.numpy as jnp
from jax import lax
from jax.experimental import pallas as pl
from jax.experimental.pallas import tpu as pltpu
from jax.sharding import PartitionSpec as P

MIB = 1024 * 1024
LEFT_PIECES, RIGHT_PIECES = 8, 2
FIRST_MIB = 48
BRING_MIB = 42

ANY = pl.BlockSpec(memory_space=pl.ANY)
HBM = pl.BlockSpec(memory_space=pltpu.HBM)
SMEM = pl.BlockSpec(memory_space=pltpu.SMEM)
WHOLE = pl.BlockSpec(memory_space=pltpu.VMEM)
TOKEN = jax.ShapeDtypeStruct((8, 128), jnp.float32)
SMALL = pl.CostEstimate(flops=200000000, bytes_accessed=1000000, transcendentals=0)


def params(mib=8):
    return pltpu.CompilerParams(vmem_limit_bytes=mib * MIB)


def fetch(info_ref, slot, left_hbm, right_hbm, left_ref, right_ref, sems):
    term = info_ref[slot]
    rows, cols = left_ref.shape[0], right_ref.shape[0]
    step = rows // LEFT_PIECES
    left, right = [], []
    for i in range(LEFT_PIECES):
        span = pl.ds(i * step, step)
        left.append(
            pltpu.make_async_copy(left_hbm.at[0, term, span, :], left_ref.at[span, :], sems.at[i])
        )
    step = cols // RIGHT_PIECES
    for i in range(RIGHT_PIECES):
        span = pl.ds(i * step, step)
        right.append(
            pltpu.make_async_copy(
                right_hbm.at[0, term, span, :], right_ref.at[span, :], sems.at[LEFT_PIECES + i]
            )
        )
    half = LEFT_PIECES // 2
    return left[:half] + right, left[half:]


def multiply(left, live, right):
    first = jnp.dot(left, live, preferred_element_type=jnp.float32).astype(jnp.bfloat16)
    return jnp.dot(first, right, preferred_element_type=jnp.float32)


def opening_kernel(slot, masks, tokens, info_ref, live_ref, left_hbm, right_hbm, *refs):
    refs = list(refs[tokens:])
    out_ref, _ = refs[:2]
    sems = refs[-1]
    operands = refs[2:-1]
    psi_ref = live_ref
    if masks:
        live_ref = operands.pop(0)
    own, late = fetch(info_ref, slot, left_hbm, right_hbm, *operands, sems)
    for copy in own + late:
        copy.start()
    if masks:
        rows, cols = psi_ref.shape
        step = 128
        col = lax.broadcasted_iota(jnp.int32, (step, cols), 1) < info_ref[5]
        row = lax.broadcasted_iota(jnp.int32, (step, cols), 0)
        for start in range(0, rows, step):
            span = pl.ds(start, step)
            inside = jnp.logical_and(row < info_ref[4] - start, col)
            values = jnp.where(inside, psi_ref[span, :].astype(jnp.float32), 0.0)
            live_ref[span, :] = values.astype(live_ref.dtype)
    for copy in own:
        copy.wait()
    out_ref[...] = multiply(operands[0][: out_ref.shape[0], :], live_ref[...], operands[1][...])
    for copy in late:
        copy.wait()


def operand_shapes(width, cols):
    return [
        jax.ShapeDtypeStruct((width, width), jnp.bfloat16),
        jax.ShapeDtypeStruct((cols, cols), jnp.bfloat16),
    ]


def opening_rows(info, live, envs, slot, count, *tokens, masks=False):
    width, cols = live.shape
    out_shape = [jax.ShapeDtypeStruct((count, cols), jnp.float32), TOKEN]
    if masks:
        out_shape.append(jax.ShapeDtypeStruct(live.shape, live.dtype))
    out_shape += operand_shapes(width, cols)
    return pl.pallas_call(
        functools.partial(opening_kernel, slot, masks, len(tokens)),
        out_shape=out_shape,
        in_specs=[SMEM, WHOLE, HBM, HBM] + [ANY] * len(tokens),
        out_specs=[WHOLE, ANY] + [WHOLE] * (len(out_shape) - 2),
        scratch_shapes=[pltpu.SemaphoreType.DMA((LEFT_PIECES + RIGHT_PIECES,))],
        compiler_params=params(FIRST_MIB if masks else BRING_MIB),
        cost_estimate=SMALL,
        name="opening_rows",
    )(info, live, *envs, *tokens)


def term_kernel(first, adds, slot, tokens, info_ref, live_ref, left_ref, right_ref, *refs):
    refs = list(refs)
    add_ref = refs.pop(0) if adds else None
    copies = []
    if slot is not None:
        left_hbm, right_hbm = refs[:2]
        sems = refs[-1]
        out_ref, _, left_next, right_next = refs[2 + tokens : -1]
        copies = sum(fetch(info_ref, slot, left_hbm, right_hbm, left_next, right_next, sems), [])
        for copy in copies:
            copy.start()
    else:
        out_ref, _ = refs[tokens:]
    count = out_ref.shape[0]
    block = min(count, 512)
    for i in range(count // block):
        span = pl.ds(i * block, block)
        value = multiply(left_ref[pl.ds(first + i * block, block), :], live_ref[...], right_ref[...])
        if adds:
            value = value + add_ref[span, :]
        out_ref[span, :] = value
    for copy in copies:
        copy.wait()


def term_rows(info, live, operands, first, count, *tokens, added=None, bring=None):
    width, cols = live.shape
    in_specs = [SMEM, WHOLE, WHOLE, WHOLE]
    args = [info, live, *operands]
    out_shape = [jax.ShapeDtypeStruct((count, cols), jnp.float32), TOKEN]
    out_specs = [WHOLE, ANY]
    scratch = []
    slot = None
    if added is not None:
        in_specs.append(WHOLE)
        args.append(added)
    if bring is not None:
        slot = bring[0]
        in_specs += [HBM, HBM]
        args += bring[1:]
        out_shape += operand_shapes(width, cols)
        out_specs += [WHOLE, WHOLE]
        scratch.append(pltpu.SemaphoreType.DMA((LEFT_PIECES + RIGHT_PIECES,)))
    return pl.pallas_call(
        functools.partial(term_kernel, first, added is not None, slot, len(tokens)),
        out_shape=out_shape,
        in_specs=in_specs + [ANY] * len(tokens),
        out_specs=out_specs,
        scratch_shapes=scratch,
        compiler_params=params(12 if slot is None else BRING_MIB),
        cost_estimate=SMALL,
        name="term_rows",
    )(*args, *tokens)


def add_kernel(a_ref, b_ref, *refs):
    out_ref = refs[-2]
    rows = a_ref.shape[0]
    step = 64

    def body(i, _):
        span = pl.ds(pl.multiple_of(i * step, step), step)
        out_ref[span, :] = a_ref[span, :] + b_ref[span, :]
        return _

    lax.fori_loop(0, rows // step, body, 0)


def add(a, b, *tokens):
    return pl.pallas_call(
        add_kernel,
        out_shape=(jax.ShapeDtypeStruct(a.shape, a.dtype), TOKEN),
        in_specs=[WHOLE, WHOLE] + [ANY] * len(tokens),
        out_specs=(WHOLE, ANY),
        compiler_params=params(),
        cost_estimate=SMALL,
        name="add_blocks",
    )(a, b, *tokens)


def touch(*values):
    return pl.pallas_call(
        lambda *refs: None,
        out_shape=TOKEN,
        in_specs=[ANY] * len(values),
        out_specs=ANY,
        compiler_params=params(),
        cost_estimate=SMALL,
        name="touch",
    )(*values)


def hold(value, token):
    return pl.pallas_call(
        lambda *refs: None,
        out_shape=(jax.ShapeDtypeStruct(value.shape, value.dtype), TOKEN),
        in_specs=[ANY, ANY],
        out_specs=(ANY, ANY),
        input_output_aliases={0: 0},
        compiler_params=params(),
        cost_estimate=SMALL,
        name="hold",
    )(value, token)


def finish_kernel(first, info_ref, live_ref, own_ref, a_ref, b_ref, c_ref, before_ref, *refs):
    sigma_hbm, energy_ref, sigma_buf, sems = refs[-4:]
    count, cols = own_ref.shape
    step = 64
    piece = count // sems.shape[0]
    col = lax.broadcasted_iota(jnp.int32, (step, cols), 1) < info_ref[5]
    row = lax.broadcasted_iota(jnp.int32, (step, cols), 0)

    def copy(i):
        span = pl.ds(i * piece, piece)
        return pltpu.make_async_copy(
            sigma_buf.at[span, :], sigma_hbm.at[0, pl.ds(first + i * piece, piece), :], sems.at[i]
        )

    def work(arrival):
        energy = jnp.zeros((8, cols), jnp.float32)
        for i in range(count // piece):

            def body(n, energy):
                start = pl.multiple_of(i * piece + n * step, step)
                span = pl.ds(start, step)
                inside = jnp.logical_and(row < info_ref[4] - first - start, col)
                total = jnp.where(inside, own_ref[span, :] + arrival[span, :], 0.0)
                sigma_buf[span, :] = total.astype(sigma_buf.dtype)
                here = pl.ds(pl.multiple_of(first + start, step), step)
                product = live_ref[here, :].astype(jnp.float32) * total
                return energy + jnp.sum(jnp.reshape(product, (step // 8, 8, cols)), axis=0)

            energy = lax.fori_loop(0, piece // step, body, energy)
            copy(i).start()
        energy_ref[...] = before_ref[...] + jnp.sum(energy)

    for n, arrival in enumerate((a_ref, b_ref, c_ref)):
        pl.when(info_ref[6] == n)(functools.partial(work, arrival))
    for i in range(count // piece):
        copy(i).wait()


def finish(info, live, own, arrivals, before, sigma, first):
    count, cols = own.shape
    in_specs = [SMEM] + [WHOLE] * 6
    operands = [info, live, own, *arrivals, before]
    aliases = {}
    if sigma is not None:
        in_specs.append(ANY)
        aliases = {len(operands): 0}
        operands.append(sigma)
    return pl.pallas_call(
        functools.partial(finish_kernel, first),
        out_shape=(
            jax.ShapeDtypeStruct((1, *live.shape), jnp.bfloat16),
            jax.ShapeDtypeStruct(before.shape, jnp.float32),
        ),
        in_specs=in_specs,
        out_specs=(ANY, WHOLE),
        scratch_shapes=[pltpu.VMEM((count, cols), jnp.bfloat16), pltpu.SemaphoreType.DMA((4,))],
        input_output_aliases=aliases,
        compiler_params=params(),
        cost_estimate=SMALL,
        name="finish_rows",
    )(*operands)


def pair_kernel(a_ref, b_ref, out_ref):
    out_ref[...] = a_ref[...] + b_ref[...]


def sum_kernel(in_ref, out_ref):
    out_ref[0] = jnp.sum(in_ref[:, :1])


def sum_over_sectors(value, sectors):
    other = lax.ppermute(value, "sec", [(s, s ^ 1) for s in range(sectors)])
    value = pl.pallas_call(
        pair_kernel,
        out_shape=jax.ShapeDtypeStruct(value.shape, value.dtype),
        in_specs=[WHOLE, WHOLE],
        out_specs=WHOLE,
        compiler_params=params(),
        cost_estimate=SMALL,
        name="pair_energy",
    )(value, other)
    groups = [list(range(core, sectors, 2)) for core in range(2)]
    arrived = lax.all_to_all(value, "sec", 0, 0, axis_index_groups=groups, tiled=True)
    return pl.pallas_call(
        sum_kernel,
        out_shape=jax.ShapeDtypeStruct((1,), jnp.float32),
        in_specs=[WHOLE],
        out_specs=SMEM,
        compiler_params=params(),
        cost_estimate=SMALL,
        name="sum_energy",
    )(arrived)


def on_device(psi, left_env, right_env, row_sizes, col_sizes):
    sectors = lax.axis_size("sec")
    sector = lax.axis_index("sec")
    even = sector % 2 == 0
    place = sector % 4

    def send(value, *hops):
        pairs = [
            (s, s + steps)
            for at, steps in hops
            for s in range(at, sectors, 4)
            if 0 <= s + steps < sectors
        ]
        return lax.ppermute(value, "sec", pairs)

    rows = psi.shape[1]
    part = rows // 2
    which = jnp.where(place == 0, 1, jnp.where(place == 2, 0, 2))
    orders = [jnp.where(even, 2, 1), jnp.where(even, 3, 2), jnp.where(even, 1, 3), 0]
    info = jnp.stack([*orders, row_sizes[0], col_sizes[0], which]).astype(jnp.int32)

    pairs_up = [(s, s + 1) for s in range(1, sectors, 4) if s + 1 < sectors]
    pairs_up += [(s, s - 3) for s in range(3, sectors, 4) if s + 1 < sectors]

    def raise_one(value):
        return lax.ppermute(value, "sec", pairs_up)

    def along(value):
        return send(value, (3, 3), (0, -3))

    def across(value):
        return send(value, (1, 2), (2, -1))

    def swap(value):
        return send(value, (0, 1), (1, -1), (2, 1), (3, -1))

    def relay(value):
        return send(value, (0, 4))

    envs = (left_env, right_env)
    first0, token, live, *ops0 = opening_rows(info, psi[0], envs, 0, part, masks=True)
    paired0 = swap(first0)
    first1, token = term_rows(info, live, ops0, part, part, token)
    paired1 = swap(first1)
    both0, token = add(first0, paired0, token)
    raised0 = raise_one(both0)
    second0, token, *ops1 = opening_rows(info, live, envs, 1, part, token)
    moved0 = along(second0)
    both1, token = add(first1, paired1, token)
    raised1 = raise_one(both1)
    second1, token, *ops2 = term_rows(info, live, ops1, part, part, token, bring=(2, *envs))
    moved1 = along(second1)
    third0, token, *ops3 = term_rows(info, live, ops2, 0, part, token, bring=(3, *envs))
    swapped0 = swap(third0)
    raised0, token = hold(raised0, token)
    relayed0 = relay(raised0)
    third1, token = term_rows(info, live, ops2, part, part, token)
    swapped1 = swap(third1)
    summed0, token = add(second0, moved0, token)
    crossed0 = across(summed0)
    raised1, token = hold(raised1, token)
    relayed1 = relay(raised1)
    own0, token = term_rows(info, live, ops3, 0, part, token, added=swapped0)
    token = touch(relayed0, token)
    summed1, token = add(second1, moved1, token)
    crossed1 = across(summed1)

    energy = jnp.zeros((sectors // 2, 128), jnp.float32)
    sigma, energy = finish(info, live, own0, (raised0, relayed0, crossed0), energy, None, 0)
    own1, token = term_rows(info, live, ops3, part, part, token, energy, added=swapped1)
    sigma, energy = finish(info, live, own1, (raised1, relayed1, crossed1), energy, sigma, part)
    return sigma, sum_over_sectors(energy, sectors)


def solution(mesh):
    return jax.shard_map(
        on_device,
        mesh=mesh,
        in_specs=(
            P(("grp", "sec"), None, None),
            P(("grp", "sec"), None, None, None),
            P(("grp", "sec"), None, None, None),
            P(("grp", "sec")),
            P(("grp", "sec")),
        ),
        out_specs=(P(("grp", "sec"), None, None), P("grp")),
        check_vma=False,
    )
```

```python
import functools

import jax
import jax.numpy as jnp
from jax import lax
from jax.experimental import pallas as pl
from jax.experimental.pallas import tpu as pltpu
from jax.sharding import PartitionSpec as P

MIB = 1024 * 1024
LEFT_PIECES, RIGHT_PIECES = 8, 2
FIRST_MIB = 48
BRING_MIB = 42

ANY = pl.BlockSpec(memory_space=pl.ANY)
HBM = pl.BlockSpec(memory_space=pltpu.HBM)
SMEM = pl.BlockSpec(memory_space=pltpu.SMEM)
WHOLE = pl.BlockSpec(memory_space=pltpu.VMEM)
TOKEN = jax.ShapeDtypeStruct((8, 128), jnp.float32)
SMALL = pl.CostEstimate(flops=200000000, bytes_accessed=1000000, transcendentals=0)


def params(mib=8):
    return pltpu.CompilerParams(vmem_limit_bytes=mib * MIB)


def fetch(info_ref, slot, left_hbm, right_hbm, left_ref, right_ref, sems):
    term = info_ref[slot]
    rows, cols = left_ref.shape[0], right_ref.shape[0]
    step = rows // LEFT_PIECES
    left, right = [], []
    for i in range(LEFT_PIECES):
        span = pl.ds(i * step, step)
        left.append(
            pltpu.make_async_copy(left_hbm.at[0, term, span, :], left_ref.at[span, :], sems.at[i])
        )
    step = cols // RIGHT_PIECES
    for i in range(RIGHT_PIECES):
        span = pl.ds(i * step, step)
        right.append(
            pltpu.make_async_copy(
                right_hbm.at[0, term, span, :], right_ref.at[span, :], sems.at[LEFT_PIECES + i]
            )
        )
    half = LEFT_PIECES // 2
    return left[:half] + right, left[half:]


def multiply(left, live, right):
    first = jnp.dot(left, live, preferred_element_type=jnp.float32).astype(jnp.bfloat16)
    return jnp.dot(first, right, preferred_element_type=jnp.float32)


def opening_kernel(slot, masks, tokens, info_ref, live_ref, left_hbm, right_hbm, *refs):
    refs = list(refs[tokens:])
    out_ref, _ = refs[:2]
    sems = refs[-1]
    operands = refs[2:-1]
    psi_ref = live_ref
    if masks:
        live_ref = operands.pop(0)
    own, late = fetch(info_ref, slot, left_hbm, right_hbm, *operands, sems)
    for copy in own + late:
        copy.start()
    if masks:
        rows, cols = psi_ref.shape
        step = 128
        col = lax.broadcasted_iota(jnp.int32, (step, cols), 1) < info_ref[5]
        row = lax.broadcasted_iota(jnp.int32, (step, cols), 0)
        for start in range(0, rows, step):
            span = pl.ds(start, step)
            inside = jnp.logical_and(row < info_ref[4] - start, col)
            values = jnp.where(inside, psi_ref[span, :].astype(jnp.float32), 0.0)
            live_ref[span, :] = values.astype(live_ref.dtype)
    for copy in own:
        copy.wait()
    out_ref[...] = multiply(operands[0][: out_ref.shape[0], :], live_ref[...], operands[1][...])
    for copy in late:
        copy.wait()


def operand_shapes(width, cols):
    return [
        jax.ShapeDtypeStruct((width, width), jnp.bfloat16),
        jax.ShapeDtypeStruct((cols, cols), jnp.bfloat16),
    ]


def opening_rows(info, live, envs, slot, count, *tokens, masks=False):
    width, cols = live.shape
    out_shape = [jax.ShapeDtypeStruct((count, cols), jnp.float32), TOKEN]
    if masks:
        out_shape.append(jax.ShapeDtypeStruct(live.shape, live.dtype))
    out_shape += operand_shapes(width, cols)
    return pl.pallas_call(
        functools.partial(opening_kernel, slot, masks, len(tokens)),
        out_shape=out_shape,
        in_specs=[SMEM, WHOLE, HBM, HBM] + [ANY] * len(tokens),
        out_specs=[WHOLE, ANY] + [WHOLE] * (len(out_shape) - 2),
        scratch_shapes=[pltpu.SemaphoreType.DMA((LEFT_PIECES + RIGHT_PIECES,))],
        compiler_params=params(FIRST_MIB if masks else BRING_MIB),
        cost_estimate=SMALL,
        name="opening_rows",
    )(info, live, *envs, *tokens)


def term_kernel(first, adds, slot, tokens, info_ref, live_ref, left_ref, right_ref, *refs):
    refs = list(refs)
    add_ref = refs.pop(0) if adds else None
    copies = []
    if slot is not None:
        left_hbm, right_hbm = refs[:2]
        sems = refs[-1]
        out_ref, _, left_next, right_next = refs[2 + tokens : -1]
        copies = sum(fetch(info_ref, slot, left_hbm, right_hbm, left_next, right_next, sems), [])
        for copy in copies:
            copy.start()
    else:
        out_ref, _ = refs[tokens:]
    count = out_ref.shape[0]
    block = min(count, 512)
    for i in range(count // block):
        span = pl.ds(i * block, block)
        value = multiply(left_ref[pl.ds(first + i * block, block), :], live_ref[...], right_ref[...])
        if adds:
            value = value + add_ref[span, :]
        out_ref[span, :] = value
    for copy in copies:
        copy.wait()


def term_rows(info, live, operands, first, count, *tokens, added=None, bring=None):
    width, cols = live.shape
    in_specs = [SMEM, WHOLE, WHOLE, WHOLE]
    args = [info, live, *operands]
    out_shape = [jax.ShapeDtypeStruct((count, cols), jnp.float32), TOKEN]
    out_specs = [WHOLE, ANY]
    scratch = []
    slot = None
    if added is not None:
        in_specs.append(WHOLE)
        args.append(added)
    if bring is not None:
        slot = bring[0]
        in_specs += [HBM, HBM]
        args += bring[1:]
        out_shape += operand_shapes(width, cols)
        out_specs += [WHOLE, WHOLE]
        scratch.append(pltpu.SemaphoreType.DMA((LEFT_PIECES + RIGHT_PIECES,)))
    return pl.pallas_call(
        functools.partial(term_kernel, first, added is not None, slot, len(tokens)),
        out_shape=out_shape,
        in_specs=in_specs + [ANY] * len(tokens),
        out_specs=out_specs,
        scratch_shapes=scratch,
        compiler_params=params(12 if slot is None else BRING_MIB),
        cost_estimate=SMALL,
        name="term_rows",
    )(*args, *tokens)


def add_kernel(a_ref, b_ref, *refs):
    out_ref = refs[-2]
    rows = a_ref.shape[0]
    step = 64

    def body(i, _):
        span = pl.ds(pl.multiple_of(i * step, step), step)
        out_ref[span, :] = a_ref[span, :] + b_ref[span, :]
        return _

    lax.fori_loop(0, rows // step, body, 0)


def add(a, b, *tokens):
    return pl.pallas_call(
        add_kernel,
        out_shape=(jax.ShapeDtypeStruct(a.shape, a.dtype), TOKEN),
        in_specs=[WHOLE, WHOLE] + [ANY] * len(tokens),
        out_specs=(WHOLE, ANY),
        compiler_params=params(),
        cost_estimate=SMALL,
        name="add_blocks",
    )(a, b, *tokens)


def touch(*values):
    return pl.pallas_call(
        lambda *refs: None,
        out_shape=TOKEN,
        in_specs=[ANY] * len(values),
        out_specs=ANY,
        compiler_params=params(),
        cost_estimate=SMALL,
        name="touch",
    )(*values)


def hold(value, token):
    return pl.pallas_call(
        lambda *refs: None,
        out_shape=(jax.ShapeDtypeStruct(value.shape, value.dtype), TOKEN),
        in_specs=[ANY, ANY],
        out_specs=(ANY, ANY),
        input_output_aliases={0: 0},
        compiler_params=params(),
        cost_estimate=SMALL,
        name="hold",
    )(value, token)


def finish_kernel(first, info_ref, live_ref, own_ref, a_ref, b_ref, c_ref, before_ref, *refs):
    sigma_hbm, energy_ref, sigma_buf, sems = refs[-4:]
    count, cols = own_ref.shape
    step = 64
    piece = count // sems.shape[0]
    col = lax.broadcasted_iota(jnp.int32, (step, cols), 1) < info_ref[5]
    row = lax.broadcasted_iota(jnp.int32, (step, cols), 0)

    def copy(i):
        span = pl.ds(i * piece, piece)
        return pltpu.make_async_copy(
            sigma_buf.at[span, :], sigma_hbm.at[0, pl.ds(first + i * piece, piece), :], sems.at[i]
        )

    def work(arrival):
        energy = jnp.zeros((8, cols), jnp.float32)
        for i in range(count // piece):

            def body(n, energy):
                start = pl.multiple_of(i * piece + n * step, step)
                span = pl.ds(start, step)
                inside = jnp.logical_and(row < info_ref[4] - first - start, col)
                total = jnp.where(inside, own_ref[span, :] + arrival[span, :], 0.0)
                sigma_buf[span, :] = total.astype(sigma_buf.dtype)
                here = pl.ds(pl.multiple_of(first + start, step), step)
                product = live_ref[here, :].astype(jnp.float32) * total
                return energy + jnp.sum(jnp.reshape(product, (step // 8, 8, cols)), axis=0)

            energy = lax.fori_loop(0, piece // step, body, energy)
            copy(i).start()
        energy_ref[...] = before_ref[...] + jnp.sum(energy)

    for n, arrival in enumerate((a_ref, b_ref, c_ref)):
        pl.when(info_ref[6] == n)(functools.partial(work, arrival))
    for i in range(count // piece):
        copy(i).wait()


def finish(info, live, own, arrivals, before, sigma, first):
    count, cols = own.shape
    in_specs = [SMEM] + [WHOLE] * 6
    operands = [info, live, own, *arrivals, before]
    aliases = {}
    if sigma is not None:
        in_specs.append(ANY)
        aliases = {len(operands): 0}
        operands.append(sigma)
    return pl.pallas_call(
        functools.partial(finish_kernel, first),
        out_shape=(
            jax.ShapeDtypeStruct((1, *live.shape), jnp.bfloat16),
            jax.ShapeDtypeStruct(before.shape, jnp.float32),
        ),
        in_specs=in_specs,
        out_specs=(ANY, WHOLE),
        scratch_shapes=[pltpu.VMEM((count, cols), jnp.bfloat16), pltpu.SemaphoreType.DMA((4,))],
        input_output_aliases=aliases,
        compiler_params=params(),
        cost_estimate=SMALL,
        name="finish_rows",
    )(*operands)


def sum_over_sectors(value):
    arrived = lax.all_to_all(value, "sec", 0, 0, tiled=True)
    return jnp.reshape(jnp.sum(arrived[:, 0]), (1,))


def on_device(psi, left_env, right_env, row_sizes, col_sizes):
    sectors = lax.axis_size("sec")
    sector = lax.axis_index("sec")
    even = sector % 2 == 0
    place = sector % 4

    def send(value, *hops):
        pairs = [
            (s, s + steps)
            for at, steps in hops
            for s in range(at, sectors, 4)
            if 0 <= s + steps < sectors
        ]
        return lax.ppermute(value, "sec", pairs)

    rows = psi.shape[1]
    part = rows // 2
    which = jnp.where(place == 0, 1, jnp.where(place == 2, 0, 2))
    orders = [jnp.where(even, 2, 1), jnp.where(even, 3, 2), jnp.where(even, 1, 3), 0]
    info = jnp.stack([*orders, row_sizes[0], col_sizes[0], which]).astype(jnp.int32)

    pairs_up = [(s, s + 1) for s in range(1, sectors, 4) if s + 1 < sectors]
    pairs_up += [(s, s - 3) for s in range(3, sectors, 4) if s + 1 < sectors]

    def raise_one(value):
        return lax.ppermute(value, "sec", pairs_up)

    def along(value):
        return send(value, (3, 3), (0, -3))

    def across(value):
        return send(value, (1, 2), (2, -1))

    def swap(value):
        return send(value, (0, 1), (1, -1), (2, 1), (3, -1))

    def relay(value):
        return send(value, (0, 4))

    envs = (left_env, right_env)
    first0, token, live, *ops0 = opening_rows(info, psi[0], envs, 0, part, masks=True)
    paired0 = swap(first0)
    first1, token = term_rows(info, live, ops0, part, part, token)
    paired1 = swap(first1)
    both0, token = add(first0, paired0, token)
    raised0 = raise_one(both0)
    second0, token, *ops1 = opening_rows(info, live, envs, 1, part, token)
    moved0 = along(second0)
    both1, token = add(first1, paired1, token)
    raised1 = raise_one(both1)
    second1, token, *ops2 = term_rows(info, live, ops1, part, part, token, bring=(2, *envs))
    moved1 = along(second1)
    third0, token, *ops3 = term_rows(info, live, ops2, 0, part, token, bring=(3, *envs))
    swapped0 = swap(third0)
    raised0, token = hold(raised0, token)
    relayed0 = relay(raised0)
    third1, token = term_rows(info, live, ops2, part, part, token)
    swapped1 = swap(third1)
    summed0, token = add(second0, moved0, token)
    crossed0 = across(summed0)
    raised1, token = hold(raised1, token)
    relayed1 = relay(raised1)
    own0, token = term_rows(info, live, ops3, 0, part, token, added=swapped0)
    token = touch(relayed0, token)
    summed1, token = add(second1, moved1, token)
    crossed1 = across(summed1)

    energy = jnp.zeros((sectors, 128), jnp.float32)
    sigma, energy = finish(info, live, own0, (raised0, relayed0, crossed0), energy, None, 0)
    own1, token = term_rows(info, live, ops3, part, part, token, energy, added=swapped1)
    sigma, energy = finish(info, live, own1, (raised1, relayed1, crossed1), energy, sigma, part)
    return sigma, sum_over_sectors(energy)


def solution(mesh):
    return jax.shard_map(
        on_device,
        mesh=mesh,
        in_specs=(
            P(("grp", "sec"), None, None),
            P(("grp", "sec"), None, None, None),
            P(("grp", "sec"), None, None, None),
            P(("grp", "sec")),
            P(("grp", "sec")),
        ),
        out_specs=(P(("grp", "sec"), None, None), P("grp")),
        check_vma=False,
    )
```

```python
import functools

import jax
import jax.numpy as jnp
from jax import lax
from jax.experimental import pallas as pl
from jax.experimental.pallas import tpu as pltpu
from jax.sharding import PartitionSpec as P

MIB = 1024 * 1024
LEFT_PIECES, RIGHT_PIECES = 8, 2
FIRST_MIB = 48
BRING_MIB = 42

ANY = pl.BlockSpec(memory_space=pl.ANY)
HBM = pl.BlockSpec(memory_space=pltpu.HBM)
SMEM = pl.BlockSpec(memory_space=pltpu.SMEM)
WHOLE = pl.BlockSpec(memory_space=pltpu.VMEM)
TOKEN = jax.ShapeDtypeStruct((8, 128), jnp.float32)
SMALL = pl.CostEstimate(flops=200000000, bytes_accessed=1000000, transcendentals=0)


def params(mib=8):
    return pltpu.CompilerParams(vmem_limit_bytes=mib * MIB)


def fetch(info_ref, slot, left_hbm, right_hbm, left_ref, right_ref, sems):
    term = info_ref[slot]
    rows, cols = left_ref.shape[0], right_ref.shape[0]
    step = rows // LEFT_PIECES
    left, right = [], []
    for i in range(LEFT_PIECES):
        span = pl.ds(i * step, step)
        left.append(
            pltpu.make_async_copy(left_hbm.at[0, term, span, :], left_ref.at[span, :], sems.at[i])
        )
    step = cols // RIGHT_PIECES
    for i in range(RIGHT_PIECES):
        span = pl.ds(i * step, step)
        right.append(
            pltpu.make_async_copy(
                right_hbm.at[0, term, span, :], right_ref.at[span, :], sems.at[LEFT_PIECES + i]
            )
        )
    half = LEFT_PIECES // 2
    return left[:half], right, left[half:]


def multiply(left, live, right):
    first = jnp.dot(left, live, preferred_element_type=jnp.float32).astype(jnp.bfloat16)
    return jnp.dot(first, right, preferred_element_type=jnp.float32)


def opening_kernel(slot, masks, tokens, info_ref, live_ref, left_hbm, right_hbm, *refs):
    refs = list(refs[tokens:])
    out_ref, _ = refs[:2]
    sems = refs[-1]
    operands = refs[2:-1]
    psi_ref = live_ref
    if masks:
        live_ref = operands.pop(0)
    left, right, late = fetch(info_ref, slot, left_hbm, right_hbm, *operands, sems)
    for copy in left + right + late:
        copy.start()
    if masks:
        rows, cols = psi_ref.shape
        step = 128
        col = lax.broadcasted_iota(jnp.int32, (step, cols), 1) < info_ref[5]
        row = lax.broadcasted_iota(jnp.int32, (step, cols), 0)
        for start in range(0, rows, step):
            span = pl.ds(start, step)
            inside = jnp.logical_and(row < info_ref[4] - start, col)
            values = jnp.where(inside, psi_ref[span, :].astype(jnp.float32), 0.0)
            live_ref[span, :] = values.astype(live_ref.dtype)
    for copy in left:
        copy.wait()
    value = jnp.dot(
        operands[0][: out_ref.shape[0], :], live_ref[...], preferred_element_type=jnp.float32
    )
    for copy in right:
        copy.wait()
    out_ref[...] = jnp.dot(
        value.astype(jnp.bfloat16), operands[1][...], preferred_element_type=jnp.float32
    )
    for copy in late:
        copy.wait()


def operand_shapes(width, cols):
    return [
        jax.ShapeDtypeStruct((width, width), jnp.bfloat16),
        jax.ShapeDtypeStruct((cols, cols), jnp.bfloat16),
    ]


def opening_rows(info, live, envs, slot, count, *tokens, masks=False):
    width, cols = live.shape
    out_shape = [jax.ShapeDtypeStruct((count, cols), jnp.float32), TOKEN]
    if masks:
        out_shape.append(jax.ShapeDtypeStruct(live.shape, live.dtype))
    out_shape += operand_shapes(width, cols)
    return pl.pallas_call(
        functools.partial(opening_kernel, slot, masks, len(tokens)),
        out_shape=out_shape,
        in_specs=[SMEM, WHOLE, HBM, HBM] + [ANY] * len(tokens),
        out_specs=[WHOLE, ANY] + [WHOLE] * (len(out_shape) - 2),
        scratch_shapes=[pltpu.SemaphoreType.DMA((LEFT_PIECES + RIGHT_PIECES,))],
        compiler_params=params(FIRST_MIB if masks else BRING_MIB),
        cost_estimate=SMALL,
        name="opening_rows",
    )(info, live, *envs, *tokens)


def term_kernel(first, adds, slot, tokens, info_ref, live_ref, left_ref, right_ref, *refs):
    refs = list(refs)
    add_ref = refs.pop(0) if adds else None
    copies = []
    if slot is not None:
        left_hbm, right_hbm = refs[:2]
        sems = refs[-1]
        out_ref, _, left_next, right_next = refs[2 + tokens : -1]
        copies = sum(fetch(info_ref, slot, left_hbm, right_hbm, left_next, right_next, sems), [])
        for copy in copies:
            copy.start()
    else:
        out_ref, _ = refs[tokens:]
    count = out_ref.shape[0]
    block = min(count, 512)
    for i in range(count // block):
        span = pl.ds(i * block, block)
        value = multiply(left_ref[pl.ds(first + i * block, block), :], live_ref[...], right_ref[...])
        if adds:
            value = value + add_ref[span, :]
        out_ref[span, :] = value
    for copy in copies:
        copy.wait()


def term_rows(info, live, operands, first, count, *tokens, added=None, bring=None):
    width, cols = live.shape
    in_specs = [SMEM, WHOLE, WHOLE, WHOLE]
    args = [info, live, *operands]
    out_shape = [jax.ShapeDtypeStruct((count, cols), jnp.float32), TOKEN]
    out_specs = [WHOLE, ANY]
    scratch = []
    slot = None
    if added is not None:
        in_specs.append(WHOLE)
        args.append(added)
    if bring is not None:
        slot = bring[0]
        in_specs += [HBM, HBM]
        args += bring[1:]
        out_shape += operand_shapes(width, cols)
        out_specs += [WHOLE, WHOLE]
        scratch.append(pltpu.SemaphoreType.DMA((LEFT_PIECES + RIGHT_PIECES,)))
    return pl.pallas_call(
        functools.partial(term_kernel, first, added is not None, slot, len(tokens)),
        out_shape=out_shape,
        in_specs=in_specs + [ANY] * len(tokens),
        out_specs=out_specs,
        scratch_shapes=scratch,
        compiler_params=params(12 if slot is None else BRING_MIB),
        cost_estimate=SMALL,
        name="term_rows",
    )(*args, *tokens)


def add_kernel(a_ref, b_ref, *refs):
    out_ref = refs[-2]
    rows = a_ref.shape[0]
    step = 64

    def body(i, _):
        span = pl.ds(pl.multiple_of(i * step, step), step)
        out_ref[span, :] = a_ref[span, :] + b_ref[span, :]
        return _

    lax.fori_loop(0, rows // step, body, 0)


def add(a, b, *tokens):
    return pl.pallas_call(
        add_kernel,
        out_shape=(jax.ShapeDtypeStruct(a.shape, a.dtype), TOKEN),
        in_specs=[WHOLE, WHOLE] + [ANY] * len(tokens),
        out_specs=(WHOLE, ANY),
        compiler_params=params(),
        cost_estimate=SMALL,
        name="add_blocks",
    )(a, b, *tokens)


def touch(*values):
    return pl.pallas_call(
        lambda *refs: None,
        out_shape=TOKEN,
        in_specs=[ANY] * len(values),
        out_specs=ANY,
        compiler_params=params(),
        cost_estimate=SMALL,
        name="touch",
    )(*values)


def hold(value, token):
    return pl.pallas_call(
        lambda *refs: None,
        out_shape=(jax.ShapeDtypeStruct(value.shape, value.dtype), TOKEN),
        in_specs=[ANY, ANY],
        out_specs=(ANY, ANY),
        input_output_aliases={0: 0},
        compiler_params=params(),
        cost_estimate=SMALL,
        name="hold",
    )(value, token)


def finish_kernel(first, info_ref, live_ref, own_ref, a_ref, b_ref, c_ref, before_ref, *refs):
    sigma_hbm, energy_ref, sigma_buf, sems = refs[-4:]
    count, cols = own_ref.shape
    step = 64
    piece = count // sems.shape[0]
    col = lax.broadcasted_iota(jnp.int32, (step, cols), 1) < info_ref[5]
    row = lax.broadcasted_iota(jnp.int32, (step, cols), 0)

    def copy(i):
        span = pl.ds(i * piece, piece)
        return pltpu.make_async_copy(
            sigma_buf.at[span, :], sigma_hbm.at[0, pl.ds(first + i * piece, piece), :], sems.at[i]
        )

    def work(arrival):
        energy = jnp.zeros((8, cols), jnp.float32)
        for i in range(count // piece):

            def body(n, energy):
                start = pl.multiple_of(i * piece + n * step, step)
                span = pl.ds(start, step)
                inside = jnp.logical_and(row < info_ref[4] - first - start, col)
                total = jnp.where(inside, own_ref[span, :] + arrival[span, :], 0.0)
                sigma_buf[span, :] = total.astype(sigma_buf.dtype)
                here = pl.ds(pl.multiple_of(first + start, step), step)
                product = live_ref[here, :].astype(jnp.float32) * total
                return energy + jnp.sum(jnp.reshape(product, (step // 8, 8, cols)), axis=0)

            energy = lax.fori_loop(0, piece // step, body, energy)
            copy(i).start()
        energy_ref[...] = before_ref[...] + jnp.sum(energy)

    for n, arrival in enumerate((a_ref, b_ref, c_ref)):
        pl.when(info_ref[6] == n)(functools.partial(work, arrival))
    for i in range(count // piece):
        copy(i).wait()


def finish(info, live, own, arrivals, before, sigma, first):
    count, cols = own.shape
    in_specs = [SMEM] + [WHOLE] * 6
    operands = [info, live, own, *arrivals, before]
    aliases = {}
    if sigma is not None:
        in_specs.append(ANY)
        aliases = {len(operands): 0}
        operands.append(sigma)
    return pl.pallas_call(
        functools.partial(finish_kernel, first),
        out_shape=(
            jax.ShapeDtypeStruct((1, *live.shape), jnp.bfloat16),
            jax.ShapeDtypeStruct(before.shape, jnp.float32),
        ),
        in_specs=in_specs,
        out_specs=(ANY, WHOLE),
        scratch_shapes=[pltpu.VMEM((count, cols), jnp.bfloat16), pltpu.SemaphoreType.DMA((4,))],
        input_output_aliases=aliases,
        compiler_params=params(),
        cost_estimate=SMALL,
        name="finish_rows",
    )(*operands)


def sum_over_sectors(value):
    arrived = lax.all_to_all(value, "sec", 0, 0, tiled=True)
    return jnp.reshape(jnp.sum(arrived[:, 0]), (1,))


def on_device(psi, left_env, right_env, row_sizes, col_sizes):
    sectors = lax.axis_size("sec")
    sector = lax.axis_index("sec")
    even = sector % 2 == 0
    place = sector % 4

    def send(value, *hops):
        pairs = [
            (s, s + steps)
            for at, steps in hops
            for s in range(at, sectors, 4)
            if 0 <= s + steps < sectors
        ]
        return lax.ppermute(value, "sec", pairs)

    rows = psi.shape[1]
    part = rows // 2
    which = jnp.where(place == 0, 1, jnp.where(place == 2, 0, 2))
    orders = [jnp.where(even, 2, 1), jnp.where(even, 3, 2), jnp.where(even, 1, 3), 0]
    info = jnp.stack([*orders, row_sizes[0], col_sizes[0], which]).astype(jnp.int32)

    pairs_up = [(s, s + 1) for s in range(1, sectors, 4) if s + 1 < sectors]
    pairs_up += [(s, s - 3) for s in range(3, sectors, 4) if s + 1 < sectors]

    def raise_one(value):
        return lax.ppermute(value, "sec", pairs_up)

    def along(value):
        return send(value, (3, 3), (0, -3))

    def across(value):
        return send(value, (1, 2), (2, -1))

    def swap(value):
        return send(value, (0, 1), (1, -1), (2, 1), (3, -1))

    def relay(value):
        return send(value, (0, 4))

    envs = (left_env, right_env)
    first0, token, live, *ops0 = opening_rows(info, psi[0], envs, 0, part, masks=True)
    paired0 = swap(first0)
    first1, token = term_rows(info, live, ops0, part, part, token)
    paired1 = swap(first1)
    both0, token = add(first0, paired0, token)
    raised0 = raise_one(both0)
    second0, token, *ops1 = opening_rows(info, live, envs, 1, part, token)
    moved0 = along(second0)
    both1, token = add(first1, paired1, token)
    raised1 = raise_one(both1)
    second1, token, *ops2 = term_rows(info, live, ops1, part, part, token, bring=(2, *envs))
    moved1 = along(second1)
    third0, token, *ops3 = term_rows(info, live, ops2, 0, part, token, bring=(3, *envs))
    swapped0 = swap(third0)
    raised0, token = hold(raised0, token)
    relayed0 = relay(raised0)
    third1, token = term_rows(info, live, ops2, part, part, token)
    swapped1 = swap(third1)
    summed0, token = add(second0, moved0, token)
    crossed0 = across(summed0)
    raised1, token = hold(raised1, token)
    relayed1 = relay(raised1)
    own0, token = term_rows(info, live, ops3, 0, part, token, added=swapped0)
    token = touch(relayed0, token)
    summed1, token = add(second1, moved1, token)
    crossed1 = across(summed1)

    energy = jnp.zeros((sectors, 128), jnp.float32)
    sigma, energy = finish(info, live, own0, (raised0, relayed0, crossed0), energy, None, 0)
    own1, token = term_rows(info, live, ops3, part, part, token, energy, added=swapped1)
    sigma, energy = finish(info, live, own1, (raised1, relayed1, crossed1), energy, sigma, part)
    return sigma, sum_over_sectors(energy)


def solution(mesh):
    return jax.shard_map(
        on_device,
        mesh=mesh,
        in_specs=(
            P(("grp", "sec"), None, None),
            P(("grp", "sec"), None, None, None),
            P(("grp", "sec"), None, None, None),
            P(("grp", "sec")),
            P(("grp", "sec")),
        ),
        out_specs=(P(("grp", "sec"), None, None), P("grp")),
        check_vma=False,
    )
```

```python
import functools

import jax
import jax.numpy as jnp
from jax import lax
from jax.experimental import pallas as pl
from jax.experimental.pallas import tpu as pltpu
from jax.sharding import PartitionSpec as P

MIB = 1024 * 1024
LEFT_PIECES, RIGHT_PIECES = 8, 2
FIRST_MIB = 48
BRING_MIB = 42

ANY = pl.BlockSpec(memory_space=pl.ANY)
HBM = pl.BlockSpec(memory_space=pltpu.HBM)
SMEM = pl.BlockSpec(memory_space=pltpu.SMEM)
WHOLE = pl.BlockSpec(memory_space=pltpu.VMEM)
TOKEN = jax.ShapeDtypeStruct((8, 128), jnp.float32)
SMALL = pl.CostEstimate(flops=200000000, bytes_accessed=1000000, transcendentals=0)


def params(mib=8):
    return pltpu.CompilerParams(vmem_limit_bytes=mib * MIB)


def fetch(info_ref, slot, left_hbm, right_hbm, left_ref, right_ref, sems):
    term = info_ref[slot]
    rows, cols = left_ref.shape[0], right_ref.shape[0]
    step = rows // LEFT_PIECES
    left, right = [], []
    for i in range(LEFT_PIECES):
        span = pl.ds(i * step, step)
        left.append(
            pltpu.make_async_copy(left_hbm.at[0, term, span, :], left_ref.at[span, :], sems.at[i])
        )
    step = cols // RIGHT_PIECES
    for i in range(RIGHT_PIECES):
        span = pl.ds(i * step, step)
        right.append(
            pltpu.make_async_copy(
                right_hbm.at[0, term, span, :], right_ref.at[span, :], sems.at[LEFT_PIECES + i]
            )
        )
    half = LEFT_PIECES // 2
    return left[:half], right, left[half:]


def multiply(left, live, right):
    first = jnp.dot(left, live, preferred_element_type=jnp.float32).astype(jnp.bfloat16)
    return jnp.dot(first, right, preferred_element_type=jnp.float32)


def opening_kernel(slot, masks, tokens, info_ref, live_ref, left_hbm, right_hbm, *refs):
    refs = list(refs[tokens:])
    out_ref, _ = refs[:2]
    sems = refs[-1]
    operands = refs[2:-1]
    psi_ref = live_ref
    if masks:
        live_ref = operands.pop(0)
    left, right, late = fetch(info_ref, slot, left_hbm, right_hbm, *operands, sems)
    for copy in left + right + late:
        copy.start()
    if masks:
        rows, cols = psi_ref.shape
        step = 128
        col = lax.broadcasted_iota(jnp.int32, (step, cols), 1) < info_ref[5]
        row = lax.broadcasted_iota(jnp.int32, (step, cols), 0)
        for start in range(0, rows, step):
            span = pl.ds(start, step)
            inside = jnp.logical_and(row < info_ref[4] - start, col)
            values = jnp.where(inside, psi_ref[span, :].astype(jnp.float32), 0.0)
            live_ref[span, :] = values.astype(live_ref.dtype)
    block = out_ref.shape[0] // 2
    for i in range(2):
        span = pl.ds(i * block, block)
        for copy in left[i * len(left) // 2 : (i + 1) * len(left) // 2]:
            copy.wait()
        value = jnp.dot(operands[0][span, :], live_ref[...], preferred_element_type=jnp.float32)
        if i == 0:
            for copy in right:
                copy.wait()
        out_ref[span, :] = jnp.dot(
            value.astype(jnp.bfloat16), operands[1][...], preferred_element_type=jnp.float32
        )
    for copy in late:
        copy.wait()


def operand_shapes(width, cols):
    return [
        jax.ShapeDtypeStruct((width, width), jnp.bfloat16),
        jax.ShapeDtypeStruct((cols, cols), jnp.bfloat16),
    ]


def opening_rows(info, live, envs, slot, count, *tokens, masks=False):
    width, cols = live.shape
    out_shape = [jax.ShapeDtypeStruct((count, cols), jnp.float32), TOKEN]
    if masks:
        out_shape.append(jax.ShapeDtypeStruct(live.shape, live.dtype))
    out_shape += operand_shapes(width, cols)
    return pl.pallas_call(
        functools.partial(opening_kernel, slot, masks, len(tokens)),
        out_shape=out_shape,
        in_specs=[SMEM, WHOLE, HBM, HBM] + [ANY] * len(tokens),
        out_specs=[WHOLE, ANY] + [WHOLE] * (len(out_shape) - 2),
        scratch_shapes=[pltpu.SemaphoreType.DMA((LEFT_PIECES + RIGHT_PIECES,))],
        compiler_params=params(FIRST_MIB if masks else BRING_MIB),
        cost_estimate=SMALL,
        name="opening_rows",
    )(info, live, *envs, *tokens)


def term_kernel(first, adds, slot, tokens, info_ref, live_ref, left_ref, right_ref, *refs):
    refs = list(refs)
    add_ref = refs.pop(0) if adds else None
    copies = []
    if slot is not None:
        left_hbm, right_hbm = refs[:2]
        sems = refs[-1]
        out_ref, _, left_next, right_next = refs[2 + tokens : -1]
        copies = sum(fetch(info_ref, slot, left_hbm, right_hbm, left_next, right_next, sems), [])
        for copy in copies:
            copy.start()
    else:
        out_ref, _ = refs[tokens:]
    count = out_ref.shape[0]
    block = min(count, 512)
    for i in range(count // block):
        span = pl.ds(i * block, block)
        value = multiply(left_ref[pl.ds(first + i * block, block), :], live_ref[...], right_ref[...])
        if adds:
            value = value + add_ref[span, :]
        out_ref[span, :] = value
    for copy in copies:
        copy.wait()


def term_rows(info, live, operands, first, count, *tokens, added=None, bring=None):
    width, cols = live.shape
    in_specs = [SMEM, WHOLE, WHOLE, WHOLE]
    args = [info, live, *operands]
    out_shape = [jax.ShapeDtypeStruct((count, cols), jnp.float32), TOKEN]
    out_specs = [WHOLE, ANY]
    scratch = []
    slot = None
    if added is not None:
        in_specs.append(WHOLE)
        args.append(added)
    if bring is not None:
        slot = bring[0]
        in_specs += [HBM, HBM]
        args += bring[1:]
        out_shape += operand_shapes(width, cols)
        out_specs += [WHOLE, WHOLE]
        scratch.append(pltpu.SemaphoreType.DMA((LEFT_PIECES + RIGHT_PIECES,)))
    return pl.pallas_call(
        functools.partial(term_kernel, first, added is not None, slot, len(tokens)),
        out_shape=out_shape,
        in_specs=in_specs + [ANY] * len(tokens),
        out_specs=out_specs,
        scratch_shapes=scratch,
        compiler_params=params(12 if slot is None else BRING_MIB),
        cost_estimate=SMALL,
        name="term_rows",
    )(*args, *tokens)


def add_kernel(a_ref, b_ref, *refs):
    out_ref = refs[-2]
    rows = a_ref.shape[0]
    step = 64

    def body(i, _):
        span = pl.ds(pl.multiple_of(i * step, step), step)
        out_ref[span, :] = a_ref[span, :] + b_ref[span, :]
        return _

    lax.fori_loop(0, rows // step, body, 0)


def add(a, b, *tokens):
    return pl.pallas_call(
        add_kernel,
        out_shape=(jax.ShapeDtypeStruct(a.shape, a.dtype), TOKEN),
        in_specs=[WHOLE, WHOLE] + [ANY] * len(tokens),
        out_specs=(WHOLE, ANY),
        compiler_params=params(),
        cost_estimate=SMALL,
        name="add_blocks",
    )(a, b, *tokens)


def touch(*values):
    return pl.pallas_call(
        lambda *refs: None,
        out_shape=TOKEN,
        in_specs=[ANY] * len(values),
        out_specs=ANY,
        compiler_params=params(),
        cost_estimate=SMALL,
        name="touch",
    )(*values)


def hold(value, token):
    return pl.pallas_call(
        lambda *refs: None,
        out_shape=(jax.ShapeDtypeStruct(value.shape, value.dtype), TOKEN),
        in_specs=[ANY, ANY],
        out_specs=(ANY, ANY),
        input_output_aliases={0: 0},
        compiler_params=params(),
        cost_estimate=SMALL,
        name="hold",
    )(value, token)


def finish_kernel(first, info_ref, live_ref, own_ref, a_ref, b_ref, c_ref, before_ref, *refs):
    sigma_hbm, energy_ref, sigma_buf, sems = refs[-4:]
    count, cols = own_ref.shape
    step = 64
    piece = count // sems.shape[0]
    col = lax.broadcasted_iota(jnp.int32, (step, cols), 1) < info_ref[5]
    row = lax.broadcasted_iota(jnp.int32, (step, cols), 0)

    def copy(i):
        span = pl.ds(i * piece, piece)
        return pltpu.make_async_copy(
            sigma_buf.at[span, :], sigma_hbm.at[0, pl.ds(first + i * piece, piece), :], sems.at[i]
        )

    def work(arrival):
        energy = jnp.zeros((8, cols), jnp.float32)
        for i in range(count // piece):

            def body(n, energy):
                start = pl.multiple_of(i * piece + n * step, step)
                span = pl.ds(start, step)
                inside = jnp.logical_and(row < info_ref[4] - first - start, col)
                total = jnp.where(inside, own_ref[span, :] + arrival[span, :], 0.0)
                sigma_buf[span, :] = total.astype(sigma_buf.dtype)
                here = pl.ds(pl.multiple_of(first + start, step), step)
                product = live_ref[here, :].astype(jnp.float32) * total
                return energy + jnp.sum(jnp.reshape(product, (step // 8, 8, cols)), axis=0)

            energy = lax.fori_loop(0, piece // step, body, energy)
            copy(i).start()
        energy_ref[...] = before_ref[...] + jnp.sum(energy)

    for n, arrival in enumerate((a_ref, b_ref, c_ref)):
        pl.when(info_ref[6] == n)(functools.partial(work, arrival))
    for i in range(count // piece):
        copy(i).wait()


def finish(info, live, own, arrivals, before, sigma, first):
    count, cols = own.shape
    in_specs = [SMEM] + [WHOLE] * 6
    operands = [info, live, own, *arrivals, before]
    aliases = {}
    if sigma is not None:
        in_specs.append(ANY)
        aliases = {len(operands): 0}
        operands.append(sigma)
    return pl.pallas_call(
        functools.partial(finish_kernel, first),
        out_shape=(
            jax.ShapeDtypeStruct((1, *live.shape), jnp.bfloat16),
            jax.ShapeDtypeStruct(before.shape, jnp.float32),
        ),
        in_specs=in_specs,
        out_specs=(ANY, WHOLE),
        scratch_shapes=[pltpu.VMEM((count, cols), jnp.bfloat16), pltpu.SemaphoreType.DMA((4,))],
        input_output_aliases=aliases,
        compiler_params=params(),
        cost_estimate=SMALL,
        name="finish_rows",
    )(*operands)


def sum_over_sectors(value):
    arrived = lax.all_to_all(value, "sec", 0, 0, tiled=True)
    return jnp.reshape(jnp.sum(arrived[:, 0]), (1,))


def on_device(psi, left_env, right_env, row_sizes, col_sizes):
    sectors = lax.axis_size("sec")
    sector = lax.axis_index("sec")
    even = sector % 2 == 0
    place = sector % 4

    def send(value, *hops):
        pairs = [
            (s, s + steps)
            for at, steps in hops
            for s in range(at, sectors, 4)
            if 0 <= s + steps < sectors
        ]
        return lax.ppermute(value, "sec", pairs)

    rows = psi.shape[1]
    part = rows // 2
    which = jnp.where(place == 0, 1, jnp.where(place == 2, 0, 2))
    orders = [jnp.where(even, 2, 1), jnp.where(even, 3, 2), jnp.where(even, 1, 3), 0]
    info = jnp.stack([*orders, row_sizes[0], col_sizes[0], which]).astype(jnp.int32)

    pairs_up = [(s, s + 1) for s in range(1, sectors, 4) if s + 1 < sectors]
    pairs_up += [(s, s - 3) for s in range(3, sectors, 4) if s + 1 < sectors]

    def raise_one(value):
        return lax.ppermute(value, "sec", pairs_up)

    def along(value):
        return send(value, (3, 3), (0, -3))

    def across(value):
        return send(value, (1, 2), (2, -1))

    def swap(value):
        return send(value, (0, 1), (1, -1), (2, 1), (3, -1))

    def relay(value):
        return send(value, (0, 4))

    envs = (left_env, right_env)
    first0, token, live, *ops0 = opening_rows(info, psi[0], envs, 0, part, masks=True)
    paired0 = swap(first0)
    first1, token = term_rows(info, live, ops0, part, part, token)
    paired1 = swap(first1)
    both0, token = add(first0, paired0, token)
    raised0 = raise_one(both0)
    second0, token, *ops1 = opening_rows(info, live, envs, 1, part, token)
    moved0 = along(second0)
    both1, token = add(first1, paired1, token)
    raised1 = raise_one(both1)
    second1, token, *ops2 = term_rows(info, live, ops1, part, part, token, bring=(2, *envs))
    moved1 = along(second1)
    third0, token, *ops3 = term_rows(info, live, ops2, 0, part, token, bring=(3, *envs))
    swapped0 = swap(third0)
    raised0, token = hold(raised0, token)
    relayed0 = relay(raised0)
    third1, token = term_rows(info, live, ops2, part, part, token)
    swapped1 = swap(third1)
    summed0, token = add(second0, moved0, token)
    crossed0 = across(summed0)
    raised1, token = hold(raised1, token)
    relayed1 = relay(raised1)
    own0, token = term_rows(info, live, ops3, 0, part, token, added=swapped0)
    token = touch(relayed0, token)
    summed1, token = add(second1, moved1, token)
    crossed1 = across(summed1)

    energy = jnp.zeros((sectors, 128), jnp.float32)
    sigma, energy = finish(info, live, own0, (raised0, relayed0, crossed0), energy, None, 0)
    own1, token = term_rows(info, live, ops3, part, part, token, energy, added=swapped1)
    sigma, energy = finish(info, live, own1, (raised1, relayed1, crossed1), energy, sigma, part)
    return sigma, sum_over_sectors(energy)


def solution(mesh):
    return jax.shard_map(
        on_device,
        mesh=mesh,
        in_specs=(
            P(("grp", "sec"), None, None),
            P(("grp", "sec"), None, None, None),
            P(("grp", "sec"), None, None, None),
            P(("grp", "sec")),
            P(("grp", "sec")),
        ),
        out_specs=(P(("grp", "sec"), None, None), P("grp")),
        check_vma=False,
    )
```

```python
import functools

import jax
import jax.numpy as jnp
from jax import lax
from jax.experimental import pallas as pl
from jax.experimental.pallas import tpu as pltpu
from jax.sharding import PartitionSpec as P

MIB = 1024 * 1024
LEFT_PIECES, RIGHT_PIECES = 8, 2
FIRST_MIB = 48
BRING_MIB = 42

ANY = pl.BlockSpec(memory_space=pl.ANY)
HBM = pl.BlockSpec(memory_space=pltpu.HBM)
SMEM = pl.BlockSpec(memory_space=pltpu.SMEM)
WHOLE = pl.BlockSpec(memory_space=pltpu.VMEM)
TOKEN = jax.ShapeDtypeStruct((8, 128), jnp.float32)
SMALL = pl.CostEstimate(flops=200000000, bytes_accessed=1000000, transcendentals=0)


def params(mib=8):
    return pltpu.CompilerParams(vmem_limit_bytes=mib * MIB)


def fetch(info_ref, slot, left_hbm, right_hbm, left_ref, right_ref, sems):
    term = info_ref[slot]
    rows, cols = left_ref.shape[0], right_ref.shape[0]
    step = rows // LEFT_PIECES
    left, right = [], []
    for i in range(LEFT_PIECES):
        span = pl.ds(i * step, step)
        left.append(
            pltpu.make_async_copy(left_hbm.at[0, term, span, :], left_ref.at[span, :], sems.at[i])
        )
    step = cols // RIGHT_PIECES
    for i in range(RIGHT_PIECES):
        span = pl.ds(i * step, step)
        right.append(
            pltpu.make_async_copy(
                right_hbm.at[0, term, span, :], right_ref.at[span, :], sems.at[LEFT_PIECES + i]
            )
        )
    half = LEFT_PIECES // 2
    return left[:half], right, left[half:]


def multiply(left, live, right):
    first = jnp.dot(left, live, preferred_element_type=jnp.float32).astype(jnp.bfloat16)
    return jnp.dot(first, right, preferred_element_type=jnp.float32)


def opening_kernel(slot, masks, tokens, info_ref, live_ref, left_hbm, right_hbm, *refs):
    refs = list(refs[tokens:])
    out_ref, _ = refs[:2]
    sems = refs[-1]
    operands = refs[2:-1]
    psi_ref = live_ref
    if masks:
        live_ref, sizes_ref = operands.pop(0), operands.pop(0)
    left, right, late = fetch(info_ref, slot, left_hbm, right_hbm, *operands, sems)
    for copy in left + right + late:
        copy.start()
    if masks:
        rows, cols = psi_ref.shape
        sizes_ref[:8, :] = jnp.full((8, cols), info_ref[4], jnp.int32)
        sizes_ref[8:, :] = jnp.full((8, cols), info_ref[5], jnp.int32)
        step = 128
        col = lax.broadcasted_iota(jnp.int32, (step, cols), 1) < info_ref[5]
        row = lax.broadcasted_iota(jnp.int32, (step, cols), 0)
        for start in range(0, rows, step):
            span = pl.ds(start, step)
            inside = jnp.logical_and(row < info_ref[4] - start, col)
            values = jnp.where(inside, psi_ref[span, :].astype(jnp.float32), 0.0)
            live_ref[span, :] = values.astype(live_ref.dtype)
    for copy in left:
        copy.wait()
    value = jnp.dot(
        operands[0][: out_ref.shape[0], :], live_ref[...], preferred_element_type=jnp.float32
    )
    for copy in right:
        copy.wait()
    out_ref[...] = jnp.dot(
        value.astype(jnp.bfloat16), operands[1][...], preferred_element_type=jnp.float32
    )
    for copy in late:
        copy.wait()


def operand_shapes(width, cols):
    return [
        jax.ShapeDtypeStruct((width, width), jnp.bfloat16),
        jax.ShapeDtypeStruct((cols, cols), jnp.bfloat16),
    ]


def opening_rows(info, live, envs, slot, count, *tokens, masks=False):
    width, cols = live.shape
    out_shape = [jax.ShapeDtypeStruct((count, cols), jnp.float32), TOKEN]
    if masks:
        out_shape.append(jax.ShapeDtypeStruct(live.shape, live.dtype))
        out_shape.append(jax.ShapeDtypeStruct((16, cols), jnp.int32))
    out_shape += operand_shapes(width, cols)
    return pl.pallas_call(
        functools.partial(opening_kernel, slot, masks, len(tokens)),
        out_shape=out_shape,
        in_specs=[SMEM, WHOLE, HBM, HBM] + [ANY] * len(tokens),
        out_specs=[WHOLE, ANY] + [WHOLE] * (len(out_shape) - 2),
        scratch_shapes=[pltpu.SemaphoreType.DMA((LEFT_PIECES + RIGHT_PIECES,))],
        compiler_params=params(FIRST_MIB if masks else BRING_MIB),
        cost_estimate=SMALL,
        name="opening_rows",
    )(info, live, *envs, *tokens)


def term_kernel(first, adds, slot, tokens, info_ref, live_ref, left_ref, right_ref, *refs):
    refs = list(refs)
    add_ref = refs.pop(0) if adds else None
    copies = []
    if slot is not None:
        left_hbm, right_hbm = refs[:2]
        sems = refs[-1]
        out_ref, _, left_next, right_next = refs[2 + tokens : -1]
        copies = sum(fetch(info_ref, slot, left_hbm, right_hbm, left_next, right_next, sems), [])
        for copy in copies:
            copy.start()
    else:
        out_ref, _ = refs[tokens:]
    count = out_ref.shape[0]
    block = min(count, 512)
    for i in range(count // block):
        span = pl.ds(i * block, block)
        value = multiply(left_ref[pl.ds(first + i * block, block), :], live_ref[...], right_ref[...])
        if adds:
            value = value + add_ref[span, :]
        out_ref[span, :] = value
    for copy in copies:
        copy.wait()


def term_rows(info, live, operands, first, count, *tokens, added=None, bring=None):
    width, cols = live.shape
    in_specs = [SMEM, WHOLE, WHOLE, WHOLE]
    args = [info, live, *operands]
    out_shape = [jax.ShapeDtypeStruct((count, cols), jnp.float32), TOKEN]
    out_specs = [WHOLE, ANY]
    scratch = []
    slot = None
    if added is not None:
        in_specs.append(WHOLE)
        args.append(added)
    if bring is not None:
        slot = bring[0]
        in_specs += [HBM, HBM]
        args += bring[1:]
        out_shape += operand_shapes(width, cols)
        out_specs += [WHOLE, WHOLE]
        scratch.append(pltpu.SemaphoreType.DMA((LEFT_PIECES + RIGHT_PIECES,)))
    return pl.pallas_call(
        functools.partial(term_kernel, first, added is not None, slot, len(tokens)),
        out_shape=out_shape,
        in_specs=in_specs + [ANY] * len(tokens),
        out_specs=out_specs,
        scratch_shapes=scratch,
        compiler_params=params(12 if slot is None else BRING_MIB),
        cost_estimate=SMALL,
        name="term_rows",
    )(*args, *tokens)


def add_kernel(a_ref, b_ref, *refs):
    out_ref = refs[-2]
    rows = a_ref.shape[0]
    step = 64

    def body(i, _):
        span = pl.ds(pl.multiple_of(i * step, step), step)
        out_ref[span, :] = a_ref[span, :] + b_ref[span, :]
        return _

    lax.fori_loop(0, rows // step, body, 0)


def add(a, b, *tokens):
    return pl.pallas_call(
        add_kernel,
        out_shape=(jax.ShapeDtypeStruct(a.shape, a.dtype), TOKEN),
        in_specs=[WHOLE, WHOLE] + [ANY] * len(tokens),
        out_specs=(WHOLE, ANY),
        compiler_params=params(),
        cost_estimate=SMALL,
        name="add_blocks",
    )(a, b, *tokens)


def touch(*values):
    return pl.pallas_call(
        lambda *refs: None,
        out_shape=TOKEN,
        in_specs=[ANY] * len(values),
        out_specs=ANY,
        compiler_params=params(),
        cost_estimate=SMALL,
        name="touch",
    )(*values)


def hold(value, token):
    return pl.pallas_call(
        lambda *refs: None,
        out_shape=(jax.ShapeDtypeStruct(value.shape, value.dtype), TOKEN),
        in_specs=[ANY, ANY],
        out_specs=(ANY, ANY),
        input_output_aliases={0: 0},
        compiler_params=params(),
        cost_estimate=SMALL,
        name="hold",
    )(value, token)


def finish_kernel(first, sizes_ref, live_ref, own_ref, a_ref, b_ref, c_ref, before_ref, *refs):
    place = lax.axis_index("sec") % 4
    which = jnp.where(place == 0, 1, jnp.where(place == 2, 0, 2))
    sigma_hbm, energy_ref, sigma_buf, sems = refs[-4:]
    count, cols = own_ref.shape
    step = 64
    piece = count // sems.shape[0]
    col = lax.broadcasted_iota(jnp.int32, (step, cols), 1) < sizes_ref[8:9, :]
    row = lax.broadcasted_iota(jnp.int32, (step, cols), 0)

    def copy(i):
        span = pl.ds(i * piece, piece)
        return pltpu.make_async_copy(
            sigma_buf.at[span, :], sigma_hbm.at[0, pl.ds(first + i * piece, piece), :], sems.at[i]
        )

    def work(arrival):
        energy = jnp.zeros((8, cols), jnp.float32)
        for i in range(count // piece):

            def body(n, energy):
                start = pl.multiple_of(i * piece + n * step, step)
                span = pl.ds(start, step)
                inside = jnp.logical_and(row < sizes_ref[0:1, :] - (first + start), col)
                total = jnp.where(inside, own_ref[span, :] + arrival[span, :], 0.0)
                sigma_buf[span, :] = total.astype(sigma_buf.dtype)
                here = pl.ds(pl.multiple_of(first + start, step), step)
                product = live_ref[here, :].astype(jnp.float32) * total
                return energy + jnp.sum(jnp.reshape(product, (step // 8, 8, cols)), axis=0)

            energy = lax.fori_loop(0, piece // step, body, energy)
            copy(i).start()
        energy_ref[...] = before_ref[...] + jnp.sum(energy)

    for n, arrival in enumerate((a_ref, b_ref, c_ref)):
        pl.when(which == n)(functools.partial(work, arrival))
    for i in range(count // piece):
        copy(i).wait()


def finish(sizes, live, own, arrivals, before, sigma, first):
    count, cols = own.shape
    in_specs = [WHOLE] * 7
    operands = [sizes, live, own, *arrivals, before]
    aliases = {}
    if sigma is not None:
        in_specs.append(ANY)
        aliases = {len(operands): 0}
        operands.append(sigma)
    return pl.pallas_call(
        functools.partial(finish_kernel, first),
        out_shape=(
            jax.ShapeDtypeStruct((1, *live.shape), jnp.bfloat16),
            jax.ShapeDtypeStruct(before.shape, jnp.float32),
        ),
        in_specs=in_specs,
        out_specs=(ANY, WHOLE),
        scratch_shapes=[pltpu.VMEM((count, cols), jnp.bfloat16), pltpu.SemaphoreType.DMA((4,))],
        input_output_aliases=aliases,
        compiler_params=params(),
        cost_estimate=SMALL,
        name="finish_rows",
    )(*operands)


def sum_over_sectors(value):
    arrived = lax.all_to_all(value, "sec", 0, 0, tiled=True)
    return jnp.reshape(jnp.sum(arrived[:, 0]), (1,))


def on_device(psi, left_env, right_env, row_sizes, col_sizes):
    sectors = lax.axis_size("sec")
    sector = lax.axis_index("sec")
    even = sector % 2 == 0
    place = sector % 4

    def send(value, *hops):
        pairs = [
            (s, s + steps)
            for at, steps in hops
            for s in range(at, sectors, 4)
            if 0 <= s + steps < sectors
        ]
        return lax.ppermute(value, "sec", pairs)

    rows = psi.shape[1]
    part = rows // 2
    which = jnp.where(place == 0, 1, jnp.where(place == 2, 0, 2))
    orders = [jnp.where(even, 2, 1), jnp.where(even, 3, 2), jnp.where(even, 1, 3), 0]
    info = jnp.stack([*orders, row_sizes[0], col_sizes[0], which]).astype(jnp.int32)

    pairs_up = [(s, s + 1) for s in range(1, sectors, 4) if s + 1 < sectors]
    pairs_up += [(s, s - 3) for s in range(3, sectors, 4) if s + 1 < sectors]

    def raise_one(value):
        return lax.ppermute(value, "sec", pairs_up)

    def along(value):
        return send(value, (3, 3), (0, -3))

    def across(value):
        return send(value, (1, 2), (2, -1))

    def swap(value):
        return send(value, (0, 1), (1, -1), (2, 1), (3, -1))

    def relay(value):
        return send(value, (0, 4))

    envs = (left_env, right_env)
    first0, token, live, sizes, *ops0 = opening_rows(info, psi[0], envs, 0, part, masks=True)
    paired0 = swap(first0)
    first1, token = term_rows(info, live, ops0, part, part, token)
    paired1 = swap(first1)
    both0, token = add(first0, paired0, token)
    raised0 = raise_one(both0)
    second0, token, *ops1 = opening_rows(info, live, envs, 1, part, token)
    moved0 = along(second0)
    both1, token = add(first1, paired1, token)
    raised1 = raise_one(both1)
    second1, token, *ops2 = term_rows(info, live, ops1, part, part, token, bring=(2, *envs))
    moved1 = along(second1)
    third0, token, *ops3 = term_rows(info, live, ops2, 0, part, token, bring=(3, *envs))
    swapped0 = swap(third0)
    raised0, token = hold(raised0, token)
    relayed0 = relay(raised0)
    third1, token = term_rows(info, live, ops2, part, part, token)
    swapped1 = swap(third1)
    summed0, token = add(second0, moved0, token)
    crossed0 = across(summed0)
    raised1, token = hold(raised1, token)
    relayed1 = relay(raised1)
    own0, token = term_rows(info, live, ops3, 0, part, token, added=swapped0)
    token = touch(relayed0, token)
    summed1, token = add(second1, moved1, token)
    crossed1 = across(summed1)

    energy = jnp.zeros((sectors, 128), jnp.float32)
    sigma, energy = finish(sizes, live, own0, (raised0, relayed0, crossed0), energy, None, 0)
    own1, token = term_rows(info, live, ops3, part, part, token, energy, added=swapped1)
    sigma, energy = finish(sizes, live, own1, (raised1, relayed1, crossed1), energy, sigma, part)
    return sigma, sum_over_sectors(energy)


def solution(mesh):
    return jax.shard_map(
        on_device,
        mesh=mesh,
        in_specs=(
            P(("grp", "sec"), None, None),
            P(("grp", "sec"), None, None, None),
            P(("grp", "sec"), None, None, None),
            P(("grp", "sec")),
            P(("grp", "sec")),
        ),
        out_specs=(P(("grp", "sec"), None, None), P("grp")),
        check_vma=False,
    )
```

```python
import functools

import jax
import jax.numpy as jnp
from jax import lax
from jax.experimental import pallas as pl
from jax.experimental.pallas import tpu as pltpu
from jax.sharding import PartitionSpec as P

MIB = 1024 * 1024
LEFT_PIECES, RIGHT_PIECES = 8, 2
FIRST_MIB = 48
BRING_MIB = 42

ANY = pl.BlockSpec(memory_space=pl.ANY)
HBM = pl.BlockSpec(memory_space=pltpu.HBM)
SMEM = pl.BlockSpec(memory_space=pltpu.SMEM)
WHOLE = pl.BlockSpec(memory_space=pltpu.VMEM)
TOKEN = jax.ShapeDtypeStruct((8, 128), jnp.float32)
SMALL = pl.CostEstimate(flops=200000000, bytes_accessed=1000000, transcendentals=0)


def params(mib=8):
    return pltpu.CompilerParams(vmem_limit_bytes=mib * MIB)


def fetch(info_ref, slot, left_hbm, right_hbm, left_ref, right_ref, sems):
    term = info_ref[slot]
    rows, cols = left_ref.shape[0], right_ref.shape[0]
    step = rows // LEFT_PIECES
    left, right = [], []
    for i in range(LEFT_PIECES):
        span = pl.ds(i * step, step)
        left.append(
            pltpu.make_async_copy(left_hbm.at[0, term, span, :], left_ref.at[span, :], sems.at[i])
        )
    step = cols // RIGHT_PIECES
    for i in range(RIGHT_PIECES):
        span = pl.ds(i * step, step)
        right.append(
            pltpu.make_async_copy(
                right_hbm.at[0, term, span, :], right_ref.at[span, :], sems.at[LEFT_PIECES + i]
            )
        )
    half = LEFT_PIECES // 2
    return left[:half], right, left[half:]


def multiply(left, live, right):
    first = jnp.dot(left, live, preferred_element_type=jnp.float32).astype(jnp.bfloat16)
    return jnp.dot(first, right, preferred_element_type=jnp.float32)


def opening_kernel(slot, masks, tokens, info_ref, live_ref, left_hbm, right_hbm, *refs):
    refs = list(refs[tokens:])
    out_ref, _ = refs[:2]
    sems = refs.pop()
    if masks:
        info_copy = pltpu.make_async_copy(info_ref, refs[-1], sems.at[sems.shape[0] - 1])
        info_copy.start()
        info_ref = refs.pop()
        terms = [jnp.where(lax.axis_index("sec") % 2 == 0, 2, 1)]
    else:
        terms = info_ref
    operands = refs[2:]
    psi_ref = live_ref
    if masks:
        live_ref, sizes_ref = operands.pop(0), operands.pop(0)
    left, right, late = fetch(terms, slot, left_hbm, right_hbm, *operands, sems)
    for copy in left + right + late:
        copy.start()
    if masks:
        info_copy.wait()
        rows, cols = psi_ref.shape
        sizes_ref[:8, :] = jnp.full((8, cols), info_ref[4], jnp.int32)
        sizes_ref[8:, :] = jnp.full((8, cols), info_ref[5], jnp.int32)
        step = 128
        col = lax.broadcasted_iota(jnp.int32, (step, cols), 1) < info_ref[5]
        row = lax.broadcasted_iota(jnp.int32, (step, cols), 0)
        for start in range(0, rows, step):
            span = pl.ds(start, step)
            inside = jnp.logical_and(row < info_ref[4] - start, col)
            values = jnp.where(inside, psi_ref[span, :].astype(jnp.float32), 0.0)
            live_ref[span, :] = values.astype(live_ref.dtype)
    for copy in left:
        copy.wait()
    value = jnp.dot(
        operands[0][: out_ref.shape[0], :], live_ref[...], preferred_element_type=jnp.float32
    )
    for copy in right:
        copy.wait()
    out_ref[...] = jnp.dot(
        value.astype(jnp.bfloat16), operands[1][...], preferred_element_type=jnp.float32
    )
    for copy in late:
        copy.wait()


def operand_shapes(width, cols):
    return [
        jax.ShapeDtypeStruct((width, width), jnp.bfloat16),
        jax.ShapeDtypeStruct((cols, cols), jnp.bfloat16),
    ]


def opening_rows(info, live, envs, slot, count, *tokens, masks=False):
    width, cols = live.shape
    out_shape = [jax.ShapeDtypeStruct((count, cols), jnp.float32), TOKEN]
    if masks:
        out_shape.append(jax.ShapeDtypeStruct(live.shape, live.dtype))
        out_shape.append(jax.ShapeDtypeStruct((16, cols), jnp.int32))
    out_shape += operand_shapes(width, cols)
    return pl.pallas_call(
        functools.partial(opening_kernel, slot, masks, len(tokens)),
        out_shape=out_shape,
        in_specs=[ANY if masks else SMEM, WHOLE, HBM, HBM] + [ANY] * len(tokens),
        out_specs=[WHOLE, ANY] + [WHOLE] * (len(out_shape) - 2),
        scratch_shapes=([pltpu.SMEM(info.shape, info.dtype)] if masks else [])
        + [pltpu.SemaphoreType.DMA((LEFT_PIECES + RIGHT_PIECES + 1,))],
        compiler_params=params(FIRST_MIB if masks else BRING_MIB),
        cost_estimate=SMALL,
        name="opening_rows",
    )(info, live, *envs, *tokens)


def term_kernel(first, adds, slot, tokens, info_ref, live_ref, left_ref, right_ref, *refs):
    refs = list(refs)
    add_ref = refs.pop(0) if adds else None
    copies = []
    if slot is not None:
        left_hbm, right_hbm = refs[:2]
        sems = refs[-1]
        out_ref, _, left_next, right_next = refs[2 + tokens : -1]
        copies = sum(fetch(info_ref, slot, left_hbm, right_hbm, left_next, right_next, sems), [])
        for copy in copies:
            copy.start()
    else:
        out_ref, _ = refs[tokens:]
    count = out_ref.shape[0]
    block = min(count, 512)
    for i in range(count // block):
        span = pl.ds(i * block, block)
        value = multiply(left_ref[pl.ds(first + i * block, block), :], live_ref[...], right_ref[...])
        if adds:
            value = value + add_ref[span, :]
        out_ref[span, :] = value
    for copy in copies:
        copy.wait()


def term_rows(info, live, operands, first, count, *tokens, added=None, bring=None):
    width, cols = live.shape
    in_specs = [ANY if bring is None else SMEM, WHOLE, WHOLE, WHOLE]
    args = [info, live, *operands]
    out_shape = [jax.ShapeDtypeStruct((count, cols), jnp.float32), TOKEN]
    out_specs = [WHOLE, ANY]
    scratch = []
    slot = None
    if added is not None:
        in_specs.append(WHOLE)
        args.append(added)
    if bring is not None:
        slot = bring[0]
        in_specs += [HBM, HBM]
        args += bring[1:]
        out_shape += operand_shapes(width, cols)
        out_specs += [WHOLE, WHOLE]
        scratch.append(pltpu.SemaphoreType.DMA((LEFT_PIECES + RIGHT_PIECES,)))
    return pl.pallas_call(
        functools.partial(term_kernel, first, added is not None, slot, len(tokens)),
        out_shape=out_shape,
        in_specs=in_specs + [ANY] * len(tokens),
        out_specs=out_specs,
        scratch_shapes=scratch,
        compiler_params=params(12 if slot is None else BRING_MIB),
        cost_estimate=SMALL,
        name="term_rows",
    )(*args, *tokens)


def add_kernel(a_ref, b_ref, *refs):
    out_ref = refs[-2]
    rows = a_ref.shape[0]
    step = 64

    def body(i, _):
        span = pl.ds(pl.multiple_of(i * step, step), step)
        out_ref[span, :] = a_ref[span, :] + b_ref[span, :]
        return _

    lax.fori_loop(0, rows // step, body, 0)


def add(a, b, *tokens):
    return pl.pallas_call(
        add_kernel,
        out_shape=(jax.ShapeDtypeStruct(a.shape, a.dtype), TOKEN),
        in_specs=[WHOLE, WHOLE] + [ANY] * len(tokens),
        out_specs=(WHOLE, ANY),
        compiler_params=params(),
        cost_estimate=SMALL,
        name="add_blocks",
    )(a, b, *tokens)


def touch(*values):
    return pl.pallas_call(
        lambda *refs: None,
        out_shape=TOKEN,
        in_specs=[ANY] * len(values),
        out_specs=ANY,
        compiler_params=params(),
        cost_estimate=SMALL,
        name="touch",
    )(*values)


def hold(value, token):
    return pl.pallas_call(
        lambda *refs: None,
        out_shape=(jax.ShapeDtypeStruct(value.shape, value.dtype), TOKEN),
        in_specs=[ANY, ANY],
        out_specs=(ANY, ANY),
        input_output_aliases={0: 0},
        compiler_params=params(),
        cost_estimate=SMALL,
        name="hold",
    )(value, token)


def finish_kernel(first, sizes_ref, live_ref, own_ref, a_ref, b_ref, c_ref, before_ref, *refs):
    place = lax.axis_index("sec") % 4
    which = jnp.where(place == 0, 1, jnp.where(place == 2, 0, 2))
    sigma_hbm, energy_ref, sigma_buf, sems = refs[-4:]
    count, cols = own_ref.shape
    step = 64
    piece = count // sems.shape[0]
    col = lax.broadcasted_iota(jnp.int32, (step, cols), 1) < sizes_ref[8:9, :]
    row = lax.broadcasted_iota(jnp.int32, (step, cols), 0)

    def copy(i):
        span = pl.ds(i * piece, piece)
        return pltpu.make_async_copy(
            sigma_buf.at[span, :], sigma_hbm.at[0, pl.ds(first + i * piece, piece), :], sems.at[i]
        )

    def work(arrival):
        energy = jnp.zeros((8, cols), jnp.float32)
        for i in range(count // piece):

            def body(n, energy):
                start = pl.multiple_of(i * piece + n * step, step)
                span = pl.ds(start, step)
                inside = jnp.logical_and(row < sizes_ref[0:1, :] - (first + start), col)
                total = jnp.where(inside, own_ref[span, :] + arrival[span, :], 0.0)
                sigma_buf[span, :] = total.astype(sigma_buf.dtype)
                here = pl.ds(pl.multiple_of(first + start, step), step)
                product = live_ref[here, :].astype(jnp.float32) * total
                return energy + jnp.sum(jnp.reshape(product, (step // 8, 8, cols)), axis=0)

            energy = lax.fori_loop(0, piece // step, body, energy)
            copy(i).start()
        energy_ref[...] = before_ref[...] + jnp.sum(energy)

    for n, arrival in enumerate((a_ref, b_ref, c_ref)):
        pl.when(which == n)(functools.partial(work, arrival))
    for i in range(count // piece):
        copy(i).wait()


def finish(sizes, live, own, arrivals, before, sigma, first):
    count, cols = own.shape
    in_specs = [WHOLE] * 7
    operands = [sizes, live, own, *arrivals, before]
    aliases = {}
    if sigma is not None:
        in_specs.append(ANY)
        aliases = {len(operands): 0}
        operands.append(sigma)
    return pl.pallas_call(
        functools.partial(finish_kernel, first),
        out_shape=(
            jax.ShapeDtypeStruct((1, *live.shape), jnp.bfloat16),
            jax.ShapeDtypeStruct(before.shape, jnp.float32),
        ),
        in_specs=in_specs,
        out_specs=(ANY, WHOLE),
        scratch_shapes=[pltpu.VMEM((count, cols), jnp.bfloat16), pltpu.SemaphoreType.DMA((4,))],
        input_output_aliases=aliases,
        compiler_params=params(),
        cost_estimate=SMALL,
        name="finish_rows",
    )(*operands)


def sum_over_sectors(value):
    arrived = lax.all_to_all(value, "sec", 0, 0, tiled=True)
    return jnp.reshape(jnp.sum(arrived[:, 0]), (1,))


def on_device(psi, left_env, right_env, row_sizes, col_sizes):
    sectors = lax.axis_size("sec")
    sector = lax.axis_index("sec")
    even = sector % 2 == 0
    place = sector % 4

    def send(value, *hops):
        pairs = [
            (s, s + steps)
            for at, steps in hops
            for s in range(at, sectors, 4)
            if 0 <= s + steps < sectors
        ]
        return lax.ppermute(value, "sec", pairs)

    rows = psi.shape[1]
    part = rows // 2
    which = jnp.where(place == 0, 1, jnp.where(place == 2, 0, 2))
    orders = [jnp.where(even, 2, 1), jnp.where(even, 3, 2), jnp.where(even, 1, 3), 0]
    info = jnp.stack([*orders, row_sizes[0], col_sizes[0], which]).astype(jnp.int32)

    pairs_up = [(s, s + 1) for s in range(1, sectors, 4) if s + 1 < sectors]
    pairs_up += [(s, s - 3) for s in range(3, sectors, 4) if s + 1 < sectors]

    def raise_one(value):
        return lax.ppermute(value, "sec", pairs_up)

    def along(value):
        return send(value, (3, 3), (0, -3))

    def across(value):
        return send(value, (1, 2), (2, -1))

    def swap(value):
        return send(value, (0, 1), (1, -1), (2, 1), (3, -1))

    def relay(value):
        return send(value, (0, 4))

    envs = (left_env, right_env)
    first0, token, live, sizes, *ops0 = opening_rows(info, psi[0], envs, 0, part, masks=True)
    paired0 = swap(first0)
    first1, token = term_rows(info, live, ops0, part, part, token)
    paired1 = swap(first1)
    both0, token = add(first0, paired0, token)
    raised0 = raise_one(both0)
    second0, token, *ops1 = opening_rows(info, live, envs, 1, part, token)
    moved0 = along(second0)
    both1, token = add(first1, paired1, token)
    raised1 = raise_one(both1)
    second1, token, *ops2 = term_rows(info, live, ops1, part, part, token, bring=(2, *envs))
    moved1 = along(second1)
    third0, token, *ops3 = term_rows(info, live, ops2, 0, part, token, bring=(3, *envs))
    swapped0 = swap(third0)
    raised0, token = hold(raised0, token)
    relayed0 = relay(raised0)
    third1, token = term_rows(info, live, ops2, part, part, token)
    swapped1 = swap(third1)
    summed0, token = add(second0, moved0, token)
    crossed0 = across(summed0)
    raised1, token = hold(raised1, token)
    relayed1 = relay(raised1)
    own0, token = term_rows(info, live, ops3, 0, part, token, added=swapped0)
    token = touch(relayed0, token)
    summed1, token = add(second1, moved1, token)
    crossed1 = across(summed1)

    energy = jnp.zeros((sectors, 128), jnp.float32)
    sigma, energy = finish(sizes, live, own0, (raised0, relayed0, crossed0), energy, None, 0)
    own1, token = term_rows(info, live, ops3, part, part, token, energy, added=swapped1)
    sigma, energy = finish(sizes, live, own1, (raised1, relayed1, crossed1), energy, sigma, part)
    return sigma, sum_over_sectors(energy)


def solution(mesh):
    return jax.shard_map(
        on_device,
        mesh=mesh,
        in_specs=(
            P(("grp", "sec"), None, None),
            P(("grp", "sec"), None, None, None),
            P(("grp", "sec"), None, None, None),
            P(("grp", "sec")),
            P(("grp", "sec")),
        ),
        out_specs=(P(("grp", "sec"), None, None), P("grp")),
        check_vma=False,
    )
```
